128 devices in a mesh: ctx: 16 (over y, z_hi, core), tp: 8 (over z_lo, x).
Axes of the slice: x: 4, y: 4, z: 4 (z_hi: 2, z_lo: 2; z = z_hi * 2 + z_lo), core: 2. Of those that a mesh axis runs over, the one named last changes fastest.
Arguments:
- ctx_heads: bfloat16 [16384, 4096], P('ctx', 'tp'), may hold values from -6 to 6
- out_weight: bfloat16 [4096, 4096], P('ctx', 'tp'), may hold values from -0.09375 to 0.09375
- hidden_in: bfloat16 [16384, 4096], P(('ctx', 'tp')), may hold values from -54 to 54
- norm_gain: float32 [4096], replicated, may hold values from 0.5 to 1.5
- expert_ids: int32 [16384, 2], P(('ctx', 'tp')), may hold values from 0 to 63, all different within a row; in each aligned block of 128 rows (0 to 127, 128 to 255, ...) at most 6 rows name the same one
- route_weights: float32 [16384, 2], P(('ctx', 'tp')), may hold values from 0.02 to 0.4
- w_gate: bfloat16 [128, 4096, 384], P(('ctx', 'tp')), may hold values from -0.09375 to 0.09375
- w_up: bfloat16 [128, 4096, 384], P(('ctx', 'tp')), may hold values from -0.09375 to 0.09375
- w_down: bfloat16 [128, 384, 4096], P(('ctx', 'tp')), may hold values from -0.21875 to 0.21875
- grad_out: bfloat16 [16384, 4096], P(('ctx', 'tp')), may hold values from -6 to 6
Outputs:
- d_ctx_heads: bfloat16 [16384, 4096], P('ctx', 'tp')
- d_out_weight: bfloat16 [4096, 4096], P('ctx', 'tp')
- d_hidden_in: bfloat16 [16384, 4096], P(('ctx', 'tp'))
- d_route_weights: float32 [16384, 2], P(('ctx', 'tp'))
- d_w_gate: bfloat16 [128, 4096, 384], P(('ctx', 'tp'))
- d_w_up: bfloat16 [128, 4096, 384], P(('ctx', 'tp'))
- d_w_down: bfloat16 [128, 384, 4096], P(('ctx', 'tp'))
The draws below stay inside these ranges and needn't reach their ends.
Inputs may be any that keep to these rules, and one draw needn't show every extreme that they name: `expert_ids`: each token names 2 different experts. In each aligned block of 128 tokens (the tokens of one device) no expert is named by more than 6 tokens, a bound that some block reaches. Every expert is named by some token.
All inputs are finite; a program needn't handle non-finite values.
Results may differ from the reference program's by a relative error of at most 0.02.
Values may be sent and summed in bfloat16 or wider, within the bound.
A program may use at most 192 MiB of HBM per device.

```python
import math
import jax
import jax.numpy as jnp
import numpy as np
from jax import lax

D = 4096
HEADS = 32
HDIM = 128
FFE = 768
TOPK = 2
TOK_DEV = 1024
ROW_DEV = 128
TOKENS = 16384
EXPERTS = 64
CAP = 6
N_CTX = 16


def draw_hidden_in(key, part):
    key = jax.random.fold_in(key, 11)
    first, second, third = jax.random.split(key, 3)
    base = jnp.clip(jax.random.normal(first, (TOKENS, D), jnp.float32), -6.0, 6.0)
    row_scale = jnp.exp(jax.random.uniform(second, (TOKENS, 1), jnp.float32, math.log(0.3), math.log(3.0)))
    col_scale = jnp.exp(jax.random.uniform(third, (1, D), jnp.float32, math.log(0.3), math.log(3.0)))
    return (base * row_scale * col_scale).astype(jnp.bfloat16)


def levels(stream_key, extent, pieces, low, high):
    level = 1.0
    for axis_at, parts in pieces:
        heights = jax.random.uniform(jax.random.fold_in(jax.random.fold_in(stream_key, 6), axis_at), (parts,), jnp.float32, low / len(pieces), high / len(pieces))
        level = level * jnp.repeat(jnp.exp(heights), extent[axis_at] // parts).reshape((-1,) + (1,) * (len(extent) - 1 - axis_at))
    return level


def assign_block(rng, own, number, rows, count, top, reach, skew):
    sequence = jax.random.permutation(rng, count)
    heavy_load, common = load_shares(count, rows * top, reach, skew, True), load_shares(count, rows * top, reach, skew, False)
    places = jnp.arange(count)

    def named(lengths, turn):
        used = int((lengths > 0).sum())
        fixed = max(1, used // 4)
        passed = fixed + (places - fixed + turn * (used - fixed)) % max(1, count - fixed)
        return jnp.zeros((count,), jnp.int32).at[sequence[jnp.where(places < fixed, places, passed)]].set(jnp.asarray(lengths, jnp.int32))

    lengths = jnp.where(number % 4 == 0, named(heavy_load, number // 4), named(common, number - number // 4 - 1))
    mixed = jax.random.permutation(jax.random.fold_in(own, 3), count)
    donor, taker = mixed[0:count // 2 * 2:2], mixed[1:count // 2 * 2:2]
    margin = jnp.minimum(lengths[donor] - 1, reach - lengths[taker]) // 2
    margin = jnp.where((donor == sequence[0]) | (taker == sequence[0]) | (lengths[taker] == 0), 0, jnp.maximum(margin, 0))
    passed = jax.random.randint(jax.random.fold_in(own, 4), (count // 2,), 0, 1 << 20) % (margin + 1)
    lengths = lengths.at[donor].add(-passed).at[taker].add(passed)
    labels = jnp.searchsorted(jnp.cumsum(lengths), jnp.arange(rows * top), side="right").astype(jnp.int32)
    listing = labels.reshape(top, rows).T
    listing = listing[jax.random.permutation(jax.random.fold_in(own, 1), rows)]
    turn = jax.random.randint(jax.random.fold_in(own, 2), (rows, 1), 0, top)
    return jnp.take_along_axis(listing, (jnp.arange(top)[None, :] + turn) % top, axis=1)


def load_shares(number_of, total, most, slope, full):
    portions = [(1 << 20) // math.isqrt(grade ** slope) + 1 for grade in range(1, number_of + 1)]
    largest = most if full else min(most, max(-(-total // number_of), total * portions[0] // sum(portions)))
    least = 1 if total - largest >= number_of - 1 else 0
    holding, rest = [largest] + [least] * (number_of - 1), total - largest - least * (number_of - 1)
    while rest > 0:
        candidates = [i for i in range(1, number_of) if holding[i] < largest] or [i for i in range(1, number_of) if holding[i] < most]
        mass, budget = sum([portions[i] for i in candidates]), rest
        for i in candidates:
            extra = min(most - holding[i], max(1, budget * portions[i] // mass), rest)
            holding[i] = holding[i] + extra
            rest = rest - extra
    return np.array(holding)


def centred(rng, extent, spread, reach, shards=(), held_as=jnp.bfloat16):
    factor_of = levels(rng, extent, shards, -0.22, 0.18) if shards else 1.0
    drawn = jax.random.normal(rng, extent, jnp.float32) * spread * factor_of
    return jnp.minimum(jnp.maximum(drawn, -reach), reach).astype(held_as)


def setup_inputs(seed: int = 0) -> dict:
    splits = jax.random.split(jax.random.key(seed), 11)
    ctx_heads = centred(splits[0], (TOKENS, HEADS * HDIM), 1.0, 6.0, ((0, 16), (1, 8)))
    out_weight = centred(splits[1], (D, HEADS * HDIM), (HEADS * HDIM) ** -0.5, 0.09375, ((0, 16), (1, 8)))
    hidden_in = draw_hidden_in(jax.random.fold_in(splits[10], 71), 0)
    norm_gain = jnp.clip(1.0 + 0.1 * jax.random.normal(splits[3], (D,), jnp.float32), 0.5, 1.5)
    expert_ids_keys = jax.random.split(jax.random.fold_in(splits[4], 1), TOKENS // ROW_DEV)
    expert_ids_turns = jax.random.permutation(jax.random.fold_in(splits[4], 3), TOKENS // ROW_DEV)
    expert_ids = jax.vmap(lambda own, number: assign_block(jax.random.fold_in(splits[4], 2), own, number, ROW_DEV, EXPERTS, TOPK, CAP, 0))(expert_ids_keys, expert_ids_turns).reshape((TOKENS, TOPK))
    route_weights = jnp.clip(jnp.exp(math.log(0.4) - 2.9957323 * jax.random.uniform(splits[5], (TOKENS, TOPK), jnp.float32) ** levels(splits[5], (TOKENS, TOPK), ((0, 128),), -0.2, 0.2)), 0.02, 0.4)
    w_gate = centred(splits[6], (2 * EXPERTS, D, FFE // 2), D ** -0.5, 0.09375, ((0, 128),))
    w_up = centred(splits[7], (2 * EXPERTS, D, FFE // 2), D ** -0.5, 0.09375, ((0, 128),))
    w_down = centred(splits[8], (2 * EXPERTS, FFE // 2, D), FFE ** -0.5, 0.21875, ((0, 128),))
    grad_out = centred(splits[9], (TOKENS, D), 1.0, 6.0, ((0, 128),))
    return dict(ctx_heads=ctx_heads, out_weight=out_weight, hidden_in=hidden_in, norm_gain=norm_gain, expert_ids=expert_ids, route_weights=route_weights, w_gate=w_gate, w_up=w_up, w_down=w_down, grad_out=grad_out)


EPSILON = 1e-06
CONTRACT_FIRST = (((0,), (0,)), ((), ()))
CONTRACT_LAST = (((1,), (1,)), ((), ()))

def normalize(hidden_in, norm_gain):
    hidden_wide = hidden_in.astype(jnp.float32)
    rms_scale = lax.rsqrt(lax.optimization_barrier(jnp.mean(hidden_wide * hidden_wide, axis=-1, keepdims=True)) + EPSILON)
    normed = (hidden_wide * rms_scale * norm_gain).astype(jnp.bfloat16)
    return (hidden_wide, rms_scale, normed)

def norm_backward(hidden_wide, rms_scale, norm_gain, normed_grad, grad_out):
    gained = normed_grad * norm_gain
    inner = lax.optimization_barrier(jnp.mean(gained * hidden_wide, axis=-1, keepdims=True))
    cubed = rms_scale * rms_scale * rms_scale
    return grad_out.astype(jnp.float32) + rms_scale * gained - hidden_wide * cubed * inner

def expert_half(slot_rows, slot_cots, slot_weights, gate_matrix, up_matrix, down_matrix):
    gate_pre = jnp.dot(slot_rows, gate_matrix, preferred_element_type=jnp.float32)
    up_value = jnp.dot(slot_rows, up_matrix, preferred_element_type=jnp.float32)
    sigmoid_gate = jax.nn.sigmoid(gate_pre)
    silu_gate = gate_pre * sigmoid_gate
    activated = (silu_gate * up_value).astype(jnp.bfloat16)
    back_proj = lax.dot_general(slot_cots, down_matrix, CONTRACT_LAST, preferred_element_type=jnp.float32)
    weight_dots = lax.optimization_barrier(jnp.sum(activated.astype(jnp.float32) * back_proj, axis=-1))
    scaled_grad = (slot_weights[:, None] * slot_cots.astype(jnp.float32)).astype(jnp.bfloat16)
    down_wgrad = lax.dot_general(activated, scaled_grad, CONTRACT_FIRST, preferred_element_type=jnp.float32)
    act_grad = slot_weights[:, None] * back_proj
    gate_grad = (act_grad * up_value * sigmoid_gate * (1.0 + gate_pre * (1.0 - sigmoid_gate))).astype(jnp.bfloat16)
    up_grad = (act_grad * silu_gate).astype(jnp.bfloat16)
    gate_wgrad = lax.dot_general(slot_rows, gate_grad, CONTRACT_FIRST, preferred_element_type=jnp.float32)
    up_wgrad = lax.dot_general(slot_rows, up_grad, CONTRACT_FIRST, preferred_element_type=jnp.float32)
    slot_grads = lax.dot_general(gate_grad, gate_matrix, CONTRACT_LAST, preferred_element_type=jnp.float32)
    slot_grads = slot_grads + lax.dot_general(up_grad, up_matrix, CONTRACT_LAST, preferred_element_type=jnp.float32)
    return (slot_grads.astype(jnp.bfloat16), weight_dots, gate_wgrad.astype(jnp.bfloat16), up_wgrad.astype(jnp.bfloat16), down_wgrad.astype(jnp.bfloat16))

def slot_ranks(expert_ids, expert_count, block_rows):
    tok_total, pick_count = expert_ids.shape
    grouped = expert_ids.reshape(tok_total // block_rows, block_rows, pick_count)
    onehot = (grouped[..., None] == jnp.arange(expert_count, dtype=jnp.int32)).astype(jnp.int32).sum(axis=2)
    before = jnp.cumsum(onehot, axis=1) - onehot
    ranks = jnp.take_along_axis(before, grouped, axis=2)
    return ranks.reshape(tok_total, pick_count).astype(jnp.int32)

def reference(ctx_heads, out_weight, hidden_in, norm_gain, expert_ids, route_weights, w_gate, w_up, w_down, grad_out):
    tok_total, features = hidden_in.shape
    expert_count = EXPERTS
    block_count = tok_total // ROW_DEV
    hidden_wide, rms_scale, normed = normalize(hidden_in, norm_gain)
    ranks = slot_ranks(expert_ids, expert_count, ROW_DEV)
    block_of = (jnp.arange(tok_total, dtype=jnp.int32) // ROW_DEV)[:, None]
    target = ((expert_ids * block_count + block_of) * CAP + ranks).astype(jnp.int32)
    rows_of = jnp.broadcast_to(jnp.arange(tok_total, dtype=jnp.int32)[:, None], target.shape)
    slot_table = jnp.full((expert_count * block_count * CAP,), tok_total, jnp.int32)
    slot_table = slot_table.at[target.reshape(-1)].set(rows_of.reshape(-1))
    weight_table = jnp.zeros((expert_count * block_count * CAP,), jnp.float32)
    weight_table = weight_table.at[target.reshape(-1)].set(route_weights.reshape(-1))
    slot_table = slot_table.reshape(expert_count, block_count * CAP)
    weight_table = weight_table.reshape(expert_count, block_count * CAP)
    zero_row = jnp.zeros((1, features), jnp.bfloat16)
    normed_pad = jnp.concatenate([normed, zero_row], axis=0)
    grad_pad = jnp.concatenate([grad_out, zero_row], axis=0)

    def per_expert(expert_index):
        picks = slot_table[expert_index]
        slot_rows = normed_pad[picks]
        slot_cots = grad_pad[picks]
        slot_weights = weight_table[expert_index]
        low_index = 2 * expert_index
        high_index = 2 * expert_index + 1
        lower = expert_half(slot_rows, slot_cots, slot_weights, w_gate[low_index], w_up[low_index], w_down[low_index])
        upper = expert_half(slot_rows, slot_cots, slot_weights, w_gate[high_index], w_up[high_index], w_down[high_index])
        slot_grads = (lower[0].astype(jnp.float32) + upper[0].astype(jnp.float32)).astype(jnp.bfloat16)
        return (slot_grads, lower[1] + upper[1], jnp.stack([lower[2], upper[2]]), jnp.stack([lower[3], upper[3]]), jnp.stack([lower[4], upper[4]]))
    slot_grads, weight_dots, gate_wgrad, up_wgrad, down_wgrad = lax.map(per_expert, jnp.arange(expert_count, dtype=jnp.int32))
    flat_grads = slot_grads.reshape(-1, features)
    flat_dots = weight_dots.reshape(-1)
    normed_grad = jnp.zeros((tok_total, features), jnp.float32)
    for pick in range(TOPK):
        normed_grad = normed_grad + flat_grads[target[:, pick]].astype(jnp.float32)
    route_grads = flat_dots[target]
    resid_grad = norm_backward(hidden_wide, rms_scale, norm_gain, normed_grad, grad_out).astype(jnp.bfloat16)
    heads_grad = jnp.dot(resid_grad, out_weight, preferred_element_type=jnp.float32).astype(jnp.bfloat16)

    def add_block(block_index, total):
        start = (block_index * TOK_DEV).astype(jnp.int32)
        grad_block = lax.dynamic_slice_in_dim(resid_grad, start, TOK_DEV, 0)
        head_block = lax.dynamic_slice_in_dim(ctx_heads, start, TOK_DEV, 0)
        partial_term = lax.dot_general(grad_block, head_block, CONTRACT_FIRST, preferred_element_type=jnp.float32)
        rounded = lax.optimization_barrier(partial_term.astype(jnp.bfloat16))
        return total + rounded.astype(jnp.float32)
    weight_total = lax.fori_loop(0, N_CTX, add_block, jnp.zeros(out_weight.shape, jnp.float32))
    shape_gate = (2 * expert_count,) + w_gate.shape[1:]
    shape_down = (2 * expert_count,) + w_down.shape[1:]
    return (heads_grad, weight_total.astype(jnp.bfloat16), resid_grad, route_grads, gate_wgrad.reshape(shape_gate), up_wgrad.reshape(shape_gate), down_wgrad.reshape(shape_down))
```

```python
import functools

import jax
import jax.numpy as jnp
from jax import lax
from jax.experimental import pallas as pl
from jax.experimental.pallas import tpu as pltpu
from jax.sharding import PartitionSpec as P

EPSILON = 1e-06
CAP = 6
BLOCKS = 8
CHUNK = CAP * BLOCKS
CONTRACT_FIRST = (((0,), (0,)), ((), ()))
CONTRACT_LAST = (((1,), (1,)), ((), ()))
MIB = 1 << 20


def iota(shape, dim):
    return lax.broadcasted_iota(jnp.int32, shape, dim)


def mm(a, b, dims=(((1,), (0,)), ((), ()))):
    return lax.dot_general(a, b, dims, preferred_element_type=jnp.float32)


def dispatch_kernel(ids_ref, weight_ref, hidden_ref, gain_ref, cot_ref, rows_ref, cots_ref,
                    slot, weight, stacked_rows, stacked_cots):
    tokens, features = hidden_ref.shape
    width = features // BLOCKS
    experts = slot.shape[0]
    group = rows_ref.shape[0]
    step = pl.program_id(0)

    @pl.when(step == 0)
    def _():
        expert = iota((experts, tokens), 0)
        first = expert == ids_ref[0:1, :]
        second = expert == ids_ref[1:2, :]
        named = jnp.where(first | second, 1.0, 0.0)
        earlier = jnp.where(iota((tokens, tokens), 0) < iota((tokens, tokens), 1), 1.0, 0.0)
        prior = mm(named.astype(jnp.bfloat16), earlier.astype(jnp.bfloat16))
        slot[...] = jnp.where(named > 0.5, prior, -1.0)
        weight[...] = jnp.where(
            first, weight_ref[0:1, :], jnp.where(second, weight_ref[1:2, :], 0.0)
        )
        wide = hidden_ref[...].astype(jnp.float32)
        scale = lax.rsqrt(jnp.mean(wide * wide, axis=-1, keepdims=True) + EPSILON)
        for block in range(BLOCKS):
            columns = slice(block * width, (block + 1) * width)
            rows = slice(block * tokens, (block + 1) * tokens)
            stacked_rows[rows, :] = (
                hidden_ref[:, columns].astype(jnp.float32) * scale * gain_ref[:, columns]
            ).astype(jnp.bfloat16)
            stacked_cots[rows, :] = cot_ref[:, columns]

    here = pl.ds(pl.multiple_of(step * group, group), group)
    shape = (group, CHUNK, tokens)
    slots = jnp.broadcast_to(slot[here, :][:, None, :], shape)
    weights = jnp.broadcast_to(weight[here, :][:, None, :], shape)
    place = iota(shape, 1)
    block_of = place // CAP
    taken = slots == (place - block_of * CAP).astype(jnp.float32)
    weights = jnp.where(taken, weights, 0.0).reshape(group * CHUNK, tokens)
    taken = jnp.where(taken, 1.0, 0.0).reshape(group * CHUNK, tokens)
    block_of = block_of.reshape(group * CHUNK, tokens)
    pick_rows = jnp.concatenate(
        [jnp.where(block_of == b, taken, 0.0).astype(jnp.bfloat16) for b in range(BLOCKS)], axis=1
    )
    pick_cots = jnp.concatenate(
        [jnp.where(block_of == b, weights, 0.0).astype(jnp.bfloat16) for b in range(BLOCKS)], axis=1
    )
    rows = mm(pick_rows, stacked_rows[...]).astype(jnp.bfloat16).reshape(group, CHUNK, width)
    cots = mm(pick_cots, stacked_cots[...]).astype(jnp.bfloat16).reshape(group, CHUNK, width)
    for half in range(2):
        rows_ref[:, half] = rows
        cots_ref[:, half] = cots


def dispatch(ids_t, weights_t, hidden, gain, cots, experts):
    tokens, features = hidden.shape
    width = features // BLOCKS
    group = 8
    whole = lambda shape: pl.BlockSpec(shape, lambda i: (0, 0))
    out = jax.ShapeDtypeStruct((experts, 2, CHUNK, width), jnp.bfloat16)
    out_spec = pl.BlockSpec((group, 2, CHUNK, width), lambda i: (i, 0, 0, 0))
    return pl.pallas_call(
        dispatch_kernel,
        grid=(experts // group,),
        in_specs=[whole(ids_t.shape), whole(weights_t.shape), whole(hidden.shape),
                  whole(gain.shape), whole(cots.shape)],
        out_specs=[out_spec, out_spec],
        out_shape=[out, out],
        scratch_shapes=[
            pltpu.VMEM((experts, tokens), jnp.float32),
            pltpu.VMEM((experts, tokens), jnp.float32),
            pltpu.VMEM((BLOCKS * tokens, width), jnp.bfloat16),
            pltpu.VMEM((BLOCKS * tokens, width), jnp.bfloat16),
        ],
        compiler_params=pltpu.CompilerParams(vmem_limit_bytes=48 * MIB),
        cost_estimate=pl.CostEstimate(
            flops=4 * experts * CHUNK * tokens * features, bytes_accessed=16 * MIB,
            transcendentals=0),
        name="dispatch",
    )(ids_t, weights_t, hidden, gain, cots)


def unpack_matrix(sources):
    rows = sources * CHUNK
    out, inp = iota((rows, rows), 0), iota((rows, rows), 1)
    block = out // (sources * CAP)
    rest = out - block * (sources * CAP)
    source = rest // CAP
    want = source * CHUNK + block * CAP + (rest - source * CAP)
    return jnp.where(inp == want, 1.0, 0.0).astype(jnp.bfloat16)


GROUP = 8


def unpack_rows(unpack, raw_ref, out_ref):
    rows = GROUP * CHUNK
    height = GROUP * CAP
    width = raw_ref.shape[1]
    for g in range(raw_ref.shape[0] // rows):
        flat = mm(unpack, raw_ref[g * rows:(g + 1) * rows, :]).astype(jnp.bfloat16)
        for b in range(BLOCKS):
            out_ref[g * height:(g + 1) * height, b * width:(b + 1) * width] = (
                flat[b * height:(b + 1) * height, :]
            )


def unpack_kernel(raw_ref, out_ref, unpack):
    @pl.when(pl.program_id(0) == 0)
    def _():
        unpack[...] = unpack_matrix(GROUP)

    unpack_rows(unpack[...], raw_ref, out_ref)


def unpack_chunks(raw, steps=8):
    total, width = raw.shape
    rows = total // steps
    return pl.pallas_call(
        unpack_kernel,
        grid=(steps,),
        in_specs=[pl.BlockSpec((rows, width), lambda i: (i, 0))],
        out_specs=pl.BlockSpec((rows // BLOCKS, width * BLOCKS), lambda i: (i, 0)),
        out_shape=jax.ShapeDtypeStruct((total // BLOCKS, width * BLOCKS), jnp.bfloat16),
        scratch_shapes=[pltpu.VMEM((GROUP * CHUNK, GROUP * CHUNK), jnp.bfloat16)],
        compiler_params=pltpu.CompilerParams(vmem_limit_bytes=40 * MIB),
        cost_estimate=pl.CostEstimate(
            flops=2 * total * GROUP * CHUNK * width, bytes_accessed=4 * total * width,
            transcendentals=0),
        name="unpack",
    )(raw)


def back_kernel(raw_ref, gate_ref, up_ref, w_gate_ref, w_up_ref, w_down_ref,
                grads_ref, cots_ref, act_ref, gate_grad_ref, up_grad_ref, dots_ref, unpack):
    @pl.when(pl.program_id(0) == 0)
    def _():
        unpack[...] = unpack_matrix(GROUP)

    unpack_rows(unpack[...], raw_ref, cots_ref)
    back = mm(cots_ref[...], w_down_ref[...], CONTRACT_LAST)
    gate_pre, up_value = gate_ref[...], up_ref[...]
    sigmoid = jax.nn.sigmoid(gate_pre)
    silu = gate_pre * sigmoid
    activated = (silu * up_value).astype(jnp.bfloat16)
    act_ref[...] = activated
    dots_ref[...] = jnp.sum(activated.astype(jnp.float32) * back, axis=-1, keepdims=True)
    gate_grad = (back * up_value * sigmoid * (1.0 + gate_pre * (1.0 - sigmoid))).astype(jnp.bfloat16)
    up_grad = (back * silu).astype(jnp.bfloat16)
    gate_grad_ref[...] = gate_grad
    up_grad_ref[...] = up_grad
    height = GROUP * CAP
    rows = GROUP * CHUNK
    width = raw_ref.shape[1]
    parts = []
    for b in range(BLOCKS):
        columns = slice(b * width, (b + 1) * width)
        parts.append(
            (mm(gate_grad, w_gate_ref[columns, :], CONTRACT_LAST)
             + mm(up_grad, w_up_ref[columns, :], CONTRACT_LAST)).astype(jnp.bfloat16)
        )
    for g in range(raw_ref.shape[0] // rows):
        stacked = jnp.concatenate([p[g * height:(g + 1) * height, :] for p in parts], axis=0)
        grads_ref[g * rows:(g + 1) * rows, :] = mm(
            unpack[...], stacked, CONTRACT_FIRST
        ).astype(jnp.bfloat16)


def expert_back(raw, gate_pre, up_value, w_gate, w_up, w_down, steps=4):
    total, width = raw.shape
    features, hidden = w_gate.shape
    slots = gate_pre.shape[0]
    rows = slots // steps
    tall = lambda shape: pl.BlockSpec(shape, lambda i: (i, 0))
    whole = lambda shape: pl.BlockSpec(shape, lambda i: (0, 0))
    small = jax.ShapeDtypeStruct((slots, hidden), jnp.bfloat16)
    return pl.pallas_call(
        back_kernel,
        grid=(steps,),
        in_specs=[tall((total // steps, width)), tall((rows, hidden)), tall((rows, hidden)),
                  whole(w_gate.shape), whole(w_up.shape), whole(w_down.shape)],
        out_specs=[tall((total // steps, width)), tall((rows, features))]
        + [tall((rows, hidden))] * 3 + [tall((rows, 1))],
        out_shape=[jax.ShapeDtypeStruct(raw.shape, jnp.bfloat16),
                   jax.ShapeDtypeStruct((slots, features), jnp.bfloat16),
                   small, small, small, jax.ShapeDtypeStruct((slots, 1), jnp.float32)],
        scratch_shapes=[pltpu.VMEM((GROUP * CHUNK, GROUP * CHUNK), jnp.bfloat16)],
        compiler_params=pltpu.CompilerParams(vmem_limit_bytes=56 * MIB),
        cost_estimate=pl.CostEstimate(
            flops=6 * slots * features * hidden + 4 * total * GROUP * CHUNK * width,
            bytes_accessed=32 * MIB, transcendentals=slots * hidden),
        name="expert_back",
    )(raw, gate_pre, up_value, w_gate, w_up, w_down)


def combine_kernel(ids_ref, back_ref, hidden_ref, gain_ref, cot_ref, resid_ref, slot, total):
    tokens, features = hidden_ref.shape
    width = features // BLOCKS
    experts = slot.shape[1]
    rows = back_ref.shape[0]
    step = pl.program_id(0)

    @pl.when(step == 0)
    def _():
        expert = iota((tokens, experts), 1)
        named = jnp.where((expert == ids_ref[:, 0:1]) | (expert == ids_ref[:, 1:2]), 1.0, 0.0)
        earlier = jnp.where(iota((tokens, tokens), 1) < iota((tokens, tokens), 0), 1.0, 0.0)
        prior = mm(earlier.astype(jnp.bfloat16), named.astype(jnp.bfloat16))
        slot[...] = jnp.where(named > 0.5, prior, -1.0).astype(jnp.bfloat16)
        total[...] = jnp.zeros_like(total)

    spread_at = iota((experts, rows), 1) // (2 * CHUNK) + step * (rows // (2 * CHUNK))
    spread = jnp.where(iota((experts, rows), 0) == spread_at, 1.0, 0.0).astype(jnp.bfloat16)
    slots = mm(slot[...], spread)
    lane = iota((tokens, rows), 1)
    piece = lane // CAP
    taken = jnp.where(slots == (lane - piece * CAP).astype(jnp.float32), 1.0, 0.0)
    block_of = piece - piece // BLOCKS * BLOCKS
    for b in range(BLOCKS):
        columns = slice(b * width, (b + 1) * width)
        pick = jnp.where(block_of == b, taken, 0.0).astype(jnp.bfloat16)
        total[:, columns] += mm(pick, back_ref[...])

    @pl.when(step == pl.num_programs(0) - 1)
    def _():
        wide = hidden_ref[...].astype(jnp.float32)
        scale = lax.rsqrt(jnp.mean(wide * wide, axis=-1, keepdims=True) + EPSILON)
        gained = total[...] * gain_ref[...]
        inner = jnp.mean(gained * wide, axis=-1, keepdims=True)
        resid_ref[...] = (
            cot_ref[...].astype(jnp.float32) + scale * gained - wide * (scale * scale * scale * inner)
        ).astype(jnp.bfloat16)


def combine(ids, back, hidden, gain, cots, experts, steps=8):
    tokens, features = hidden.shape
    total, width = back.shape
    whole = lambda shape: pl.BlockSpec(shape, lambda i: (0, 0))
    return pl.pallas_call(
        combine_kernel,
        grid=(steps,),
        in_specs=[whole(ids.shape), pl.BlockSpec((total // steps, width), lambda i: (i, 0)),
                  whole(hidden.shape), whole(gain.shape), whole(cots.shape)],
        out_specs=whole(hidden.shape),
        out_shape=jax.ShapeDtypeStruct(hidden.shape, jnp.bfloat16),
        scratch_shapes=[pltpu.VMEM((tokens, experts), jnp.bfloat16),
                        pltpu.VMEM((tokens, features), jnp.float32)],
        compiler_params=pltpu.CompilerParams(vmem_limit_bytes=40 * MIB),
        cost_estimate=pl.CostEstimate(
            flops=2 * BLOCKS * tokens * total * width, bytes_accessed=12 * MIB, transcendentals=0),
        name="combine",
    )(ids, back, hidden, gain, cots)


def per_device(
    ctx_heads,
    out_weight,
    hidden_in,
    norm_gain,
    expert_ids,
    route_weights,
    w_gate,
    w_up,
    w_down,
    grad_out,
):
    tokens, features = hidden_in.shape
    devices = lax.axis_size(("ctx", "tp"))
    experts = devices // 2
    axes = ("ctx", "tp")
    exchange = functools.partial(
        lax.all_to_all, axis_name=axes, split_axis=0, concat_axis=0, tiled=True
    )
    width = features // BLOCKS
    gain = norm_gain.reshape(1, features)
    rounded_weights = route_weights.astype(jnp.bfloat16).astype(jnp.float32)
    send_rows, send_cots = dispatch(
        expert_ids.T, rounded_weights.T, hidden_in, gain, grad_out, experts
    )
    raw_rows = exchange(send_rows.reshape(devices, CHUNK, width)).reshape(-1, width)
    raw_cots = exchange(send_cots.reshape(devices, CHUNK, width)).reshape(-1, width)
    slot_rows = unpack_chunks(raw_rows)
    gate_pre = mm(slot_rows, w_gate[0])
    up_value = mm(slot_rows, w_up[0])
    grads, slot_cots, activated, gate_grad, up_grad, dots = expert_back(
        raw_cots, gate_pre, up_value, w_gate[0], w_up[0], w_down[0]
    )
    back = exchange(grads.reshape(devices, CHUNK, width)).reshape(-1, width)
    back_dots = exchange(dots.reshape(devices, CAP).astype(jnp.bfloat16)).astype(jnp.float32)
    down_wgrad = mm(activated, slot_cots, CONTRACT_FIRST).astype(jnp.bfloat16)
    gate_wgrad = mm(slot_rows, gate_grad, CONTRACT_FIRST).astype(jnp.bfloat16)
    up_wgrad = mm(slot_rows, up_grad, CONTRACT_FIRST).astype(jnp.bfloat16)
    resid_grad = combine(expert_ids, back, hidden_in, gain, grad_out, experts)

    flat_ids = expert_ids.reshape(-1)
    onehot = (flat_ids[:, None] == jnp.arange(experts, dtype=jnp.int32)[None, :]).astype(jnp.int32)
    slot_rank = jnp.sum((jnp.cumsum(onehot, axis=0) - onehot) * onehot, axis=1)
    summed_dots = back_dots.reshape(experts, 2, CAP).sum(axis=1)
    picked = jnp.dot(onehot.astype(jnp.float32), summed_dots, precision=lax.Precision.HIGHEST)
    at_rank = slot_rank[:, None] == jnp.arange(CAP, dtype=jnp.int32)[None, :]
    route_grads = (
        jnp.sum(jnp.where(at_rank, picked, 0.0), axis=1).reshape(tokens, -1) / rounded_weights
    )

    grads_all = lax.all_gather(resid_grad, "tp", axis=0, tiled=True)
    heads_grad = mm(grads_all, lax.all_gather(out_weight, "ctx", axis=0, tiled=True)).astype(
        jnp.bfloat16
    )
    weight_grad = lax.psum_scatter(
        mm(grads_all, ctx_heads, CONTRACT_FIRST).astype(jnp.bfloat16),
        "ctx",
        scatter_dimension=0,
        tiled=True,
    )
    return (
        heads_grad,
        weight_grad,
        resid_grad,
        route_grads,
        gate_wgrad[None],
        up_wgrad[None],
        down_wgrad[None],
    )


def solution(mesh):
    split = P(("ctx", "tp"), None)
    stack = P(("ctx", "tp"), None, None)
    in_specs = (
        P("ctx", "tp"),
        P("ctx", "tp"),
        split,
        P(),
        split,
        split,
        stack,
        stack,
        stack,
        split,
    )
    out_specs = (P("ctx", "tp"), P("ctx", "tp"), split, split, stack, stack, stack)
    return jax.shard_map(
        per_device, mesh=mesh, in_specs=in_specs, out_specs=out_specs, check_vma=False
    )
```

```python
import functools

import jax
import jax.numpy as jnp
from jax import lax
from jax.experimental import pallas as pl
from jax.experimental.pallas import tpu as pltpu
from jax.sharding import PartitionSpec as P

EPSILON = 1e-06
CAP = 6
BLOCKS = 8
CHUNK = CAP * BLOCKS
CONTRACT_FIRST = (((0,), (0,)), ((), ()))
CONTRACT_LAST = (((1,), (1,)), ((), ()))
MIB = 1 << 20


def iota(shape, dim):
    return lax.broadcasted_iota(jnp.int32, shape, dim)


def mm(a, b, dims=(((1,), (0,)), ((), ()))):
    return lax.dot_general(a, b, dims, preferred_element_type=jnp.float32)


def dispatch_kernel(ids_ref, weight_ref, hidden_ref, gain_ref, cot_ref, rows_ref, cots_ref,
                    slot, weight, stacked_rows, stacked_cots):
    tokens, features = hidden_ref.shape
    width = features // BLOCKS
    experts = slot.shape[0]
    group = rows_ref.shape[0]
    step = pl.program_id(0)

    @pl.when(step == 0)
    def _():
        expert = iota((experts, tokens), 0)
        first = expert == ids_ref[0:1, :]
        second = expert == ids_ref[1:2, :]
        named = jnp.where(first | second, 1.0, 0.0)
        earlier = jnp.where(iota((tokens, tokens), 0) < iota((tokens, tokens), 1), 1.0, 0.0)
        prior = mm(named.astype(jnp.bfloat16), earlier.astype(jnp.bfloat16))
        slot[...] = jnp.where(named > 0.5, prior, -1.0)
        weight[...] = jnp.where(
            first, weight_ref[0:1, :], jnp.where(second, weight_ref[1:2, :], 0.0)
        )
        wide = hidden_ref[...].astype(jnp.float32)
        scale = lax.rsqrt(jnp.mean(wide * wide, axis=-1, keepdims=True) + EPSILON)
        for block in range(BLOCKS):
            columns = slice(block * width, (block + 1) * width)
            rows = slice(block * tokens, (block + 1) * tokens)
            stacked_rows[rows, :] = (
                hidden_ref[:, columns].astype(jnp.float32) * scale * gain_ref[:, columns]
            ).astype(jnp.bfloat16)
            stacked_cots[rows, :] = cot_ref[:, columns]

    here = pl.ds(pl.multiple_of(step * group, group), group)
    shape = (group, CHUNK, tokens)
    slots = jnp.broadcast_to(slot[here, :][:, None, :], shape)
    weights = jnp.broadcast_to(weight[here, :][:, None, :], shape)
    place = iota(shape, 1)
    block_of = place // CAP
    taken = slots == (place - block_of * CAP).astype(jnp.float32)
    weights = jnp.where(taken, weights, 0.0).reshape(group * CHUNK, tokens)
    taken = jnp.where(taken, 1.0, 0.0).reshape(group * CHUNK, tokens)
    block_of = block_of.reshape(group * CHUNK, tokens)
    pick_rows = jnp.concatenate(
        [jnp.where(block_of == b, taken, 0.0).astype(jnp.bfloat16) for b in range(BLOCKS)], axis=1
    )
    pick_cots = jnp.concatenate(
        [jnp.where(block_of == b, weights, 0.0).astype(jnp.bfloat16) for b in range(BLOCKS)], axis=1
    )
    rows = mm(pick_rows, stacked_rows[...]).astype(jnp.bfloat16).reshape(group, CHUNK, width)
    cots = mm(pick_cots, stacked_cots[...]).astype(jnp.bfloat16).reshape(group, CHUNK, width)
    for half in range(2):
        rows_ref[:, half] = rows
        cots_ref[:, half] = cots


def dispatch(ids_t, weights_t, hidden, gain, cots, experts):
    tokens, features = hidden.shape
    width = features // BLOCKS
    group = 8
    whole = lambda shape: pl.BlockSpec(shape, lambda i: (0, 0))
    out = jax.ShapeDtypeStruct((experts, 2, CHUNK, width), jnp.bfloat16)
    out_spec = pl.BlockSpec((group, 2, CHUNK, width), lambda i: (i, 0, 0, 0))
    return pl.pallas_call(
        dispatch_kernel,
        grid=(experts // group,),
        in_specs=[whole(ids_t.shape), whole(weights_t.shape), whole(hidden.shape),
                  whole(gain.shape), whole(cots.shape)],
        out_specs=[out_spec, out_spec],
        out_shape=[out, out],
        scratch_shapes=[
            pltpu.VMEM((experts, tokens), jnp.float32),
            pltpu.VMEM((experts, tokens), jnp.float32),
            pltpu.VMEM((BLOCKS * tokens, width), jnp.bfloat16),
            pltpu.VMEM((BLOCKS * tokens, width), jnp.bfloat16),
        ],
        compiler_params=pltpu.CompilerParams(vmem_limit_bytes=48 * MIB),
        cost_estimate=pl.CostEstimate(
            flops=4 * experts * CHUNK * tokens * features, bytes_accessed=16 * MIB,
            transcendentals=0),
        name="dispatch",
    )(ids_t, weights_t, hidden, gain, cots)


def unpack_matrix(sources):
    rows = sources * CHUNK
    out, inp = iota((rows, rows), 0), iota((rows, rows), 1)
    block = out // (sources * CAP)
    rest = out - block * (sources * CAP)
    source = rest // CAP
    want = source * CHUNK + block * CAP + (rest - source * CAP)
    return jnp.where(inp == want, 1.0, 0.0).astype(jnp.bfloat16)


GROUP = 8


def unpack_rows(unpack, raw_ref, out_ref):
    rows = GROUP * CHUNK
    height = GROUP * CAP
    width = raw_ref.shape[1]
    for g in range(raw_ref.shape[0] // rows):
        flat = mm(unpack, raw_ref[g * rows:(g + 1) * rows, :]).astype(jnp.bfloat16)
        for b in range(BLOCKS):
            out_ref[g * height:(g + 1) * height, b * width:(b + 1) * width] = (
                flat[b * height:(b + 1) * height, :]
            )


def unpack_kernel(raw_ref, out_ref, unpack):
    @pl.when(pl.program_id(0) == 0)
    def _():
        unpack[...] = unpack_matrix(GROUP)

    unpack_rows(unpack[...], raw_ref, out_ref)


def unpack_chunks(raw, steps=8):
    total, width = raw.shape
    rows = total // steps
    return pl.pallas_call(
        unpack_kernel,
        grid=(steps,),
        in_specs=[pl.BlockSpec((rows, width), lambda i: (i, 0))],
        out_specs=pl.BlockSpec((rows // BLOCKS, width * BLOCKS), lambda i: (i, 0)),
        out_shape=jax.ShapeDtypeStruct((total // BLOCKS, width * BLOCKS), jnp.bfloat16),
        scratch_shapes=[pltpu.VMEM((GROUP * CHUNK, GROUP * CHUNK), jnp.bfloat16)],
        compiler_params=pltpu.CompilerParams(vmem_limit_bytes=40 * MIB),
        cost_estimate=pl.CostEstimate(
            flops=2 * total * GROUP * CHUNK * width, bytes_accessed=4 * total * width,
            transcendentals=0),
        name="unpack",
    )(raw)


def back_kernel(raw_ref, gate_ref, up_ref, w_gate_ref, w_up_ref, w_down_ref,
                grads_ref, cots_ref, act_ref, gate_grad_ref, up_grad_ref, dots_ref, unpack):
    @pl.when(pl.program_id(0) == 0)
    def _():
        unpack[...] = unpack_matrix(GROUP)

    unpack_rows(unpack[...], raw_ref, cots_ref)
    back = mm(cots_ref[...], w_down_ref[...], CONTRACT_LAST)
    gate_pre, up_value = gate_ref[...], up_ref[...]
    sigmoid = jax.nn.sigmoid(gate_pre)
    silu = gate_pre * sigmoid
    activated = (silu * up_value).astype(jnp.bfloat16)
    act_ref[...] = activated
    dots_ref[...] = jnp.sum(activated.astype(jnp.float32) * back, axis=-1, keepdims=True)
    gate_grad = (back * up_value * sigmoid * (1.0 + gate_pre * (1.0 - sigmoid))).astype(jnp.bfloat16)
    up_grad = (back * silu).astype(jnp.bfloat16)
    gate_grad_ref[...] = gate_grad
    up_grad_ref[...] = up_grad
    height = GROUP * CAP
    rows = GROUP * CHUNK
    width = raw_ref.shape[1]
    parts = []
    for b in range(BLOCKS):
        columns = slice(b * width, (b + 1) * width)
        parts.append(
            (mm(gate_grad, w_gate_ref[columns, :], CONTRACT_LAST)
             + mm(up_grad, w_up_ref[columns, :], CONTRACT_LAST)).astype(jnp.bfloat16)
        )
    for g in range(raw_ref.shape[0] // rows):
        stacked = jnp.concatenate([p[g * height:(g + 1) * height, :] for p in parts], axis=0)
        grads_ref[g * rows:(g + 1) * rows, :] = mm(
            unpack[...], stacked, CONTRACT_FIRST
        ).astype(jnp.bfloat16)


def expert_back(raw, gate_pre, up_value, w_gate, w_up, w_down, steps=4):
    total, width = raw.shape
    features, hidden = w_gate.shape
    slots = gate_pre.shape[0]
    rows = slots // steps
    tall = lambda shape: pl.BlockSpec(shape, lambda i: (i, 0))
    whole = lambda shape: pl.BlockSpec(shape, lambda i: (0, 0))
    small = jax.ShapeDtypeStruct((slots, hidden), jnp.bfloat16)
    return pl.pallas_call(
        back_kernel,
        grid=(steps,),
        in_specs=[tall((total // steps, width)), tall((rows, hidden)), tall((rows, hidden)),
                  whole(w_gate.shape), whole(w_up.shape), whole(w_down.shape)],
        out_specs=[tall((total // steps, width)), tall((rows, features))]
        + [tall((rows, hidden))] * 3 + [tall((rows, 1))],
        out_shape=[jax.ShapeDtypeStruct(raw.shape, jnp.bfloat16),
                   jax.ShapeDtypeStruct((slots, features), jnp.bfloat16),
                   small, small, small, jax.ShapeDtypeStruct((slots, 1), jnp.float32)],
        scratch_shapes=[pltpu.VMEM((GROUP * CHUNK, GROUP * CHUNK), jnp.bfloat16)],
        compiler_params=pltpu.CompilerParams(vmem_limit_bytes=56 * MIB),
        cost_estimate=pl.CostEstimate(
            flops=6 * slots * features * hidden + 4 * total * GROUP * CHUNK * width,
            bytes_accessed=32 * MIB, transcendentals=slots * hidden),
        name="expert_back",
    )(raw, gate_pre, up_value, w_gate, w_up, w_down)


def combine_kernel(ids_ref, back_ref, hidden_ref, gain_ref, cot_ref, resid_ref, slot, total):
    tokens, features = hidden_ref.shape
    width = features // BLOCKS
    experts = slot.shape[1]
    rows = back_ref.shape[0]
    step = pl.program_id(0)

    @pl.when(step == 0)
    def _():
        expert = iota((tokens, experts), 1)
        named = jnp.where((expert == ids_ref[:, 0:1]) | (expert == ids_ref[:, 1:2]), 1.0, 0.0)
        earlier = jnp.where(iota((tokens, tokens), 1) < iota((tokens, tokens), 0), 1.0, 0.0)
        prior = mm(earlier.astype(jnp.bfloat16), named.astype(jnp.bfloat16))
        slot[...] = jnp.where(named > 0.5, prior, -1.0).astype(jnp.bfloat16)
        total[...] = jnp.zeros_like(total)

    spread_at = iota((experts, rows), 1) // (2 * CHUNK) + step * (rows // (2 * CHUNK))
    spread = jnp.where(iota((experts, rows), 0) == spread_at, 1.0, 0.0).astype(jnp.bfloat16)
    slots = mm(slot[...], spread)
    lane = iota((tokens, rows), 1)
    piece = lane // CAP
    taken = jnp.where(slots == (lane - piece * CAP).astype(jnp.float32), 1.0, 0.0)
    block_of = piece - piece // BLOCKS * BLOCKS
    for b in range(BLOCKS):
        columns = slice(b * width, (b + 1) * width)
        pick = jnp.where(block_of == b, taken, 0.0).astype(jnp.bfloat16)
        total[:, columns] += mm(pick, back_ref[...])

    @pl.when(step == pl.num_programs(0) - 1)
    def _():
        wide = hidden_ref[...].astype(jnp.float32)
        scale = lax.rsqrt(jnp.mean(wide * wide, axis=-1, keepdims=True) + EPSILON)
        gained = total[...] * gain_ref[...]
        inner = jnp.mean(gained * wide, axis=-1, keepdims=True)
        resid_ref[...] = (
            cot_ref[...].astype(jnp.float32) + scale * gained - wide * (scale * scale * scale * inner)
        ).astype(jnp.bfloat16)


def combine(ids, back, hidden, gain, cots, experts, steps=8):
    tokens, features = hidden.shape
    total, width = back.shape
    whole = lambda shape: pl.BlockSpec(shape, lambda i: (0, 0))
    return pl.pallas_call(
        combine_kernel,
        grid=(steps,),
        in_specs=[whole(ids.shape), pl.BlockSpec((total // steps, width), lambda i: (i, 0)),
                  whole(hidden.shape), whole(gain.shape), whole(cots.shape)],
        out_specs=whole(hidden.shape),
        out_shape=jax.ShapeDtypeStruct(hidden.shape, jnp.bfloat16),
        scratch_shapes=[pltpu.VMEM((tokens, experts), jnp.bfloat16),
                        pltpu.VMEM((tokens, features), jnp.float32)],
        compiler_params=pltpu.CompilerParams(vmem_limit_bytes=40 * MIB),
        cost_estimate=pl.CostEstimate(
            flops=2 * BLOCKS * tokens * total * width, bytes_accessed=12 * MIB, transcendentals=0),
        name="combine",
    )(ids, back, hidden, gain, cots)


STEPS = 4
SAME_L, SAME_R, SAME_T, SAME_B, FAR_C, FAR_L, FAR_R, FAR_T, FAR_B = range(9)
TO_Z, TO_R, TO_L, PASS_R, PASS_L, EXTRA_A, EXTRA_B, EXTRA_C, EXTRA_D = range(9)


def project_kernel(resid_ref, heads_ref, weight_ref, out_heads_ref, out_weight_ref,
                   pieces, total, partial, from_core, summed, from_y, to_z, from_z,
                   piece_send, piece_recv, core_send, core_recv, y_send, y_recv, z_send, z_recv):
    ctx, tp = lax.axis_index("ctx"), lax.axis_index("tp")
    y, z_hi, core = ctx // 4, (ctx // 2) % 2, ctx % 2
    z_lo, x = tp // 4, tp % 4
    right_x, left_x, opposite_x = (x + 1) % 4, (x + 3) % 4, (x + 2) % 4
    here, there = z_lo * 4, (1 - z_lo) * 4
    right, left, far = (ctx, here + right_x), (ctx, here + left_x), (ctx, there + x)
    sibling = (y * 4 + z_hi * 2 + (1 - core), tp)
    across = (y * 4 + (1 - z_hi) * 2 + core, tp)
    plane = lambda other: (other * 4 + z_hi * 2 + core, tp)
    tokens, features = resid_ref.shape
    chunk = features // STEPS
    rows = chunk // 4
    half = tokens // 2
    group = pieces.shape[1]

    barrier = pltpu.get_barrier_semaphore()
    peers = [right, left, far, sibling, across] + [plane((y + d) % 4) for d in (1, 2, 3)]
    for peer in peers:
        pl.semaphore_signal(barrier, inc=1, device_id=peer, device_id_type=pl.DeviceIdType.MESH)
    pl.semaphore_wait(barrier, len(peers))

    def remote(src, dst, send, recv, device):
        return pltpu.make_async_remote_copy(
            src_ref=src, dst_ref=dst, send_sem=send, recv_sem=recv,
            device_id=device, device_id_type=pl.DeviceIdType.MESH,
        )

    whole, top, bottom = pl.ds(0, tokens), pl.ds(0, half), pl.ds(half, half)
    sent = []

    def send(i, piece, part, kind, lands, device):
        ref = pieces.at[i, piece, part]
        copy = remote(ref, ref, piece_send.at[i, kind], piece_recv.at[i, lands], device)
        copy.start()
        sent.append(copy)

    def arrive(i, piece, part, lands):
        ref = pieces.at[i, piece, part]
        remote(ref, ref, piece_send.at[i, 0], piece_recv.at[i, lands], far).wait_recv()

    def owner(i):
        return (y + 1 + i) % 4

    def start_own(i):
        columns = pl.ds(pl.multiple_of(owner(i) * chunk, chunk), chunk)
        pieces[i, tp] = resid_ref[:, columns]
        send(i, tp, whole, TO_R, SAME_L, right)
        send(i, tp, whole, TO_L, SAME_R, left)
        send(i, tp, whole, TO_Z, FAR_C, far)

    def spread(i):
        if i % 2 == 0:
            arrive(i, there + x, whole, FAR_C)
            send(i, there + x, whole, EXTRA_A, FAR_L, right)
            send(i, there + x, whole, EXTRA_B, FAR_R, left)
        arrive(i, here + left_x, whole, SAME_L)
        send(i, here + left_x, top, PASS_R, SAME_T, right)
        if i % 2 == 1:
            send(i, here + left_x, whole, EXTRA_A, FAR_L, far)
        arrive(i, here + right_x, whole, SAME_R)
        send(i, here + right_x, bottom, PASS_L, SAME_B, left)
        if i % 2 == 1:
            send(i, here + right_x, whole, EXTRA_B, FAR_R, far)
        if i + 1 < STEPS:
            start_own(i + 1)
        if i % 2 == 0:
            arrive(i, there + left_x, whole, FAR_L)
            send(i, there + left_x, top, EXTRA_C, FAR_T, right)
            arrive(i, there + right_x, whole, FAR_R)
            send(i, there + right_x, bottom, EXTRA_D, FAR_B, left)
            arrive(i, here + opposite_x, top, SAME_T)
            arrive(i, here + opposite_x, bottom, SAME_B)
        else:
            arrive(i, here + opposite_x, top, SAME_T)
            send(i, here + opposite_x, top, EXTRA_C, FAR_T, far)
            arrive(i, here + opposite_x, bottom, SAME_B)
            send(i, here + opposite_x, bottom, EXTRA_D, FAR_B, far)
            arrive(i, there + x, whole, FAR_C)
            arrive(i, there + left_x, whole, FAR_L)
            arrive(i, there + right_x, whole, FAR_R)
        arrive(i, there + opposite_x, top, FAR_T)
        arrive(i, there + opposite_x, bottom, FAR_B)

    def weight_partial(i, whose):
        def one(zh, carry):
            first = pl.multiple_of((2 * zh + (core if whose == 0 else 1 - core)) * rows, rows)
            left_side = pieces[i, :, :, pl.ds(first, rows)].reshape(group * tokens, rows)
            partial[i, whose, zh] = mm(left_side, heads_ref[...], CONTRACT_FIRST).astype(jnp.bfloat16)
            return carry

        lax.fori_loop(0, 2, one, 0)

    def heads_partial(i):
        weight_rows = pl.ds(pl.multiple_of(owner(i) * chunk, chunk), chunk)

        def one(r, carry):
            tall = pl.ds(pl.multiple_of(r * 2 * tokens, 2 * tokens), 2 * tokens)
            left_side = pieces[i, pl.ds(2 * r, 2)].reshape(2 * tokens, chunk)
            value = mm(left_side, weight_ref[weight_rows, :])
            if i > 0:
                value = value + total[tall, :]
            if i < STEPS - 1:
                total[tall, :] = value
            else:
                out_heads_ref[tall, :] = value.astype(jnp.bfloat16)
            return carry

        lax.fori_loop(0, group // 2, one, 0)

    start_own(0)
    for i in range(STEPS):
        spread(i)
        weight_partial(i, 1)
        to_core = remote(partial.at[i, 1], from_core.at[i], core_send.at[i], core_recv.at[i], sibling)
        to_core.start()
        weight_partial(i, 0)
        heads_partial(i)
        to_core.wait()
        if i < STEPS - 1:
            summed[i] = (
                partial[i, 0].astype(jnp.float32) + from_core[i].astype(jnp.float32)
            ).astype(jnp.bfloat16)
            copy = remote(summed.at[i], from_y.at[i], y_send.at[i], y_recv.at[i], plane(owner(i)))
            copy.start()
            sent.append(copy)

    last = STEPS - 1
    for i in range(last):
        remote(summed.at[i], from_y.at[i], y_send.at[i], y_recv.at[i], across).wait_recv()

    def reduced(zh):
        value = partial[last, 0, zh].astype(jnp.float32) + from_core[last, zh].astype(jnp.float32)
        for i in range(last):
            value = value + from_y[i, zh].astype(jnp.float32)
        return value

    to_z[...] = reduced(1 - z_hi).astype(jnp.bfloat16)
    copy = remote(to_z, from_z, z_send, z_recv, across)
    copy.start()
    own = reduced(z_hi)
    copy.wait()
    out_weight_ref[...] = (own + from_z[...].astype(jnp.float32)).astype(jnp.bfloat16)
    for copy in sent:
        copy.wait_send()


def project(resid, heads, weight, group):
    tokens, features = resid.shape
    columns = heads.shape[1]
    chunk = features // STEPS
    rows = chunk // 4
    bf16 = jnp.bfloat16
    dma = pltpu.SemaphoreType.DMA
    vmem = pl.BlockSpec(memory_space=pltpu.VMEM)
    return pl.pallas_call(
        project_kernel,
        in_specs=[vmem] * 3,
        out_specs=[vmem] * 2,
        out_shape=[jax.ShapeDtypeStruct(heads.shape, bf16), jax.ShapeDtypeStruct((rows, columns), bf16)],
        scratch_shapes=[
            pltpu.VMEM((STEPS, group, tokens, chunk), bf16),
            pltpu.VMEM(heads.shape, jnp.float32),
            pltpu.VMEM((STEPS, 2, 2, rows, columns), bf16),
            pltpu.VMEM((STEPS, 2, rows, columns), bf16),
            pltpu.VMEM((STEPS - 1, 2, rows, columns), bf16),
            pltpu.VMEM((STEPS - 1, 2, rows, columns), bf16),
            pltpu.VMEM((rows, columns), bf16),
            pltpu.VMEM((rows, columns), bf16),
            dma((STEPS, 9)), dma((STEPS, 9)), dma((STEPS,)), dma((STEPS,)),
            dma((STEPS - 1,)), dma((STEPS - 1,)), dma, dma,
        ],
        compiler_params=pltpu.CompilerParams(
            collective_id=0, has_side_effects=True, vmem_limit_bytes=48 * MIB),
        cost_estimate=pl.CostEstimate(
            flops=4 * group * tokens * features * columns, bytes_accessed=8 * MIB, transcendentals=0),
        name="project",
    )(resid, heads, weight)


def per_device(
    ctx_heads,
    out_weight,
    hidden_in,
    norm_gain,
    expert_ids,
    route_weights,
    w_gate,
    w_up,
    w_down,
    grad_out,
):
    tokens, features = hidden_in.shape
    devices = lax.axis_size(("ctx", "tp"))
    experts = devices // 2
    axes = ("ctx", "tp")
    exchange = functools.partial(
        lax.all_to_all, axis_name=axes, split_axis=0, concat_axis=0, tiled=True
    )
    width = features // BLOCKS
    gain = norm_gain.reshape(1, features)
    rounded_weights = route_weights.astype(jnp.bfloat16).astype(jnp.float32)
    send_rows, send_cots = dispatch(
        expert_ids.T, rounded_weights.T, hidden_in, gain, grad_out, experts
    )
    raw_rows = exchange(send_rows.reshape(devices, CHUNK, width)).reshape(-1, width)
    raw_cots = exchange(send_cots.reshape(devices, CHUNK, width)).reshape(-1, width)
    slot_rows = unpack_chunks(raw_rows)
    full_weight = lax.all_gather(out_weight, "ctx", axis=0, tiled=True)
    gate_pre = mm(slot_rows, w_gate[0])
    up_value = mm(slot_rows, w_up[0])
    gate_pre, full_weight = lax.optimization_barrier((gate_pre, full_weight))
    grads, slot_cots, activated, gate_grad, up_grad, dots = expert_back(
        raw_cots, gate_pre, up_value, w_gate[0], w_up[0], w_down[0]
    )
    back = exchange(grads.reshape(devices, CHUNK, width)).reshape(-1, width)
    back_dots = exchange(dots.reshape(devices, CAP).astype(jnp.bfloat16)).astype(jnp.float32)
    down_wgrad = mm(activated, slot_cots, CONTRACT_FIRST).astype(jnp.bfloat16)
    gate_wgrad = mm(slot_rows, gate_grad, CONTRACT_FIRST).astype(jnp.bfloat16)
    up_wgrad = mm(slot_rows, up_grad, CONTRACT_FIRST).astype(jnp.bfloat16)
    resid_grad = combine(expert_ids, back, hidden_in, gain, grad_out, experts)

    flat_ids = expert_ids.reshape(-1)
    onehot = (flat_ids[:, None] == jnp.arange(experts, dtype=jnp.int32)[None, :]).astype(jnp.int32)
    slot_rank = jnp.sum((jnp.cumsum(onehot, axis=0) - onehot) * onehot, axis=1)
    summed_dots = back_dots.reshape(experts, 2, CAP).sum(axis=1)
    picked = jnp.dot(onehot.astype(jnp.float32), summed_dots, precision=lax.Precision.HIGHEST)
    at_rank = slot_rank[:, None] == jnp.arange(CAP, dtype=jnp.int32)[None, :]
    route_grads = (
        jnp.sum(jnp.where(at_rank, picked, 0.0), axis=1).reshape(tokens, -1) / rounded_weights
    )

    heads_grad, weight_grad = project(resid_grad, ctx_heads, full_weight, lax.axis_size("tp"))
    return (
        heads_grad,
        weight_grad,
        resid_grad,
        route_grads,
        gate_wgrad[None],
        up_wgrad[None],
        down_wgrad[None],
    )


def solution(mesh):
    split = P(("ctx", "tp"), None)
    stack = P(("ctx", "tp"), None, None)
    in_specs = (
        P("ctx", "tp"),
        P("ctx", "tp"),
        split,
        P(),
        split,
        split,
        stack,
        stack,
        stack,
        split,
    )
    out_specs = (P("ctx", "tp"), P("ctx", "tp"), split, split, stack, stack, stack)
    return jax.shard_map(
        per_device, mesh=mesh, in_specs=in_specs, out_specs=out_specs, check_vma=False
    )
```

```python
import functools

import jax
import jax.numpy as jnp
from jax import lax
from jax.experimental import pallas as pl
from jax.experimental.pallas import tpu as pltpu
from jax.sharding import PartitionSpec as P

EPSILON = 1e-06
CAP = 6
BLOCKS = 8
CHUNK = CAP * BLOCKS
CONTRACT_FIRST = (((0,), (0,)), ((), ()))
CONTRACT_LAST = (((1,), (1,)), ((), ()))
MIB = 1 << 20


def iota(shape, dim):
    return lax.broadcasted_iota(jnp.int32, shape, dim)


def mm(a, b, dims=(((1,), (0,)), ((), ()))):
    return lax.dot_general(a, b, dims, preferred_element_type=jnp.float32)


def dispatch_kernel(ids_ref, weight_ref, hidden_ref, gain_ref, cot_ref, rows_ref, cots_ref,
                    flat_rows, flat_cots, unpack):
    tokens, features = hidden_ref.shape
    width = features // BLOCKS
    experts = flat_rows.shape[0] // CAP
    group = rows_ref.shape[0]
    step = pl.program_id(0)

    @pl.when(step == 0)
    def _():
        expert = iota((experts, tokens), 0)
        first = expert == ids_ref[0:1, :]
        second = expert == ids_ref[1:2, :]
        named = jnp.where(first | second, 1.0, 0.0)
        earlier = jnp.where(iota((tokens, tokens), 0) < iota((tokens, tokens), 1), 1.0, 0.0)
        prior = mm(named.astype(jnp.bfloat16), earlier.astype(jnp.bfloat16))
        unpack[...] = unpack_matrix(group)
        slots = jnp.where(named > 0.5, prior, -1.0).astype(jnp.bfloat16)
        weights = jnp.where(
            first, weight_ref[0:1, :], jnp.where(second, weight_ref[1:2, :], 0.0)
        ).astype(jnp.bfloat16)
        row = iota((experts * CAP, experts), 0)
        expert_of = row // CAP
        spread = jnp.where(expert_of == iota((experts * CAP, experts), 1), 1.0, 0.0)
        spread = spread.astype(jnp.bfloat16)
        place = iota((experts * CAP, tokens), 0)
        place = (place - place // CAP * CAP).astype(jnp.float32)
        taken = mm(spread, slots) == place
        pick_rows = jnp.where(taken, 1.0, 0.0).astype(jnp.bfloat16)
        pick_cots = jnp.where(taken, mm(spread, weights), 0.0).astype(jnp.bfloat16)
        wide = hidden_ref[...].astype(jnp.float32)
        scale = lax.rsqrt(jnp.mean(wide * wide, axis=-1, keepdims=True) + EPSILON)
        for block in range(BLOCKS):
            columns = slice(block * width, (block + 1) * width)
            normed = (
                hidden_ref[:, columns].astype(jnp.float32) * scale * gain_ref[:, columns]
            ).astype(jnp.bfloat16)
            flat_rows[:, columns] = mm(pick_rows, normed).astype(jnp.bfloat16)
            flat_cots[:, columns] = mm(pick_cots, cot_ref[:, columns]).astype(jnp.bfloat16)

    height = group * CAP
    here = pl.ds(pl.multiple_of(step * height, height), height)
    rows, cots = (
        mm(
            unpack[...],
            jnp.concatenate(
                [flat[here, b * width:(b + 1) * width] for b in range(BLOCKS)], axis=0
            ),
            CONTRACT_FIRST,
        ).astype(jnp.bfloat16).reshape(group, CHUNK, width)
        for flat in (flat_rows, flat_cots)
    )
    for half in range(2):
        rows_ref[:, half] = rows
        cots_ref[:, half] = cots


def dispatch(ids_t, weights_t, hidden, gain, cots, experts):
    tokens, features = hidden.shape
    width = features // BLOCKS
    group = 8
    whole = lambda shape: pl.BlockSpec(shape, lambda i: (0, 0))
    out = jax.ShapeDtypeStruct((experts, 2, CHUNK, width), jnp.bfloat16)
    out_spec = pl.BlockSpec((group, 2, CHUNK, width), lambda i: (i, 0, 0, 0))
    return pl.pallas_call(
        dispatch_kernel,
        grid=(experts // group,),
        in_specs=[whole(ids_t.shape), whole(weights_t.shape), whole(hidden.shape),
                  whole(gain.shape), whole(cots.shape)],
        out_specs=[out_spec, out_spec],
        out_shape=[out, out],
        scratch_shapes=[
            pltpu.VMEM((experts * CAP, features), jnp.bfloat16),
            pltpu.VMEM((experts * CAP, features), jnp.bfloat16),
            pltpu.VMEM((group * CHUNK, group * CHUNK), jnp.bfloat16),
        ],
        compiler_params=pltpu.CompilerParams(vmem_limit_bytes=48 * MIB),
        cost_estimate=pl.CostEstimate(
            flops=4 * experts * CHUNK * tokens * features, bytes_accessed=16 * MIB,
            transcendentals=0),
        name="dispatch",
    )(ids_t, weights_t, hidden, gain, cots)


def unpack_matrix(sources):
    rows = sources * CHUNK
    out, inp = iota((rows, rows), 0), iota((rows, rows), 1)
    block = out // (sources * CAP)
    rest = out - block * (sources * CAP)
    source = rest // CAP
    want = source * CHUNK + block * CAP + (rest - source * CAP)
    return jnp.where(inp == want, 1.0, 0.0).astype(jnp.bfloat16)


GROUP = 8


def unpack_rows(unpack, raw_ref, out_ref):
    rows = GROUP * CHUNK
    height = GROUP * CAP
    width = raw_ref.shape[1]
    for g in range(raw_ref.shape[0] // rows):
        flat = mm(unpack, raw_ref[g * rows:(g + 1) * rows, :]).astype(jnp.bfloat16)
        for b in range(BLOCKS):
            out_ref[g * height:(g + 1) * height, b * width:(b + 1) * width] = (
                flat[b * height:(b + 1) * height, :]
            )


def unpack_kernel(raw_ref, out_ref, unpack):
    @pl.when(pl.program_id(0) == 0)
    def _():
        unpack[...] = unpack_matrix(GROUP)

    unpack_rows(unpack[...], raw_ref, out_ref)


def unpack_chunks(raw, steps=8):
    total, width = raw.shape
    rows = total // steps
    return pl.pallas_call(
        unpack_kernel,
        grid=(steps,),
        in_specs=[pl.BlockSpec((rows, width), lambda i: (i, 0))],
        out_specs=pl.BlockSpec((rows // BLOCKS, width * BLOCKS), lambda i: (i, 0)),
        out_shape=jax.ShapeDtypeStruct((total // BLOCKS, width * BLOCKS), jnp.bfloat16),
        scratch_shapes=[pltpu.VMEM((GROUP * CHUNK, GROUP * CHUNK), jnp.bfloat16)],
        compiler_params=pltpu.CompilerParams(vmem_limit_bytes=40 * MIB),
        cost_estimate=pl.CostEstimate(
            flops=2 * total * GROUP * CHUNK * width, bytes_accessed=4 * total * width,
            transcendentals=0),
        name="unpack",
    )(raw)


def back_kernel(raw_ref, gate_ref, up_ref, w_gate_ref, w_up_ref, w_down_ref,
                grads_ref, cots_ref, act_ref, gate_grad_ref, up_grad_ref, dots_ref, unpack):
    @pl.when(pl.program_id(0) == 0)
    def _():
        unpack[...] = unpack_matrix(GROUP)

    unpack_rows(unpack[...], raw_ref, cots_ref)
    back = mm(cots_ref[...], w_down_ref[...], CONTRACT_LAST)
    gate_pre, up_value = gate_ref[...], up_ref[...]
    sigmoid = jax.nn.sigmoid(gate_pre)
    silu = gate_pre * sigmoid
    activated = (silu * up_value).astype(jnp.bfloat16)
    act_ref[...] = activated
    dots_ref[...] = jnp.sum(activated.astype(jnp.float32) * back, axis=-1, keepdims=True)
    gate_grad = (back * up_value * sigmoid * (1.0 + gate_pre * (1.0 - sigmoid))).astype(jnp.bfloat16)
    up_grad = (back * silu).astype(jnp.bfloat16)
    gate_grad_ref[...] = gate_grad
    up_grad_ref[...] = up_grad
    height = GROUP * CAP
    rows = GROUP * CHUNK
    width = raw_ref.shape[1]
    parts = []
    for b in range(BLOCKS):
        columns = slice(b * width, (b + 1) * width)
        parts.append(
            (mm(gate_grad, w_gate_ref[columns, :], CONTRACT_LAST)
             + mm(up_grad, w_up_ref[columns, :], CONTRACT_LAST)).astype(jnp.bfloat16)
        )
    for g in range(raw_ref.shape[0] // rows):
        stacked = jnp.concatenate([p[g * height:(g + 1) * height, :] for p in parts], axis=0)
        grads_ref[g * rows:(g + 1) * rows, :] = mm(
            unpack[...], stacked, CONTRACT_FIRST
        ).astype(jnp.bfloat16)


def expert_back(raw, gate_pre, up_value, w_gate, w_up, w_down, steps=2):
    total, width = raw.shape
    features, hidden = w_gate.shape
    slots = gate_pre.shape[0]
    rows = slots // steps
    tall = lambda shape: pl.BlockSpec(shape, lambda i: (i, 0))
    whole = lambda shape: pl.BlockSpec(shape, lambda i: (0, 0))
    small = jax.ShapeDtypeStruct((slots, hidden), jnp.bfloat16)
    return pl.pallas_call(
        back_kernel,
        grid=(steps,),
        in_specs=[tall((total // steps, width)), tall((rows, hidden)), tall((rows, hidden)),
                  whole(w_gate.shape), whole(w_up.shape), whole(w_down.shape)],
        out_specs=[tall((total // steps, width)), tall((rows, features))]
        + [tall((rows, hidden))] * 3 + [tall((rows, 1))],
        out_shape=[jax.ShapeDtypeStruct(raw.shape, jnp.bfloat16),
                   jax.ShapeDtypeStruct((slots, features), jnp.bfloat16),
                   small, small, small, jax.ShapeDtypeStruct((slots, 1), jnp.float32)],
        scratch_shapes=[pltpu.VMEM((GROUP * CHUNK, GROUP * CHUNK), jnp.bfloat16)],
        compiler_params=pltpu.CompilerParams(vmem_limit_bytes=56 * MIB),
        cost_estimate=pl.CostEstimate(
            flops=6 * slots * features * hidden + 4 * total * GROUP * CHUNK * width,
            bytes_accessed=32 * MIB, transcendentals=slots * hidden),
        name="expert_back",
    )(raw, gate_pre, up_value, w_gate, w_up, w_down)


def combine_kernel(ids_ref, back_ref, hidden_ref, gain_ref, cot_ref, resid_ref, slot, total):
    tokens, features = hidden_ref.shape
    width = features // BLOCKS
    experts = slot.shape[1]
    rows = back_ref.shape[0]
    step = pl.program_id(0)

    @pl.when(step == 0)
    def _():
        expert = iota((tokens, experts), 1)
        named = jnp.where((expert == ids_ref[:, 0:1]) | (expert == ids_ref[:, 1:2]), 1.0, 0.0)
        earlier = jnp.where(iota((tokens, tokens), 1) < iota((tokens, tokens), 0), 1.0, 0.0)
        prior = mm(earlier.astype(jnp.bfloat16), named.astype(jnp.bfloat16))
        slot[...] = jnp.where(named > 0.5, prior, -1.0).astype(jnp.bfloat16)
        total[...] = jnp.zeros_like(total)

    spread_at = iota((experts, rows), 1) // (2 * CHUNK) + step * (rows // (2 * CHUNK))
    spread = jnp.where(iota((experts, rows), 0) == spread_at, 1.0, 0.0).astype(jnp.bfloat16)
    slots = mm(slot[...], spread)
    lane = iota((tokens, rows), 1)
    piece = lane // CAP
    taken = jnp.where(slots == (lane - piece * CAP).astype(jnp.float32), 1.0, 0.0)
    block_of = piece - piece // BLOCKS * BLOCKS
    picks = jnp.concatenate(
        [jnp.where(block_of == b, taken, 0.0).astype(jnp.bfloat16) for b in range(BLOCKS)], axis=0
    )
    total[...] += mm(picks, back_ref[...])

    @pl.when(step == pl.num_programs(0) - 1)
    def _():
        wide = hidden_ref[...].astype(jnp.float32)
        scale = lax.rsqrt(jnp.mean(wide * wide, axis=-1, keepdims=True) + EPSILON)
        inner = jnp.zeros((tokens, 1), jnp.float32)
        for b in range(BLOCKS):
            columns = slice(b * width, (b + 1) * width)
            rows = slice(b * tokens, (b + 1) * tokens)
            gained = total[rows, :] * gain_ref[:, columns]
            inner += jnp.sum(
                gained * hidden_ref[:, columns].astype(jnp.float32), axis=-1, keepdims=True
            )
        inner = (scale * scale * scale) * (inner / features)
        for b in range(BLOCKS):
            columns = slice(b * width, (b + 1) * width)
            rows = slice(b * tokens, (b + 1) * tokens)
            gained = total[rows, :] * gain_ref[:, columns]
            resid_ref[:, columns] = (
                cot_ref[:, columns].astype(jnp.float32) + scale * gained
                - hidden_ref[:, columns].astype(jnp.float32) * inner
            ).astype(jnp.bfloat16)


def combine(ids, back, hidden, gain, cots, experts, steps=8):
    tokens, features = hidden.shape
    total, width = back.shape
    whole = lambda shape: pl.BlockSpec(shape, lambda i: (0, 0))
    return pl.pallas_call(
        combine_kernel,
        grid=(steps,),
        in_specs=[whole(ids.shape), pl.BlockSpec((total // steps, width), lambda i: (i, 0)),
                  whole(hidden.shape), whole(gain.shape), whole(cots.shape)],
        out_specs=whole(hidden.shape),
        out_shape=jax.ShapeDtypeStruct(hidden.shape, jnp.bfloat16),
        scratch_shapes=[pltpu.VMEM((tokens, experts), jnp.bfloat16),
                        pltpu.VMEM((BLOCKS * tokens, width), jnp.float32)],
        compiler_params=pltpu.CompilerParams(vmem_limit_bytes=40 * MIB),
        cost_estimate=pl.CostEstimate(
            flops=2 * BLOCKS * tokens * total * width, bytes_accessed=12 * MIB, transcendentals=0),
        name="combine",
    )(ids, back, hidden, gain, cots)


STEPS = 4
SAME_L, SAME_R, SAME_T, SAME_B, FAR_C, FAR_L, FAR_R, FAR_T, FAR_B = range(9)
TO_Z, TO_R, TO_L, PASS_R, PASS_L, EXTRA_A, EXTRA_B, EXTRA_C, EXTRA_D = range(9)


def project_kernel(resid_ref, heads_ref, weight_ref, out_heads_ref, out_weight_ref,
                   pieces, total, partial, from_core, summed, from_y, to_z, from_z,
                   piece_send, piece_recv, core_send, core_recv, y_send, y_recv, z_send, z_recv):
    ctx, tp = lax.axis_index("ctx"), lax.axis_index("tp")
    y, z_hi, core = ctx // 4, (ctx // 2) % 2, ctx % 2
    z_lo, x = tp // 4, tp % 4
    right_x, left_x, opposite_x = (x + 1) % 4, (x + 3) % 4, (x + 2) % 4
    here, there = z_lo * 4, (1 - z_lo) * 4
    right, left, far = (ctx, here + right_x), (ctx, here + left_x), (ctx, there + x)
    sibling = (y * 4 + z_hi * 2 + (1 - core), tp)
    across = (y * 4 + (1 - z_hi) * 2 + core, tp)
    plane = lambda other: (other * 4 + z_hi * 2 + core, tp)
    tokens, features = resid_ref.shape
    chunk = features // STEPS
    rows = chunk // 4
    half = tokens // 2
    group = pieces.shape[1]

    barrier = pltpu.get_barrier_semaphore()
    peers = [right, left, far, sibling, across] + [plane((y + d) % 4) for d in (1, 2, 3)]
    for peer in peers:
        pl.semaphore_signal(barrier, inc=1, device_id=peer, device_id_type=pl.DeviceIdType.MESH)
    pl.semaphore_wait(barrier, len(peers))

    def remote(src, dst, send, recv, device):
        return pltpu.make_async_remote_copy(
            src_ref=src, dst_ref=dst, send_sem=send, recv_sem=recv,
            device_id=device, device_id_type=pl.DeviceIdType.MESH,
        )

    whole, top, bottom = pl.ds(0, tokens), pl.ds(0, half), pl.ds(half, half)
    sent = []

    def send(i, piece, part, kind, lands, device):
        ref = pieces.at[i, piece, part]
        copy = remote(ref, ref, piece_send.at[i, kind], piece_recv.at[i, lands], device)
        copy.start()
        sent.append(copy)

    def arrive(i, piece, part, lands):
        ref = pieces.at[i, piece, part]
        remote(ref, ref, piece_send.at[i, 0], piece_recv.at[i, lands], far).wait_recv()

    def owner(i):
        return (y + 1 + i) % 4

    def start_own(i):
        columns = pl.ds(pl.multiple_of(owner(i) * chunk, chunk), chunk)
        pieces[i, tp] = resid_ref[:, columns]
        send(i, tp, whole, TO_R, SAME_L, right)
        send(i, tp, whole, TO_L, SAME_R, left)
        send(i, tp, whole, TO_Z, FAR_C, far)

    def first_hops(i):
        if i % 2 == 0:
            arrive(i, there + x, whole, FAR_C)
            send(i, there + x, whole, EXTRA_A, FAR_L, right)
            send(i, there + x, whole, EXTRA_B, FAR_R, left)
        arrive(i, here + left_x, whole, SAME_L)
        send(i, here + left_x, top, PASS_R, SAME_T, right)
        if i % 2 == 1:
            send(i, here + left_x, whole, EXTRA_A, FAR_L, far)
        arrive(i, here + right_x, whole, SAME_R)
        send(i, here + right_x, bottom, PASS_L, SAME_B, left)
        if i % 2 == 1:
            send(i, here + right_x, whole, EXTRA_B, FAR_R, far)

    def second_hops(i):
        if i % 2 == 0:
            arrive(i, there + left_x, whole, FAR_L)
            send(i, there + left_x, top, EXTRA_C, FAR_T, right)
            arrive(i, there + right_x, whole, FAR_R)
            send(i, there + right_x, bottom, EXTRA_D, FAR_B, left)
        else:
            arrive(i, here + opposite_x, top, SAME_T)
            send(i, here + opposite_x, top, EXTRA_C, FAR_T, far)
            arrive(i, here + opposite_x, bottom, SAME_B)
            send(i, here + opposite_x, bottom, EXTRA_D, FAR_B, far)

    def arrivals(i):
        if i % 2 == 0:
            arrive(i, here + opposite_x, top, SAME_T)
            arrive(i, here + opposite_x, bottom, SAME_B)
        else:
            arrive(i, there + x, whole, FAR_C)
            arrive(i, there + left_x, whole, FAR_L)
            arrive(i, there + right_x, whole, FAR_R)
        arrive(i, there + opposite_x, top, FAR_T)
        arrive(i, there + opposite_x, bottom, FAR_B)

    def weight_partial(i, whose):
        def one(zh, carry):
            first = pl.multiple_of((2 * zh + (core if whose == 0 else 1 - core)) * rows, rows)
            left_side = pieces[i, :, :, pl.ds(first, rows)].reshape(group * tokens, rows)
            partial[i, whose, zh] = mm(left_side, heads_ref[...], CONTRACT_FIRST).astype(jnp.bfloat16)
            return carry

        lax.fori_loop(0, 2, one, 0)

    def heads_partial(i):
        weight_rows = pl.ds(pl.multiple_of(owner(i) * chunk, chunk), chunk)

        def one(r, carry):
            tall = pl.ds(pl.multiple_of(r * 2 * tokens, 2 * tokens), 2 * tokens)
            left_side = pieces[i, pl.ds(2 * r, 2)].reshape(2 * tokens, chunk)
            value = mm(left_side, weight_ref[weight_rows, :])
            if i > 0:
                value = value + total[tall, :]
            if i < STEPS - 1:
                total[tall, :] = value
            else:
                out_heads_ref[tall, :] = value.astype(jnp.bfloat16)
            return carry

        lax.fori_loop(0, group // 2, one, 0)

    def multiply(i, between=()):
        weight_partial(i, 1)
        to_core = remote(partial.at[i, 1], from_core.at[i], core_send.at[i], core_recv.at[i], sibling)
        to_core.start()
        weight_partial(i, 0)
        for hops, other in between:
            hops(other)
        heads_partial(i)
        to_core.wait()
        if i < STEPS - 1:
            summed[i] = (
                partial[i, 0].astype(jnp.float32) + from_core[i].astype(jnp.float32)
            ).astype(jnp.bfloat16)
            copy = remote(summed.at[i], from_y.at[i], y_send.at[i], y_recv.at[i], plane(owner(i)))
            copy.start()
            sent.append(copy)

    start_own(0)
    start_own(1)
    first_hops(0)
    first_hops(1)
    second_hops(0)
    start_own(2)
    second_hops(1)
    start_own(3)
    arrivals(0)
    multiply(0)
    arrivals(1)
    multiply(1, ((first_hops, 2), (first_hops, 3)))
    second_hops(2)
    second_hops(3)
    arrivals(2)
    multiply(2)
    arrivals(3)
    multiply(3)

    last = STEPS - 1
    for i in range(last):
        remote(summed.at[i], from_y.at[i], y_send.at[i], y_recv.at[i], across).wait_recv()

    def reduced(zh):
        value = partial[last, 0, zh].astype(jnp.float32) + from_core[last, zh].astype(jnp.float32)
        for i in range(last):
            value = value + from_y[i, zh].astype(jnp.float32)
        return value

    to_z[...] = reduced(1 - z_hi).astype(jnp.bfloat16)
    copy = remote(to_z, from_z, z_send, z_recv, across)
    copy.start()
    own = reduced(z_hi)
    copy.wait()
    out_weight_ref[...] = (own + from_z[...].astype(jnp.float32)).astype(jnp.bfloat16)
    for copy in sent:
        copy.wait_send()


def project(resid, heads, weight, group):
    tokens, features = resid.shape
    columns = heads.shape[1]
    chunk = features // STEPS
    rows = chunk // 4
    bf16 = jnp.bfloat16
    dma = pltpu.SemaphoreType.DMA
    vmem = pl.BlockSpec(memory_space=pltpu.VMEM)
    return pl.pallas_call(
        project_kernel,
        in_specs=[vmem] * 3,
        out_specs=[vmem] * 2,
        out_shape=[jax.ShapeDtypeStruct(heads.shape, bf16), jax.ShapeDtypeStruct((rows, columns), bf16)],
        scratch_shapes=[
            pltpu.VMEM((STEPS, group, tokens, chunk), bf16),
            pltpu.VMEM(heads.shape, jnp.float32),
            pltpu.VMEM((STEPS, 2, 2, rows, columns), bf16),
            pltpu.VMEM((STEPS, 2, rows, columns), bf16),
            pltpu.VMEM((STEPS - 1, 2, rows, columns), bf16),
            pltpu.VMEM((STEPS - 1, 2, rows, columns), bf16),
            pltpu.VMEM((rows, columns), bf16),
            pltpu.VMEM((rows, columns), bf16),
            dma((STEPS, 9)), dma((STEPS, 9)), dma((STEPS,)), dma((STEPS,)),
            dma((STEPS - 1,)), dma((STEPS - 1,)), dma, dma,
        ],
        compiler_params=pltpu.CompilerParams(
            collective_id=0, has_side_effects=True, vmem_limit_bytes=48 * MIB),
        cost_estimate=pl.CostEstimate(
            flops=4 * group * tokens * features * columns, bytes_accessed=8 * MIB, transcendentals=0),
        name="project",
    )(resid, heads, weight)


def per_device(
    ctx_heads,
    out_weight,
    hidden_in,
    norm_gain,
    expert_ids,
    route_weights,
    w_gate,
    w_up,
    w_down,
    grad_out,
):
    tokens, features = hidden_in.shape
    devices = lax.axis_size(("ctx", "tp"))
    experts = devices // 2
    axes = ("ctx", "tp")
    exchange = functools.partial(
        lax.all_to_all, axis_name=axes, split_axis=0, concat_axis=0, tiled=True
    )
    width = features // BLOCKS
    gain = norm_gain.reshape(1, features)
    rounded_weights = route_weights.astype(jnp.bfloat16).astype(jnp.float32)
    send_rows, send_cots = dispatch(
        expert_ids.T, rounded_weights.T, hidden_in, gain, grad_out, experts
    )
    raw_rows = exchange(send_rows.reshape(devices, CHUNK, width)).reshape(-1, width)
    raw_cots = exchange(send_cots.reshape(devices, CHUNK, width)).reshape(-1, width)
    slot_rows = unpack_chunks(raw_rows)
    full_weight = lax.all_gather(out_weight, "ctx", axis=0, tiled=True)
    gate_pre = mm(slot_rows, w_gate[0])
    up_value = mm(slot_rows, w_up[0])
    gate_pre, full_weight = lax.optimization_barrier((gate_pre, full_weight))
    grads, slot_cots, activated, gate_grad, up_grad, dots = expert_back(
        raw_cots, gate_pre, up_value, w_gate[0], w_up[0], w_down[0]
    )
    back = exchange(grads.reshape(devices, CHUNK, width)).reshape(-1, width)
    lanes = 128
    sent_dots = jnp.pad(dots.reshape(-1, lanes), ((0, 2), (0, 0))).astype(jnp.bfloat16)
    all_dots = lax.all_gather(sent_dots, axes, axis=0, tiled=True)
    me = lax.axis_index(axes)
    back_dots = lax.dynamic_slice(
        all_dots.reshape(devices, -1), (0, me * CAP), (devices, CAP)
    ).astype(jnp.float32)
    down_wgrad = mm(activated, slot_cots, CONTRACT_FIRST).astype(jnp.bfloat16)
    gate_wgrad = mm(slot_rows, gate_grad, CONTRACT_FIRST).astype(jnp.bfloat16)
    up_wgrad = mm(slot_rows, up_grad, CONTRACT_FIRST).astype(jnp.bfloat16)
    resid_grad = combine(expert_ids, back, hidden_in, gain, grad_out, experts)

    flat_ids = expert_ids.reshape(-1)
    onehot = (flat_ids[:, None] == jnp.arange(experts, dtype=jnp.int32)[None, :]).astype(jnp.int32)
    slot_rank = jnp.sum((jnp.cumsum(onehot, axis=0) - onehot) * onehot, axis=1)
    summed_dots = back_dots.reshape(experts, 2, CAP).sum(axis=1)
    picked = jnp.dot(onehot.astype(jnp.float32), summed_dots, precision=lax.Precision.HIGHEST)
    at_rank = slot_rank[:, None] == jnp.arange(CAP, dtype=jnp.int32)[None, :]
    route_grads = (
        jnp.sum(jnp.where(at_rank, picked, 0.0), axis=1).reshape(tokens, -1) / rounded_weights
    )

    heads_grad, weight_grad = project(resid_grad, ctx_heads, full_weight, lax.axis_size("tp"))
    return (
        heads_grad,
        weight_grad,
        resid_grad,
        route_grads,
        gate_wgrad[None],
        up_wgrad[None],
        down_wgrad[None],
    )


def solution(mesh):
    split = P(("ctx", "tp"), None)
    stack = P(("ctx", "tp"), None, None)
    in_specs = (
        P("ctx", "tp"),
        P("ctx", "tp"),
        split,
        P(),
        split,
        split,
        stack,
        stack,
        stack,
        split,
    )
    out_specs = (P("ctx", "tp"), P("ctx", "tp"), split, split, stack, stack, stack)
    return jax.shard_map(
        per_device, mesh=mesh, in_specs=in_specs, out_specs=out_specs, check_vma=False
    )
```

```python
import functools

import jax
import jax.numpy as jnp
from jax import lax
from jax.experimental import pallas as pl
from jax.experimental.pallas import tpu as pltpu
from jax.sharding import PartitionSpec as P

EPSILON = 1e-06
CAP = 6
BLOCKS = 8
CHUNK = CAP * BLOCKS
CONTRACT_FIRST = (((0,), (0,)), ((), ()))
CONTRACT_LAST = (((1,), (1,)), ((), ()))
MIB = 1 << 20


def iota(shape, dim):
    return lax.broadcasted_iota(jnp.int32, shape, dim)


def mm(a, b, dims=(((1,), (0,)), ((), ()))):
    return lax.dot_general(a, b, dims, preferred_element_type=jnp.float32)


def dispatch_kernel(normalize, ids_ref, weight_ref, value_ref, gain_ref, out_ref, flat, unpack):
    tokens, features = value_ref.shape
    width = features // BLOCKS
    experts = flat.shape[0] // CAP
    group = out_ref.shape[0]
    step = pl.program_id(0)

    @pl.when(step == 0)
    def _():
        expert = iota((experts, tokens), 0)
        first = expert == ids_ref[0:1, :]
        second = expert == ids_ref[1:2, :]
        named = jnp.where(first | second, 1.0, 0.0)
        earlier = jnp.where(iota((tokens, tokens), 0) < iota((tokens, tokens), 1), 1.0, 0.0)
        prior = mm(named.astype(jnp.bfloat16), earlier.astype(jnp.bfloat16))
        unpack[...] = unpack_matrix(group)
        slots = jnp.where(named > 0.5, prior, -1.0).astype(jnp.bfloat16)
        weights = jnp.where(
            first, weight_ref[0:1, :], jnp.where(second, weight_ref[1:2, :], 0.0)
        ).astype(jnp.bfloat16)
        row = iota((experts * CAP, experts), 0)
        expert_of = row // CAP
        spread = jnp.where(expert_of == iota((experts * CAP, experts), 1), 1.0, 0.0)
        spread = spread.astype(jnp.bfloat16)
        place = iota((experts * CAP, tokens), 0)
        place = (place - place // CAP * CAP).astype(jnp.float32)
        taken = mm(spread, slots) == place
        if normalize:
            picks = jnp.where(taken, 1.0, 0.0).astype(jnp.bfloat16)
            wide = value_ref[...].astype(jnp.float32)
            scale = lax.rsqrt(jnp.mean(wide * wide, axis=-1, keepdims=True) + EPSILON)
        else:
            picks = jnp.where(taken, mm(spread, weights), 0.0).astype(jnp.bfloat16)
        for block in range(BLOCKS):
            columns = slice(block * width, (block + 1) * width)
            values = value_ref[:, columns]
            if normalize:
                values = (values.astype(jnp.float32) * scale * gain_ref[:, columns]).astype(jnp.bfloat16)
            flat[:, columns] = mm(picks, values).astype(jnp.bfloat16)

    height = group * CAP
    here = pl.ds(pl.multiple_of(step * height, height), height)
    stacked = jnp.concatenate(
        [flat[here, b * width:(b + 1) * width] for b in range(BLOCKS)], axis=0
    )
    chunks = mm(unpack[...], stacked, CONTRACT_FIRST).astype(jnp.bfloat16)
    chunks = chunks.reshape(group, CHUNK, width)
    for half in range(2):
        out_ref[:, half] = chunks


def dispatch(normalize, ids_t, weights_t, values, gain, experts):
    tokens, features = values.shape
    width = features // BLOCKS
    group = 8
    whole = lambda shape: pl.BlockSpec(shape, lambda i: (0, 0))
    return pl.pallas_call(
        functools.partial(dispatch_kernel, normalize),
        grid=(experts // group,),
        in_specs=[whole(ids_t.shape), whole(weights_t.shape), whole(values.shape), whole(gain.shape)],
        out_specs=pl.BlockSpec((group, 2, CHUNK, width), lambda i: (i, 0, 0, 0)),
        out_shape=jax.ShapeDtypeStruct((experts, 2, CHUNK, width), jnp.bfloat16),
        scratch_shapes=[
            pltpu.VMEM((experts * CAP, features), jnp.bfloat16),
            pltpu.VMEM((group * CHUNK, group * CHUNK), jnp.bfloat16),
        ],
        compiler_params=pltpu.CompilerParams(vmem_limit_bytes=32 * MIB),
        cost_estimate=pl.CostEstimate(
            flops=2 * experts * CHUNK * tokens * features, bytes_accessed=8 * MIB,
            transcendentals=0),
        name="dispatch_rows" if normalize else "dispatch_cots",
    )(ids_t, weights_t, values, gain)


def unpack_matrix(sources):
    rows = sources * CHUNK
    out, inp = iota((rows, rows), 0), iota((rows, rows), 1)
    block = out // (sources * CAP)
    rest = out - block * (sources * CAP)
    source = rest // CAP
    want = source * CHUNK + block * CAP + (rest - source * CAP)
    return jnp.where(inp == want, 1.0, 0.0).astype(jnp.bfloat16)


GROUP = 8


def unpack_rows(unpack, raw_ref, out_ref):
    rows = GROUP * CHUNK
    height = GROUP * CAP
    width = raw_ref.shape[1]
    for g in range(raw_ref.shape[0] // rows):
        flat = mm(unpack, raw_ref[g * rows:(g + 1) * rows, :]).astype(jnp.bfloat16)
        for b in range(BLOCKS):
            out_ref[g * height:(g + 1) * height, b * width:(b + 1) * width] = (
                flat[b * height:(b + 1) * height, :]
            )


def unpack_kernel(raw_ref, out_ref, unpack):
    @pl.when(pl.program_id(0) == 0)
    def _():
        unpack[...] = unpack_matrix(GROUP)

    unpack_rows(unpack[...], raw_ref, out_ref)


def unpack_chunks(raw, steps=8):
    total, width = raw.shape
    rows = total // steps
    return pl.pallas_call(
        unpack_kernel,
        grid=(steps,),
        in_specs=[pl.BlockSpec((rows, width), lambda i: (i, 0))],
        out_specs=pl.BlockSpec((rows // BLOCKS, width * BLOCKS), lambda i: (i, 0)),
        out_shape=jax.ShapeDtypeStruct((total // BLOCKS, width * BLOCKS), jnp.bfloat16),
        scratch_shapes=[pltpu.VMEM((GROUP * CHUNK, GROUP * CHUNK), jnp.bfloat16)],
        compiler_params=pltpu.CompilerParams(vmem_limit_bytes=40 * MIB),
        cost_estimate=pl.CostEstimate(
            flops=2 * total * GROUP * CHUNK * width, bytes_accessed=4 * total * width,
            transcendentals=0),
        name="unpack",
    )(raw)


def back_kernel(raw_ref, gate_ref, up_ref, w_gate_ref, w_up_ref, w_down_ref,
                grads_ref, cots_ref, act_ref, gate_grad_ref, up_grad_ref, dots_ref, unpack):
    @pl.when(pl.program_id(0) == 0)
    def _():
        unpack[...] = unpack_matrix(GROUP)

    unpack_rows(unpack[...], raw_ref, cots_ref)
    back = mm(cots_ref[...], w_down_ref[...], CONTRACT_LAST)
    gate_pre, up_value = gate_ref[...], up_ref[...]
    sigmoid = jax.nn.sigmoid(gate_pre)
    silu = gate_pre * sigmoid
    activated = (silu * up_value).astype(jnp.bfloat16)
    act_ref[...] = activated
    dots_ref[...] = jnp.sum(activated.astype(jnp.float32) * back, axis=-1, keepdims=True)
    gate_grad = (back * up_value * sigmoid * (1.0 + gate_pre * (1.0 - sigmoid))).astype(jnp.bfloat16)
    up_grad = (back * silu).astype(jnp.bfloat16)
    gate_grad_ref[...] = gate_grad
    up_grad_ref[...] = up_grad
    height = GROUP * CAP
    rows = GROUP * CHUNK
    width = raw_ref.shape[1]
    parts = []
    for b in range(BLOCKS):
        columns = slice(b * width, (b + 1) * width)
        parts.append(
            (mm(gate_grad, w_gate_ref[columns, :], CONTRACT_LAST)
             + mm(up_grad, w_up_ref[columns, :], CONTRACT_LAST)).astype(jnp.bfloat16)
        )
    for g in range(raw_ref.shape[0] // rows):
        stacked = jnp.concatenate([p[g * height:(g + 1) * height, :] for p in parts], axis=0)
        grads_ref[g * rows:(g + 1) * rows, :] = mm(
            unpack[...], stacked, CONTRACT_FIRST
        ).astype(jnp.bfloat16)


def expert_back(raw, gate_pre, up_value, w_gate, w_up, w_down, steps=2):
    total, width = raw.shape
    features, hidden = w_gate.shape
    slots = gate_pre.shape[0]
    rows = slots // steps
    tall = lambda shape: pl.BlockSpec(shape, lambda i: (i, 0))
    whole = lambda shape: pl.BlockSpec(shape, lambda i: (0, 0))
    small = jax.ShapeDtypeStruct((slots, hidden), jnp.bfloat16)
    return pl.pallas_call(
        back_kernel,
        grid=(steps,),
        in_specs=[tall((total // steps, width)), tall((rows, hidden)), tall((rows, hidden)),
                  whole(w_gate.shape), whole(w_up.shape), whole(w_down.shape)],
        out_specs=[tall((total // steps, width)), tall((rows, features))]
        + [tall((rows, hidden))] * 3 + [tall((rows, 1))],
        out_shape=[jax.ShapeDtypeStruct(raw.shape, jnp.bfloat16),
                   jax.ShapeDtypeStruct((slots, features), jnp.bfloat16),
                   small, small, small, jax.ShapeDtypeStruct((slots, 1), jnp.float32)],
        scratch_shapes=[pltpu.VMEM((GROUP * CHUNK, GROUP * CHUNK), jnp.bfloat16)],
        compiler_params=pltpu.CompilerParams(vmem_limit_bytes=56 * MIB),
        cost_estimate=pl.CostEstimate(
            flops=6 * slots * features * hidden + 4 * total * GROUP * CHUNK * width,
            bytes_accessed=32 * MIB, transcendentals=slots * hidden),
        name="expert_back",
    )(raw, gate_pre, up_value, w_gate, w_up, w_down)


def combine_kernel(ids_ref, back_ref, hidden_ref, gain_ref, cot_ref, resid_ref, slot, total):
    tokens, features = hidden_ref.shape
    width = features // BLOCKS
    experts = slot.shape[1]
    rows = back_ref.shape[0]
    step = pl.program_id(0)

    @pl.when(step == 0)
    def _():
        expert = iota((tokens, experts), 1)
        named = jnp.where((expert == ids_ref[:, 0:1]) | (expert == ids_ref[:, 1:2]), 1.0, 0.0)
        earlier = jnp.where(iota((tokens, tokens), 1) < iota((tokens, tokens), 0), 1.0, 0.0)
        prior = mm(earlier.astype(jnp.bfloat16), named.astype(jnp.bfloat16))
        slot[...] = jnp.where(named > 0.5, prior, -1.0).astype(jnp.bfloat16)
        total[...] = jnp.zeros_like(total)

    spread_at = iota((experts, rows), 1) // (2 * CHUNK) + step * (rows // (2 * CHUNK))
    spread = jnp.where(iota((experts, rows), 0) == spread_at, 1.0, 0.0).astype(jnp.bfloat16)
    slots = mm(slot[...], spread)
    lane = iota((tokens, rows), 1)
    piece = lane // CAP
    taken = jnp.where(slots == (lane - piece * CAP).astype(jnp.float32), 1.0, 0.0)
    block_of = piece - piece // BLOCKS * BLOCKS
    picks = jnp.concatenate(
        [jnp.where(block_of == b, taken, 0.0).astype(jnp.bfloat16) for b in range(BLOCKS)], axis=0
    )
    total[...] += mm(picks, back_ref[...])

    @pl.when(step == pl.num_programs(0) - 1)
    def _():
        wide = hidden_ref[...].astype(jnp.float32)
        scale = lax.rsqrt(jnp.mean(wide * wide, axis=-1, keepdims=True) + EPSILON)
        inner = jnp.zeros((tokens, 1), jnp.float32)
        for b in range(BLOCKS):
            columns = slice(b * width, (b + 1) * width)
            rows = slice(b * tokens, (b + 1) * tokens)
            gained = total[rows, :] * gain_ref[:, columns]
            inner += jnp.sum(
                gained * hidden_ref[:, columns].astype(jnp.float32), axis=-1, keepdims=True
            )
        inner = (scale * scale * scale) * (inner / features)
        for b in range(BLOCKS):
            columns = slice(b * width, (b + 1) * width)
            rows = slice(b * tokens, (b + 1) * tokens)
            gained = total[rows, :] * gain_ref[:, columns]
            resid_ref[:, columns] = (
                cot_ref[:, columns].astype(jnp.float32) + scale * gained
                - hidden_ref[:, columns].astype(jnp.float32) * inner
            ).astype(jnp.bfloat16)


def combine(ids, back, hidden, gain, cots, experts, steps=8):
    tokens, features = hidden.shape
    total, width = back.shape
    whole = lambda shape: pl.BlockSpec(shape, lambda i: (0, 0))
    return pl.pallas_call(
        combine_kernel,
        grid=(steps,),
        in_specs=[whole(ids.shape), pl.BlockSpec((total // steps, width), lambda i: (i, 0)),
                  whole(hidden.shape), whole(gain.shape), whole(cots.shape)],
        out_specs=whole(hidden.shape),
        out_shape=jax.ShapeDtypeStruct(hidden.shape, jnp.bfloat16),
        scratch_shapes=[pltpu.VMEM((tokens, experts), jnp.bfloat16),
                        pltpu.VMEM((BLOCKS * tokens, width), jnp.float32)],
        compiler_params=pltpu.CompilerParams(vmem_limit_bytes=40 * MIB),
        cost_estimate=pl.CostEstimate(
            flops=2 * BLOCKS * tokens * total * width, bytes_accessed=12 * MIB, transcendentals=0),
        name="combine",
    )(ids, back, hidden, gain, cots)


STEPS = 4
SAME_L, SAME_R, SAME_T, SAME_B, FAR_C, FAR_L, FAR_R, FAR_T, FAR_B = range(9)
TO_Z, TO_R, TO_L, PASS_R, PASS_L, EXTRA_A, EXTRA_B, EXTRA_C, EXTRA_D = range(9)


def project_kernel(resid_ref, heads_ref, weight_ref, out_heads_ref, out_weight_ref,
                   pieces, total, partial, from_core, summed, from_y, to_z, from_z, blocks,
                   piece_send, piece_recv, core_send, core_recv, y_send, y_recv, z_send, z_recv,
                   block_send, block_y_recv, block_core_recv, block_z_recv):
    ctx, tp = lax.axis_index("ctx"), lax.axis_index("tp")
    y, z_hi, core = ctx // 4, (ctx // 2) % 2, ctx % 2
    z_lo, x = tp // 4, tp % 4
    right_x, left_x, opposite_x = (x + 1) % 4, (x + 3) % 4, (x + 2) % 4
    here, there = z_lo * 4, (1 - z_lo) * 4
    right, left, far = (ctx, here + right_x), (ctx, here + left_x), (ctx, there + x)
    sibling = (y * 4 + z_hi * 2 + (1 - core), tp)
    across = (y * 4 + (1 - z_hi) * 2 + core, tp)
    plane = lambda other: (other * 4 + z_hi * 2 + core, tp)
    tokens, features = resid_ref.shape
    chunk = features // STEPS
    rows = chunk // 4
    half = tokens // 2
    group = pieces.shape[1]

    barrier = pltpu.get_barrier_semaphore()
    peers = [right, left, far, sibling, across] + [plane((y + d) % 4) for d in (1, 2, 3)]
    for peer in peers:
        pl.semaphore_signal(barrier, inc=1, device_id=peer, device_id_type=pl.DeviceIdType.MESH)
    pl.semaphore_wait(barrier, len(peers))

    def remote(src, dst, send, recv, device):
        return pltpu.make_async_remote_copy(
            src_ref=src, dst_ref=dst, send_sem=send, recv_sem=recv,
            device_id=device, device_id_type=pl.DeviceIdType.MESH,
        )

    whole, top, bottom = pl.ds(0, tokens), pl.ds(0, half), pl.ds(half, half)
    sent = []

    def send(i, piece, part, kind, lands, device):
        ref = pieces.at[i, piece, part]
        copy = remote(ref, ref, piece_send.at[i, kind], piece_recv.at[i, lands], device)
        copy.start()
        sent.append(copy)

    def arrive(i, piece, part, lands):
        ref = pieces.at[i, piece, part]
        remote(ref, ref, piece_send.at[i, 0], piece_recv.at[i, lands], far).wait_recv()

    def owner(i):
        return (y + 1 + i) % 4

    def start_own(i):
        columns = pl.ds(pl.multiple_of(owner(i) * chunk, chunk), chunk)
        pieces[i, tp] = resid_ref[:, columns]
        send(i, tp, whole, TO_R, SAME_L, right)
        send(i, tp, whole, TO_L, SAME_R, left)
        send(i, tp, whole, TO_Z, FAR_C, far)

    def send_block(p, zh, semaphore, lands, device):
        ref = blocks.at[p, zh, core]
        copy = remote(ref, ref, semaphore, lands, device)
        copy.start()
        sent.append(copy)

    def block_arrives(p, zh, whose, lands):
        ref = blocks.at[p, zh, whose]
        remote(ref, ref, block_send.at[0], lands, sibling).wait_recv()

    def start_blocks():
        blocks[y, z_hi, core] = weight_ref[...]
        send_block(y, z_hi, block_send.at[0], block_z_recv, across)
        for i in range(STEPS - 1):
            send_block(y, z_hi, block_send.at[1 + i], block_y_recv.at[0, i], plane((y + 3 - i) % 4))
        send_block(y, z_hi, block_send.at[7], block_core_recv.at[0, STEPS - 1], sibling)

    def pass_blocks():
        block_arrives(y, 1 - z_hi, core, block_z_recv)
        for i in range(STEPS - 1):
            send_block(
                y, 1 - z_hi, block_send.at[4 + i], block_y_recv.at[1, i], plane((y + 3 - i) % 4)
            )
        send_block(y, 1 - z_hi, block_send.at[8], block_core_recv.at[1, STEPS - 1], sibling)

    def share_blocks(i):
        for side in range(2):
            zh = z_hi if side == 0 else 1 - z_hi
            block_arrives(owner(i), zh, core, block_y_recv.at[side, i])
            send_block(
                owner(i), zh, block_send.at[9 + 2 * i + side], block_core_recv.at[side, i], sibling
            )

    def blocks_ready(i):
        for side in range(2):
            zh = z_hi if side == 0 else 1 - z_hi
            block_arrives(owner(i), zh, 1 - core, block_core_recv.at[side, i])

    def first_hops(i):
        if i % 2 == 0:
            arrive(i, there + x, whole, FAR_C)
            send(i, there + x, whole, EXTRA_A, FAR_L, right)
            send(i, there + x, whole, EXTRA_B, FAR_R, left)
        arrive(i, here + left_x, whole, SAME_L)
        send(i, here + left_x, top, PASS_R, SAME_T, right)
        if i % 2 == 1:
            send(i, here + left_x, whole, EXTRA_A, FAR_L, far)
        arrive(i, here + right_x, whole, SAME_R)
        send(i, here + right_x, bottom, PASS_L, SAME_B, left)
        if i % 2 == 1:
            send(i, here + right_x, whole, EXTRA_B, FAR_R, far)

    def second_hops(i):
        if i % 2 == 0:
            arrive(i, there + left_x, whole, FAR_L)
            send(i, there + left_x, top, EXTRA_C, FAR_T, right)
            arrive(i, there + right_x, whole, FAR_R)
            send(i, there + right_x, bottom, EXTRA_D, FAR_B, left)
        else:
            arrive(i, here + opposite_x, top, SAME_T)
            send(i, here + opposite_x, top, EXTRA_C, FAR_T, far)
            arrive(i, here + opposite_x, bottom, SAME_B)
            send(i, here + opposite_x, bottom, EXTRA_D, FAR_B, far)

    def arrivals(i):
        if i % 2 == 0:
            arrive(i, here + opposite_x, top, SAME_T)
            arrive(i, here + opposite_x, bottom, SAME_B)
        else:
            arrive(i, there + x, whole, FAR_C)
            arrive(i, there + left_x, whole, FAR_L)
            arrive(i, there + right_x, whole, FAR_R)
        arrive(i, there + opposite_x, top, FAR_T)
        arrive(i, there + opposite_x, bottom, FAR_B)

    def weight_partial(i, whose):
        def one(zh, carry):
            first = pl.multiple_of((2 * zh + (core if whose == 0 else 1 - core)) * rows, rows)
            left_side = pieces[i, :, :, pl.ds(first, rows)].reshape(group * tokens, rows)
            partial[i, whose, zh] = mm(left_side, heads_ref[...], CONTRACT_FIRST).astype(jnp.bfloat16)
            return carry

        lax.fori_loop(0, 2, one, 0)

    def heads_partial(i):
        def one(r, carry):
            tall = pl.ds(pl.multiple_of(r * 2 * tokens, 2 * tokens), 2 * tokens)
            left_side = pieces[i, pl.ds(2 * r, 2)].reshape(2 * tokens, chunk)
            value = mm(left_side, blocks[owner(i)].reshape(chunk, blocks.shape[-1]))
            if i > 0:
                value = value + total[tall, :]
            if i < STEPS - 1:
                total[tall, :] = value
            else:
                out_heads_ref[tall, :] = value.astype(jnp.bfloat16)
            return carry

        lax.fori_loop(0, group // 2, one, 0)

    def multiply(i, between=()):
        weight_partial(i, 1)
        to_core = remote(partial.at[i, 1], from_core.at[i], core_send.at[i], core_recv.at[i], sibling)
        to_core.start()
        weight_partial(i, 0)
        for hops, other in between:
            hops(other)
        blocks_ready(i)
        heads_partial(i)
        to_core.wait()
        if i < STEPS - 1:
            summed[i] = (
                partial[i, 0].astype(jnp.float32) + from_core[i].astype(jnp.float32)
            ).astype(jnp.bfloat16)
            copy = remote(summed.at[i], from_y.at[i], y_send.at[i], y_recv.at[i], plane(owner(i)))
            copy.start()
            sent.append(copy)

    start_own(0)
    start_own(1)
    start_blocks()
    first_hops(0)
    pass_blocks()
    first_hops(1)
    second_hops(0)
    start_own(2)
    second_hops(1)
    start_own(3)
    share_blocks(0)
    arrivals(0)
    multiply(0, ((share_blocks, 1),))
    arrivals(1)
    multiply(1, ((first_hops, 2), (first_hops, 3), (share_blocks, 2)))
    second_hops(2)
    second_hops(3)
    arrivals(2)
    multiply(2)
    arrivals(3)
    multiply(3)

    last = STEPS - 1
    for i in range(last):
        remote(summed.at[i], from_y.at[i], y_send.at[i], y_recv.at[i], across).wait_recv()

    def reduced(zh):
        value = partial[last, 0, zh].astype(jnp.float32) + from_core[last, zh].astype(jnp.float32)
        for i in range(last):
            value = value + from_y[i, zh].astype(jnp.float32)
        return value

    to_z[...] = reduced(1 - z_hi).astype(jnp.bfloat16)
    copy = remote(to_z, from_z, z_send, z_recv, across)
    copy.start()
    own = reduced(z_hi)
    copy.wait()
    out_weight_ref[...] = (own + from_z[...].astype(jnp.float32)).astype(jnp.bfloat16)
    for copy in sent:
        copy.wait_send()


def project(resid, heads, weight, group):
    tokens, features = resid.shape
    columns = heads.shape[1]
    chunk = features // STEPS
    rows = chunk // 4
    bf16 = jnp.bfloat16
    dma = pltpu.SemaphoreType.DMA
    vmem = pl.BlockSpec(memory_space=pltpu.VMEM)
    return pl.pallas_call(
        project_kernel,
        in_specs=[vmem] * 3,
        out_specs=[vmem] * 2,
        out_shape=[jax.ShapeDtypeStruct(heads.shape, bf16), jax.ShapeDtypeStruct((rows, columns), bf16)],
        scratch_shapes=[
            pltpu.VMEM((STEPS, group, tokens, chunk), bf16),
            pltpu.VMEM(heads.shape, jnp.float32),
            pltpu.VMEM((STEPS, 2, 2, rows, columns), bf16),
            pltpu.VMEM((STEPS, 2, rows, columns), bf16),
            pltpu.VMEM((STEPS - 1, 2, rows, columns), bf16),
            pltpu.VMEM((STEPS - 1, 2, rows, columns), bf16),
            pltpu.VMEM((rows, columns), bf16),
            pltpu.VMEM((rows, columns), bf16),
            pltpu.VMEM((STEPS, 2, 2, rows, columns), bf16),
            dma((STEPS, 9)), dma((STEPS, 9)), dma((STEPS,)), dma((STEPS,)),
            dma((STEPS - 1,)), dma((STEPS - 1,)), dma, dma,
            dma((15,)), dma((2, STEPS - 1)), dma((2, STEPS)), dma,
        ],
        compiler_params=pltpu.CompilerParams(
            collective_id=0, has_side_effects=True, vmem_limit_bytes=48 * MIB),
        cost_estimate=pl.CostEstimate(
            flops=4 * group * tokens * features * columns, bytes_accessed=8 * MIB, transcendentals=0),
        name="project",
    )(resid, heads, weight)


def per_device(
    ctx_heads,
    out_weight,
    hidden_in,
    norm_gain,
    expert_ids,
    route_weights,
    w_gate,
    w_up,
    w_down,
    grad_out,
):
    tokens, features = hidden_in.shape
    devices = lax.axis_size(("ctx", "tp"))
    experts = devices // 2
    axes = ("ctx", "tp")
    exchange = functools.partial(
        lax.all_to_all, axis_name=axes, split_axis=0, concat_axis=0, tiled=True
    )
    width = features // BLOCKS
    gain = norm_gain.reshape(1, features)
    rounded_weights = route_weights.astype(jnp.bfloat16).astype(jnp.float32)
    ids_t, weights_t = expert_ids.T, rounded_weights.T
    send_rows = dispatch(True, ids_t, weights_t, hidden_in, gain, experts)
    send_cots = dispatch(False, ids_t, weights_t, grad_out, gain, experts)
    raw_rows = exchange(send_rows.reshape(devices, CHUNK, width)).reshape(-1, width)
    raw_cots = exchange(send_cots.reshape(devices, CHUNK, width)).reshape(-1, width)
    slot_rows = unpack_chunks(raw_rows)
    gate_pre = mm(slot_rows, w_gate[0])
    up_value = mm(slot_rows, w_up[0])
    grads, slot_cots, activated, gate_grad, up_grad, dots = expert_back(
        raw_cots, gate_pre, up_value, w_gate[0], w_up[0], w_down[0]
    )
    back = exchange(grads.reshape(devices, CHUNK, width)).reshape(-1, width)
    back, dots = lax.optimization_barrier((back, dots))
    back_dots = exchange(dots.reshape(devices, CAP).astype(jnp.bfloat16)).astype(jnp.float32)
    down_wgrad = mm(activated, slot_cots, CONTRACT_FIRST).astype(jnp.bfloat16)
    gate_wgrad = mm(slot_rows, gate_grad, CONTRACT_FIRST).astype(jnp.bfloat16)
    up_wgrad = mm(slot_rows, up_grad, CONTRACT_FIRST).astype(jnp.bfloat16)
    resid_grad = combine(expert_ids, back, hidden_in, gain, grad_out, experts)

    flat_ids = expert_ids.reshape(-1)
    onehot = (flat_ids[:, None] == jnp.arange(experts, dtype=jnp.int32)[None, :]).astype(jnp.int32)
    slot_rank = jnp.sum((jnp.cumsum(onehot, axis=0) - onehot) * onehot, axis=1)
    summed_dots = back_dots.reshape(experts, 2, CAP).sum(axis=1)
    picked = jnp.dot(onehot.astype(jnp.float32), summed_dots, precision=lax.Precision.HIGHEST)
    at_rank = slot_rank[:, None] == jnp.arange(CAP, dtype=jnp.int32)[None, :]
    route_grads = (
        jnp.sum(jnp.where(at_rank, picked, 0.0), axis=1).reshape(tokens, -1) / rounded_weights
    )

    heads_grad, weight_grad = project(resid_grad, ctx_heads, out_weight, lax.axis_size("tp"))
    return (
        heads_grad,
        weight_grad,
        resid_grad,
        route_grads,
        gate_wgrad[None],
        up_wgrad[None],
        down_wgrad[None],
    )


def solution(mesh):
    split = P(("ctx", "tp"), None)
    stack = P(("ctx", "tp"), None, None)
    in_specs = (
        P("ctx", "tp"),
        P("ctx", "tp"),
        split,
        P(),
        split,
        split,
        stack,
        stack,
        stack,
        split,
    )
    out_specs = (P("ctx", "tp"), P("ctx", "tp"), split, split, stack, stack, stack)
    return jax.shard_map(
        per_device, mesh=mesh, in_specs=in_specs, out_specs=out_specs, check_vma=False
    )
```

```python
import functools

import jax
import jax.numpy as jnp
from jax import lax
from jax.experimental import pallas as pl
from jax.experimental.pallas import tpu as pltpu
from jax.sharding import PartitionSpec as P

EPSILON = 1e-06
CAP = 6
BLOCKS = 4
CHUNK = CAP * BLOCKS
CONTRACT_FIRST = (((0,), (0,)), ((), ()))
CONTRACT_LAST = (((1,), (1,)), ((), ()))
MIB = 1 << 20


def iota(shape, dim):
    return lax.broadcasted_iota(jnp.int32, shape, dim)


def mm(a, b, dims=(((1,), (0,)), ((), ()))):
    return lax.dot_general(a, b, dims, preferred_element_type=jnp.float32)


def dispatch_kernel(normalize, ids_ref, weight_ref, value_ref, gain_ref, out_ref, flat, unpack):
    tokens, features = value_ref.shape
    width = features // BLOCKS
    experts = flat.shape[0] // CAP
    group = out_ref.shape[0]
    step = pl.program_id(0)

    @pl.when(step == 0)
    def _():
        expert = iota((experts, tokens), 0)
        first = expert == ids_ref[0:1, :]
        second = expert == ids_ref[1:2, :]
        named = jnp.where(first | second, 1.0, 0.0)
        earlier = jnp.where(iota((tokens, tokens), 0) < iota((tokens, tokens), 1), 1.0, 0.0)
        prior = mm(named.astype(jnp.bfloat16), earlier.astype(jnp.bfloat16))
        unpack[...] = unpack_matrix(group)
        slots = jnp.where(named > 0.5, prior, -1.0).astype(jnp.bfloat16)
        weights = jnp.where(
            first, weight_ref[0:1, :], jnp.where(second, weight_ref[1:2, :], 0.0)
        ).astype(jnp.bfloat16)
        row = iota((experts * CAP, experts), 0)
        expert_of = row // CAP
        spread = jnp.where(expert_of == iota((experts * CAP, experts), 1), 1.0, 0.0)
        spread = spread.astype(jnp.bfloat16)
        place = iota((experts * CAP, tokens), 0)
        place = (place - place // CAP * CAP).astype(jnp.float32)
        taken = mm(spread, slots) == place
        if normalize:
            picks = jnp.where(taken, 1.0, 0.0).astype(jnp.bfloat16)
            wide = value_ref[...].astype(jnp.float32)
            scale = lax.rsqrt(jnp.mean(wide * wide, axis=-1, keepdims=True) + EPSILON)
        else:
            picks = jnp.where(taken, mm(spread, weights), 0.0).astype(jnp.bfloat16)
        for block in range(BLOCKS):
            columns = slice(block * width, (block + 1) * width)
            values = value_ref[:, columns]
            if normalize:
                values = (values.astype(jnp.float32) * scale * gain_ref[:, columns]).astype(jnp.bfloat16)
            flat[:, columns] = mm(picks, values).astype(jnp.bfloat16)

    height = group * CAP
    here = pl.ds(pl.multiple_of(step * height, height), height)
    stacked = jnp.concatenate(
        [flat[here, b * width:(b + 1) * width] for b in range(BLOCKS)], axis=0
    )
    chunks = mm(unpack[...], stacked, CONTRACT_FIRST).reshape(group, CHUNK, width)
    chunks = chunks.astype(jnp.bfloat16)
    for half in range(2):
        out_ref[:, half] = chunks


def dispatch(normalize, ids_t, weights_t, values, gain, experts):
    tokens, features = values.shape
    width = features // BLOCKS
    group = 8
    whole = lambda shape: pl.BlockSpec(shape, lambda i: (0, 0))
    return pl.pallas_call(
        functools.partial(dispatch_kernel, normalize),
        grid=(experts // group,),
        in_specs=[whole(ids_t.shape), whole(weights_t.shape), whole(values.shape), whole(gain.shape)],
        out_specs=pl.BlockSpec((group, 2, CHUNK, width), lambda i: (i, 0, 0, 0)),
        out_shape=jax.ShapeDtypeStruct((experts, 2, CHUNK, width), jnp.bfloat16),
        scratch_shapes=[
            pltpu.VMEM((experts * CAP, features), jnp.bfloat16),
            pltpu.VMEM((group * CHUNK, group * CHUNK), jnp.bfloat16),
        ],
        compiler_params=pltpu.CompilerParams(vmem_limit_bytes=60 * MIB),
        cost_estimate=pl.CostEstimate(
            flops=2 * experts * CHUNK * tokens * features, bytes_accessed=8 * MIB,
            transcendentals=0),
        name="dispatch_rows" if normalize else "dispatch_cots",
    )(ids_t, weights_t, values, gain)


def unpack_matrix(sources):
    rows = sources * CHUNK
    out, inp = iota((rows, rows), 0), iota((rows, rows), 1)
    block = out // (sources * CAP)
    rest = out - block * (sources * CAP)
    source = rest // CAP
    want = source * CHUNK + block * CAP + (rest - source * CAP)
    return jnp.where(inp == want, 1.0, 0.0).astype(jnp.bfloat16)


GROUP = 8


def unpack_rows(unpack, raw_ref, out_ref):
    rows = GROUP * CHUNK
    height = GROUP * CAP
    width = raw_ref.shape[1]
    for g in range(raw_ref.shape[0] // rows):
        flat = mm(unpack, raw_ref[g * rows:(g + 1) * rows, :]).astype(jnp.bfloat16)
        for b in range(BLOCKS):
            out_ref[g * height:(g + 1) * height, b * width:(b + 1) * width] = (
                flat[b * height:(b + 1) * height, :]
            )


def unpack_kernel(raw_ref, out_ref, unpack):
    @pl.when(pl.program_id(0) == 0)
    def _():
        unpack[...] = unpack_matrix(GROUP)

    unpack_rows(unpack[...], raw_ref, out_ref)


def unpack_chunks(raw, steps=8):
    total, width = raw.shape
    rows = total // steps
    return pl.pallas_call(
        unpack_kernel,
        grid=(steps,),
        in_specs=[pl.BlockSpec((rows, width), lambda i: (i, 0))],
        out_specs=pl.BlockSpec((rows // BLOCKS, width * BLOCKS), lambda i: (i, 0)),
        out_shape=jax.ShapeDtypeStruct((total // BLOCKS, width * BLOCKS), jnp.bfloat16),
        scratch_shapes=[pltpu.VMEM((GROUP * CHUNK, GROUP * CHUNK), jnp.bfloat16)],
        compiler_params=pltpu.CompilerParams(vmem_limit_bytes=40 * MIB),
        cost_estimate=pl.CostEstimate(
            flops=2 * total * GROUP * CHUNK * width, bytes_accessed=4 * total * width,
            transcendentals=0),
        name="unpack",
    )(raw)


def back_kernel(raw_ref, gate_ref, up_ref, w_gate_ref, w_up_ref, w_down_ref,
                grads_ref, cots_ref, act_ref, gate_grad_ref, up_grad_ref, dots_ref, unpack):
    @pl.when(pl.program_id(0) == 0)
    def _():
        unpack[...] = unpack_matrix(GROUP)

    unpack_rows(unpack[...], raw_ref, cots_ref)
    back = mm(cots_ref[...], w_down_ref[...], CONTRACT_LAST)
    gate_pre, up_value = gate_ref[...], up_ref[...]
    sigmoid = jax.nn.sigmoid(gate_pre)
    silu = gate_pre * sigmoid
    activated = (silu * up_value).astype(jnp.bfloat16)
    act_ref[...] = activated
    dots_ref[...] = jnp.sum(activated.astype(jnp.float32) * back, axis=-1, keepdims=True)
    gate_grad = (back * up_value * sigmoid * (1.0 + gate_pre * (1.0 - sigmoid))).astype(jnp.bfloat16)
    up_grad = (back * silu).astype(jnp.bfloat16)
    gate_grad_ref[...] = gate_grad
    up_grad_ref[...] = up_grad
    height = GROUP * CAP
    rows = GROUP * CHUNK
    width = raw_ref.shape[1]
    parts = []
    for b in range(BLOCKS):
        columns = slice(b * width, (b + 1) * width)
        parts.append(
            (mm(gate_grad, w_gate_ref[columns, :], CONTRACT_LAST)
             + mm(up_grad, w_up_ref[columns, :], CONTRACT_LAST)).astype(jnp.bfloat16)
        )
    for g in range(raw_ref.shape[0] // rows):
        stacked = jnp.concatenate([p[g * height:(g + 1) * height, :] for p in parts], axis=0)
        grads_ref[g * rows:(g + 1) * rows, :] = mm(
            unpack[...], stacked, CONTRACT_FIRST
        ).astype(jnp.bfloat16)


def expert_back(raw, gate_pre, up_value, w_gate, w_up, w_down, steps=2):
    total, width = raw.shape
    features, hidden = w_gate.shape
    slots = gate_pre.shape[0]
    rows = slots // steps
    tall = lambda shape: pl.BlockSpec(shape, lambda i: (i, 0))
    whole = lambda shape: pl.BlockSpec(shape, lambda i: (0, 0))
    small = jax.ShapeDtypeStruct((slots, hidden), jnp.bfloat16)
    return pl.pallas_call(
        back_kernel,
        grid=(steps,),
        in_specs=[tall((total // steps, width)), tall((rows, hidden)), tall((rows, hidden)),
                  whole(w_gate.shape), whole(w_up.shape), whole(w_down.shape)],
        out_specs=[tall((total // steps, width)), tall((rows, features))]
        + [tall((rows, hidden))] * 3 + [tall((rows, 1))],
        out_shape=[jax.ShapeDtypeStruct(raw.shape, jnp.bfloat16),
                   jax.ShapeDtypeStruct((slots, features), jnp.bfloat16),
                   small, small, small, jax.ShapeDtypeStruct((slots, 1), jnp.float32)],
        scratch_shapes=[pltpu.VMEM((GROUP * CHUNK, GROUP * CHUNK), jnp.bfloat16)],
        compiler_params=pltpu.CompilerParams(vmem_limit_bytes=56 * MIB),
        cost_estimate=pl.CostEstimate(
            flops=6 * slots * features * hidden + 4 * total * GROUP * CHUNK * width,
            bytes_accessed=32 * MIB, transcendentals=slots * hidden),
        name="expert_back",
    )(raw, gate_pre, up_value, w_gate, w_up, w_down)


def combine_kernel(ids_ref, back_ref, hidden_ref, gain_ref, cot_ref, resid_ref, slot, total):
    tokens, features = hidden_ref.shape
    width = features // BLOCKS
    experts = slot.shape[1]
    rows = back_ref.shape[0]
    step = pl.program_id(0)

    @pl.when(step == 0)
    def _():
        expert = iota((tokens, experts), 1)
        named = jnp.where((expert == ids_ref[:, 0:1]) | (expert == ids_ref[:, 1:2]), 1.0, 0.0)
        earlier = jnp.where(iota((tokens, tokens), 1) < iota((tokens, tokens), 0), 1.0, 0.0)
        prior = mm(earlier.astype(jnp.bfloat16), named.astype(jnp.bfloat16))
        slot[...] = jnp.where(named > 0.5, prior, -1.0).astype(jnp.bfloat16)
        total[...] = jnp.zeros_like(total)

    spread_at = iota((experts, rows), 1) // (2 * CHUNK) + step * (rows // (2 * CHUNK))
    spread = jnp.where(iota((experts, rows), 0) == spread_at, 1.0, 0.0).astype(jnp.bfloat16)
    slots = mm(slot[...], spread)
    lane = iota((tokens, rows), 1)
    piece = lane // CAP
    taken = jnp.where(slots == (lane - piece * CAP).astype(jnp.float32), 1.0, 0.0)
    block_of = piece - piece // BLOCKS * BLOCKS
    picks = jnp.concatenate(
        [jnp.where(block_of == b, taken, 0.0).astype(jnp.bfloat16) for b in range(BLOCKS)], axis=0
    )
    total[...] += mm(picks, back_ref[...])

    @pl.when(step == pl.num_programs(0) - 1)
    def _():
        wide = hidden_ref[...].astype(jnp.float32)
        scale = lax.rsqrt(jnp.mean(wide * wide, axis=-1, keepdims=True) + EPSILON)
        inner = jnp.zeros((tokens, 1), jnp.float32)
        for b in range(BLOCKS):
            columns = slice(b * width, (b + 1) * width)
            rows = slice(b * tokens, (b + 1) * tokens)
            gained = total[rows, :] * gain_ref[:, columns]
            inner += jnp.sum(
                gained * hidden_ref[:, columns].astype(jnp.float32), axis=-1, keepdims=True
            )
        inner = (scale * scale * scale) * (inner / features)
        for b in range(BLOCKS):
            columns = slice(b * width, (b + 1) * width)
            rows = slice(b * tokens, (b + 1) * tokens)
            gained = total[rows, :] * gain_ref[:, columns]
            resid_ref[:, columns] = (
                cot_ref[:, columns].astype(jnp.float32) + scale * gained
                - hidden_ref[:, columns].astype(jnp.float32) * inner
            ).astype(jnp.bfloat16)


def combine(ids, back, hidden, gain, cots, experts, steps=4):
    tokens, features = hidden.shape
    total, width = back.shape
    whole = lambda shape: pl.BlockSpec(shape, lambda i: (0, 0))
    return pl.pallas_call(
        combine_kernel,
        grid=(steps,),
        in_specs=[whole(ids.shape), pl.BlockSpec((total // steps, width), lambda i: (i, 0)),
                  whole(hidden.shape), whole(gain.shape), whole(cots.shape)],
        out_specs=whole(hidden.shape),
        out_shape=jax.ShapeDtypeStruct(hidden.shape, jnp.bfloat16),
        scratch_shapes=[pltpu.VMEM((tokens, experts), jnp.bfloat16),
                        pltpu.VMEM((BLOCKS * tokens, width), jnp.float32)],
        compiler_params=pltpu.CompilerParams(vmem_limit_bytes=40 * MIB),
        cost_estimate=pl.CostEstimate(
            flops=2 * BLOCKS * tokens * total * width, bytes_accessed=12 * MIB, transcendentals=0),
        name="combine",
    )(ids, back, hidden, gain, cots)


STEPS = 4
SAME_L, SAME_R, SAME_T, SAME_B, FAR_C, FAR_L, FAR_R, FAR_T, FAR_B = range(9)
TO_Z, TO_R, TO_L, PASS_R, PASS_L, EXTRA_A, EXTRA_B, EXTRA_C, EXTRA_D = range(9)


def project_kernel(resid_ref, heads_ref, weight_ref, out_heads_ref, out_weight_ref,
                   pieces, total, partial, from_core, summed, from_y, to_z, from_z, blocks,
                   piece_send, piece_recv, core_send, core_recv, y_send, y_recv, z_send, z_recv,
                   block_send, block_y_recv, block_core_recv, block_z_recv):
    ctx, tp = lax.axis_index("ctx"), lax.axis_index("tp")
    y, z_hi, core = ctx // 4, (ctx // 2) % 2, ctx % 2
    z_lo, x = tp // 4, tp % 4
    right_x, left_x, opposite_x = (x + 1) % 4, (x + 3) % 4, (x + 2) % 4
    here, there = z_lo * 4, (1 - z_lo) * 4
    right, left, far = (ctx, here + right_x), (ctx, here + left_x), (ctx, there + x)
    sibling = (y * 4 + z_hi * 2 + (1 - core), tp)
    across = (y * 4 + (1 - z_hi) * 2 + core, tp)
    plane = lambda other: (other * 4 + z_hi * 2 + core, tp)
    tokens, features = resid_ref.shape
    chunk = features // STEPS
    rows = chunk // 4
    half = tokens // 2
    group = pieces.shape[1]

    barrier = pltpu.get_barrier_semaphore()
    peers = [right, left, far, sibling, across] + [plane((y + d) % 4) for d in (1, 2, 3)]
    for peer in peers:
        pl.semaphore_signal(barrier, inc=1, device_id=peer, device_id_type=pl.DeviceIdType.MESH)
    pl.semaphore_wait(barrier, len(peers))

    def remote(src, dst, send, recv, device):
        return pltpu.make_async_remote_copy(
            src_ref=src, dst_ref=dst, send_sem=send, recv_sem=recv,
            device_id=device, device_id_type=pl.DeviceIdType.MESH,
        )

    whole, top, bottom = pl.ds(0, tokens), pl.ds(0, half), pl.ds(half, half)
    sent = []

    def send(i, piece, part, kind, lands, device):
        ref = pieces.at[i, piece, part]
        copy = remote(ref, ref, piece_send.at[i, kind], piece_recv.at[i, lands], device)
        copy.start()
        sent.append(copy)

    def arrive(i, piece, part, lands):
        ref = pieces.at[i, piece, part]
        remote(ref, ref, piece_send.at[i, 0], piece_recv.at[i, lands], far).wait_recv()

    def owner(i):
        return (y + 1 + i) % 4

    def start_own(i):
        columns = pl.ds(pl.multiple_of(owner(i) * chunk, chunk), chunk)
        pieces[i, tp] = resid_ref[:, columns]
        send(i, tp, whole, TO_R, SAME_L, right)
        send(i, tp, whole, TO_L, SAME_R, left)
        send(i, tp, whole, TO_Z, FAR_C, far)

    def send_block(p, zh, semaphore, lands, device):
        ref = blocks.at[p, zh, core]
        copy = remote(ref, ref, semaphore, lands, device)
        copy.start()
        sent.append(copy)

    def block_arrives(p, zh, whose, lands):
        ref = blocks.at[p, zh, whose]
        remote(ref, ref, block_send.at[0], lands, sibling).wait_recv()

    def start_blocks():
        blocks[y, z_hi, core] = weight_ref[...]
        send_block(y, z_hi, block_send.at[0], block_z_recv, across)
        for i in range(STEPS - 1):
            send_block(y, z_hi, block_send.at[1 + i], block_y_recv.at[0, i], plane((y + 3 - i) % 4))
        send_block(y, z_hi, block_send.at[7], block_core_recv.at[0, STEPS - 1], sibling)

    def pass_blocks():
        block_arrives(y, 1 - z_hi, core, block_z_recv)
        for i in range(STEPS - 1):
            send_block(
                y, 1 - z_hi, block_send.at[4 + i], block_y_recv.at[1, i], plane((y + 3 - i) % 4)
            )
        send_block(y, 1 - z_hi, block_send.at[8], block_core_recv.at[1, STEPS - 1], sibling)

    def share_blocks(i):
        for side in range(2):
            zh = z_hi if side == 0 else 1 - z_hi
            block_arrives(owner(i), zh, core, block_y_recv.at[side, i])
            send_block(
                owner(i), zh, block_send.at[9 + 2 * i + side], block_core_recv.at[side, i], sibling
            )

    def blocks_ready(i):
        for side in range(2):
            zh = z_hi if side == 0 else 1 - z_hi
            block_arrives(owner(i), zh, 1 - core, block_core_recv.at[side, i])

    def first_hops(i):
        if i % 2 == 0:
            arrive(i, there + x, whole, FAR_C)
            send(i, there + x, whole, EXTRA_A, FAR_L, right)
            send(i, there + x, whole, EXTRA_B, FAR_R, left)
        arrive(i, here + left_x, whole, SAME_L)
        send(i, here + left_x, top, PASS_R, SAME_T, right)
        if i % 2 == 1:
            send(i, here + left_x, whole, EXTRA_A, FAR_L, far)
        arrive(i, here + right_x, whole, SAME_R)
        send(i, here + right_x, bottom, PASS_L, SAME_B, left)
        if i % 2 == 1:
            send(i, here + right_x, whole, EXTRA_B, FAR_R, far)

    def second_hops(i):
        if i % 2 == 0:
            arrive(i, there + left_x, whole, FAR_L)
            send(i, there + left_x, top, EXTRA_C, FAR_T, right)
            arrive(i, there + right_x, whole, FAR_R)
            send(i, there + right_x, bottom, EXTRA_D, FAR_B, left)
        else:
            arrive(i, here + opposite_x, top, SAME_T)
            send(i, here + opposite_x, top, EXTRA_C, FAR_T, far)
            arrive(i, here + opposite_x, bottom, SAME_B)
            send(i, here + opposite_x, bottom, EXTRA_D, FAR_B, far)

    def arrivals(i):
        if i % 2 == 0:
            arrive(i, here + opposite_x, top, SAME_T)
            arrive(i, here + opposite_x, bottom, SAME_B)
        else:
            arrive(i, there + x, whole, FAR_C)
            arrive(i, there + left_x, whole, FAR_L)
            arrive(i, there + right_x, whole, FAR_R)
        arrive(i, there + opposite_x, top, FAR_T)
        arrive(i, there + opposite_x, bottom, FAR_B)

    def weight_partial(i, whose):
        def one(zh, carry):
            first = pl.multiple_of((2 * zh + (core if whose == 0 else 1 - core)) * rows, rows)
            left_side = pieces[i, :, :, pl.ds(first, rows)].reshape(group * tokens, rows)
            partial[i, whose, zh] = mm(left_side, heads_ref[...], CONTRACT_FIRST).astype(jnp.bfloat16)
            return carry

        lax.fori_loop(0, 2, one, 0)

    def heads_partial(i):
        def one(r, carry):
            tall = pl.ds(pl.multiple_of(r * 2 * tokens, 2 * tokens), 2 * tokens)
            left_side = pieces[i, pl.ds(2 * r, 2)].reshape(2 * tokens, chunk)
            value = mm(left_side, blocks[owner(i)].reshape(chunk, blocks.shape[-1]))
            if i > 0:
                value = value + total[tall, :]
            if i < STEPS - 1:
                total[tall, :] = value
            else:
                out_heads_ref[tall, :] = value.astype(jnp.bfloat16)
            return carry

        lax.fori_loop(0, group // 2, one, 0)

    def multiply(i, between=()):
        weight_partial(i, 1)
        to_core = remote(partial.at[i, 1], from_core.at[i], core_send.at[i], core_recv.at[i], sibling)
        to_core.start()
        weight_partial(i, 0)
        for hops, other in between:
            hops(other)
        if i == STEPS - 1:
            return to_core
        blocks_ready(i)
        heads_partial(i)
        to_core.wait()
        summed[i] = (
            partial[i, 0].astype(jnp.float32) + from_core[i].astype(jnp.float32)
        ).astype(jnp.bfloat16)
        copy = remote(summed.at[i], from_y.at[i], y_send.at[i], y_recv.at[i], plane(owner(i)))
        copy.start()
        sent.append(copy)

    start_own(0)
    start_own(1)
    start_blocks()
    first_hops(0)
    first_hops(1)
    pass_blocks()
    start_own(2)
    second_hops(0)
    second_hops(1)
    start_own(3)
    first_hops(2)
    arrivals(0)
    multiply(0, ((first_hops, 3), (share_blocks, 0)))
    second_hops(2)
    arrivals(1)
    multiply(1, ((second_hops, 3), (share_blocks, 1)))
    share_blocks(2)
    arrivals(2)
    multiply(2)
    arrivals(3)
    to_core = multiply(3)

    last = STEPS - 1

    def reduced(zh):
        value = partial[last, 0, zh].astype(jnp.float32) + from_core[last, zh].astype(jnp.float32)
        for i in range(last):
            value = value + from_y[i, zh].astype(jnp.float32)
        return value

    to_core.wait()
    for i in range(last):
        remote(summed.at[i], from_y.at[i], y_send.at[i], y_recv.at[i], across).wait_recv()
    to_z[...] = reduced(1 - z_hi).astype(jnp.bfloat16)
    copy = remote(to_z, from_z, z_send, z_recv, across)
    copy.start()
    blocks_ready(last)
    heads_partial(last)
    own = reduced(z_hi)
    copy.wait()
    out_weight_ref[...] = (own + from_z[...].astype(jnp.float32)).astype(jnp.bfloat16)
    for copy in sent:
        copy.wait_send()


def project(resid, heads, weight, group):
    tokens, features = resid.shape
    columns = heads.shape[1]
    chunk = features // STEPS
    rows = chunk // 4
    bf16 = jnp.bfloat16
    dma = pltpu.SemaphoreType.DMA
    vmem = pl.BlockSpec(memory_space=pltpu.VMEM)
    return pl.pallas_call(
        project_kernel,
        in_specs=[vmem] * 3,
        out_specs=[vmem] * 2,
        out_shape=[jax.ShapeDtypeStruct(heads.shape, bf16), jax.ShapeDtypeStruct((rows, columns), bf16)],
        scratch_shapes=[
            pltpu.VMEM((STEPS, group, tokens, chunk), bf16),
            pltpu.VMEM(heads.shape, jnp.float32),
            pltpu.VMEM((STEPS, 2, 2, rows, columns), bf16),
            pltpu.VMEM((STEPS, 2, rows, columns), bf16),
            pltpu.VMEM((STEPS - 1, 2, rows, columns), bf16),
            pltpu.VMEM((STEPS - 1, 2, rows, columns), bf16),
            pltpu.VMEM((rows, columns), bf16),
            pltpu.VMEM((rows, columns), bf16),
            pltpu.VMEM((STEPS, 2, 2, rows, columns), bf16),
            dma((STEPS, 9)), dma((STEPS, 9)), dma((STEPS,)), dma((STEPS,)),
            dma((STEPS - 1,)), dma((STEPS - 1,)), dma, dma,
            dma((15,)), dma((2, STEPS - 1)), dma((2, STEPS)), dma,
        ],
        compiler_params=pltpu.CompilerParams(
            collective_id=0, has_side_effects=True, vmem_limit_bytes=48 * MIB),
        cost_estimate=pl.CostEstimate(
            flops=4 * group * tokens * features * columns, bytes_accessed=8 * MIB, transcendentals=0),
        name="project",
    )(resid, heads, weight)


def per_device(
    ctx_heads,
    out_weight,
    hidden_in,
    norm_gain,
    expert_ids,
    route_weights,
    w_gate,
    w_up,
    w_down,
    grad_out,
):
    tokens, features = hidden_in.shape
    devices = lax.axis_size(("ctx", "tp"))
    experts = devices // 2
    axes = ("ctx", "tp")
    exchange = functools.partial(
        lax.all_to_all, axis_name=axes, split_axis=0, concat_axis=0, tiled=True
    )
    width = features // BLOCKS
    gain = norm_gain.reshape(1, features)
    rounded_weights = route_weights.astype(jnp.bfloat16).astype(jnp.float32)
    ids_t, weights_t = expert_ids.T, rounded_weights.T
    send_rows = dispatch(True, ids_t, weights_t, hidden_in, gain, experts)
    send_cots = dispatch(False, ids_t, weights_t, grad_out, gain, experts)
    raw_rows = exchange(send_rows.reshape(devices, CHUNK, width)).reshape(-1, width)
    raw_cots = exchange(send_cots.reshape(devices, CHUNK, width)).reshape(-1, width)
    slot_rows = unpack_chunks(raw_rows)
    gate_pre = mm(slot_rows, w_gate[0])
    up_value = mm(slot_rows, w_up[0])
    grads, slot_cots, activated, gate_grad, up_grad, dots = expert_back(
        raw_cots, gate_pre, up_value, w_gate[0], w_up[0], w_down[0]
    )
    back = exchange(grads.reshape(devices, CHUNK, width)).reshape(-1, width)
    back, dots = lax.optimization_barrier((back, dots))
    back_dots = exchange(dots.reshape(devices, CAP).astype(jnp.bfloat16)).astype(jnp.float32)
    down_wgrad = mm(activated, slot_cots, CONTRACT_FIRST).astype(jnp.bfloat16)
    gate_wgrad = mm(slot_rows, gate_grad, CONTRACT_FIRST).astype(jnp.bfloat16)
    up_wgrad = mm(slot_rows, up_grad, CONTRACT_FIRST).astype(jnp.bfloat16)
    resid_grad = combine(expert_ids, back, hidden_in, gain, grad_out, experts)

    flat_ids = expert_ids.reshape(-1)
    onehot = (flat_ids[:, None] == jnp.arange(experts, dtype=jnp.int32)[None, :]).astype(jnp.int32)
    slot_rank = jnp.sum((jnp.cumsum(onehot, axis=0) - onehot) * onehot, axis=1)
    summed_dots = back_dots.reshape(experts, 2, CAP).sum(axis=1)
    picked = jnp.dot(onehot.astype(jnp.float32), summed_dots, precision=lax.Precision.HIGHEST)
    at_rank = slot_rank[:, None] == jnp.arange(CAP, dtype=jnp.int32)[None, :]
    route_grads = (
        jnp.sum(jnp.where(at_rank, picked, 0.0), axis=1).reshape(tokens, -1) / rounded_weights
    )

    heads_grad, weight_grad = project(resid_grad, ctx_heads, out_weight, lax.axis_size("tp"))
    return (
        heads_grad,
        weight_grad,
        resid_grad,
        route_grads,
        gate_wgrad[None],
        up_wgrad[None],
        down_wgrad[None],
    )


def solution(mesh):
    split = P(("ctx", "tp"), None)
    stack = P(("ctx", "tp"), None, None)
    in_specs = (
        P("ctx", "tp"),
        P("ctx", "tp"),
        split,
        P(),
        split,
        split,
        stack,
        stack,
        stack,
        split,
    )
    out_specs = (P("ctx", "tp"), P("ctx", "tp"), split, split, stack, stack, stack)
    return jax.shard_map(
        per_device, mesh=mesh, in_specs=in_specs, out_specs=out_specs, check_vma=False
    )
```

```python
import functools

import jax
import jax.numpy as jnp
from jax import lax
from jax.experimental import pallas as pl
from jax.experimental.pallas import tpu as pltpu
from jax.sharding import PartitionSpec as P

EPSILON = 1e-06
CAP = 6
BLOCKS = 4
CHUNK = CAP * BLOCKS
CONTRACT_FIRST = (((0,), (0,)), ((), ()))
CONTRACT_LAST = (((1,), (1,)), ((), ()))
MIB = 1 << 20


def iota(shape, dim):
    return lax.broadcasted_iota(jnp.int32, shape, dim)


def mm(a, b, dims=(((1,), (0,)), ((), ()))):
    return lax.dot_general(a, b, dims, preferred_element_type=jnp.float32)


def dispatch_kernel(normalize, ids_ref, weight_ref, value_ref, gain_ref, out_ref, flat, unpack):
    tokens, features = value_ref.shape
    width = features // BLOCKS
    experts = flat.shape[0] // CAP
    group = out_ref.shape[0]
    step = pl.program_id(0)

    @pl.when(step == 0)
    def _():
        expert = iota((experts, tokens), 0)
        first = expert == ids_ref[0:1, :]
        second = expert == ids_ref[1:2, :]
        named = jnp.where(first | second, 1.0, 0.0)
        earlier = jnp.where(iota((tokens, tokens), 0) < iota((tokens, tokens), 1), 1.0, 0.0)
        prior = mm(named.astype(jnp.bfloat16), earlier.astype(jnp.bfloat16))
        unpack[...] = unpack_matrix(group)
        slots = jnp.where(named > 0.5, prior, -1.0).astype(jnp.bfloat16)
        weights = jnp.where(
            first, weight_ref[0:1, :], jnp.where(second, weight_ref[1:2, :], 0.0)
        ).astype(jnp.bfloat16)
        row = iota((experts * CAP, experts), 0)
        expert_of = row // CAP
        spread = jnp.where(expert_of == iota((experts * CAP, experts), 1), 1.0, 0.0)
        spread = spread.astype(jnp.bfloat16)
        place = iota((experts * CAP, tokens), 0)
        place = (place - place // CAP * CAP).astype(jnp.float32)
        taken = mm(spread, slots) == place
        if normalize:
            picks = jnp.where(taken, 1.0, 0.0).astype(jnp.bfloat16)
            wide = value_ref[...].astype(jnp.float32)
            scale = lax.rsqrt(jnp.mean(wide * wide, axis=-1, keepdims=True) + EPSILON)
        else:
            picks = jnp.where(taken, mm(spread, weights), 0.0).astype(jnp.bfloat16)
        for block in range(BLOCKS):
            columns = slice(block * width, (block + 1) * width)
            values = value_ref[:, columns]
            if normalize:
                values = (values.astype(jnp.float32) * scale * gain_ref[:, columns]).astype(jnp.bfloat16)
            flat[:, columns] = mm(picks, values).astype(jnp.bfloat16)

    height = group * CAP
    here = pl.ds(pl.multiple_of(step * height, height), height)
    stacked = jnp.concatenate(
        [flat[here, b * width:(b + 1) * width] for b in range(BLOCKS)], axis=0
    )
    chunks = mm(unpack[...], stacked, CONTRACT_FIRST).reshape(group, CHUNK, width)
    chunks = chunks.astype(jnp.bfloat16)
    for half in range(2):
        out_ref[:, half] = chunks


def dispatch(normalize, ids_t, weights_t, values, gain, experts):
    tokens, features = values.shape
    width = features // BLOCKS
    group = 8
    whole = lambda shape: pl.BlockSpec(shape, lambda i: (0, 0))
    return pl.pallas_call(
        functools.partial(dispatch_kernel, normalize),
        grid=(experts // group,),
        in_specs=[whole(ids_t.shape), whole(weights_t.shape), whole(values.shape), whole(gain.shape)],
        out_specs=pl.BlockSpec((group, 2, CHUNK, width), lambda i: (i, 0, 0, 0)),
        out_shape=jax.ShapeDtypeStruct((experts, 2, CHUNK, width), jnp.bfloat16),
        scratch_shapes=[
            pltpu.VMEM((experts * CAP, features), jnp.bfloat16),
            pltpu.VMEM((group * CHUNK, group * CHUNK), jnp.bfloat16),
        ],
        compiler_params=pltpu.CompilerParams(vmem_limit_bytes=60 * MIB),
        cost_estimate=pl.CostEstimate(
            flops=2 * experts * CHUNK * tokens * features, bytes_accessed=8 * MIB,
            transcendentals=0),
        name="dispatch_rows" if normalize else "dispatch_cots",
    )(ids_t, weights_t, values, gain)


def unpack_matrix(sources):
    rows = sources * CHUNK
    out, inp = iota((rows, rows), 0), iota((rows, rows), 1)
    block = out // (sources * CAP)
    rest = out - block * (sources * CAP)
    source = rest // CAP
    want = source * CHUNK + block * CAP + (rest - source * CAP)
    return jnp.where(inp == want, 1.0, 0.0).astype(jnp.bfloat16)


GROUP = 8


def unpack_rows(unpack, raw_ref, out_ref):
    rows = GROUP * CHUNK
    height = GROUP * CAP
    width = raw_ref.shape[1]
    for g in range(raw_ref.shape[0] // rows):
        flat = mm(unpack, raw_ref[g * rows:(g + 1) * rows, :]).astype(jnp.bfloat16)
        for b in range(BLOCKS):
            out_ref[g * height:(g + 1) * height, b * width:(b + 1) * width] = (
                flat[b * height:(b + 1) * height, :]
            )


def unpack_kernel(raw_ref, out_ref, unpack):
    @pl.when(pl.program_id(0) == 0)
    def _():
        unpack[...] = unpack_matrix(GROUP)

    unpack_rows(unpack[...], raw_ref, out_ref)


def unpack_chunks(raw, steps=8):
    total, width = raw.shape
    rows = total // steps
    return pl.pallas_call(
        unpack_kernel,
        grid=(steps,),
        in_specs=[pl.BlockSpec((rows, width), lambda i: (i, 0))],
        out_specs=pl.BlockSpec((rows // BLOCKS, width * BLOCKS), lambda i: (i, 0)),
        out_shape=jax.ShapeDtypeStruct((total // BLOCKS, width * BLOCKS), jnp.bfloat16),
        scratch_shapes=[pltpu.VMEM((GROUP * CHUNK, GROUP * CHUNK), jnp.bfloat16)],
        compiler_params=pltpu.CompilerParams(vmem_limit_bytes=40 * MIB),
        cost_estimate=pl.CostEstimate(
            flops=2 * total * GROUP * CHUNK * width, bytes_accessed=4 * total * width,
            transcendentals=0),
        name="unpack",
    )(raw)


def back_kernel(raw_ref, gate_ref, up_ref, w_gate_ref, w_up_ref, w_down_ref,
                grads_ref, cots_ref, act_ref, gate_grad_ref, up_grad_ref, dots_ref, unpack):
    @pl.when(pl.program_id(0) == 0)
    def _():
        unpack[...] = unpack_matrix(GROUP)

    unpack_rows(unpack[...], raw_ref, cots_ref)
    back = mm(cots_ref[...], w_down_ref[...], CONTRACT_LAST)
    gate_pre, up_value = gate_ref[...], up_ref[...]
    sigmoid = jax.nn.sigmoid(gate_pre)
    silu = gate_pre * sigmoid
    activated = (silu * up_value).astype(jnp.bfloat16)
    act_ref[...] = activated
    dots_ref[...] = jnp.sum(activated.astype(jnp.float32) * back, axis=-1, keepdims=True)
    gate_grad = (back * up_value * sigmoid * (1.0 + gate_pre * (1.0 - sigmoid))).astype(jnp.bfloat16)
    up_grad = (back * silu).astype(jnp.bfloat16)
    gate_grad_ref[...] = gate_grad
    up_grad_ref[...] = up_grad
    height = GROUP * CAP
    rows = GROUP * CHUNK
    width = raw_ref.shape[1]
    parts = []
    for b in range(BLOCKS):
        columns = slice(b * width, (b + 1) * width)
        parts.append(
            (mm(gate_grad, w_gate_ref[columns, :], CONTRACT_LAST)
             + mm(up_grad, w_up_ref[columns, :], CONTRACT_LAST)).astype(jnp.bfloat16)
        )
    for g in range(raw_ref.shape[0] // rows):
        stacked = jnp.concatenate([p[g * height:(g + 1) * height, :] for p in parts], axis=0)
        grads_ref[g * rows:(g + 1) * rows, :] = mm(
            unpack[...], stacked, CONTRACT_FIRST
        ).astype(jnp.bfloat16)


def expert_back(raw, gate_pre, up_value, w_gate, w_up, w_down, steps=2):
    total, width = raw.shape
    features, hidden = w_gate.shape
    slots = gate_pre.shape[0]
    rows = slots // steps
    tall = lambda shape: pl.BlockSpec(shape, lambda i: (i, 0))
    whole = lambda shape: pl.BlockSpec(shape, lambda i: (0, 0))
    small = jax.ShapeDtypeStruct((slots, hidden), jnp.bfloat16)
    return pl.pallas_call(
        back_kernel,
        grid=(steps,),
        in_specs=[tall((total // steps, width)), tall((rows, hidden)), tall((rows, hidden)),
                  whole(w_gate.shape), whole(w_up.shape), whole(w_down.shape)],
        out_specs=[tall((total // steps, width)), tall((rows, features))]
        + [tall((rows, hidden))] * 3 + [tall((rows, 1))],
        out_shape=[jax.ShapeDtypeStruct(raw.shape, jnp.bfloat16),
                   jax.ShapeDtypeStruct((slots, features), jnp.bfloat16),
                   small, small, small, jax.ShapeDtypeStruct((slots, 1), jnp.float32)],
        scratch_shapes=[pltpu.VMEM((GROUP * CHUNK, GROUP * CHUNK), jnp.bfloat16)],
        compiler_params=pltpu.CompilerParams(vmem_limit_bytes=56 * MIB),
        cost_estimate=pl.CostEstimate(
            flops=6 * slots * features * hidden + 4 * total * GROUP * CHUNK * width,
            bytes_accessed=32 * MIB, transcendentals=slots * hidden),
        name="expert_back",
    )(raw, gate_pre, up_value, w_gate, w_up, w_down)


def combine_kernel(ids_ref, back_ref, hidden_ref, gain_ref, cot_ref, resid_ref, slot, total):
    tokens, features = hidden_ref.shape
    width = features // BLOCKS
    experts = slot.shape[1]
    rows = back_ref.shape[0]
    step = pl.program_id(0)

    @pl.when(step == 0)
    def _():
        expert = iota((tokens, experts), 1)
        named = jnp.where((expert == ids_ref[:, 0:1]) | (expert == ids_ref[:, 1:2]), 1.0, 0.0)
        earlier = jnp.where(iota((tokens, tokens), 1) < iota((tokens, tokens), 0), 1.0, 0.0)
        prior = mm(earlier.astype(jnp.bfloat16), named.astype(jnp.bfloat16))
        slot[...] = jnp.where(named > 0.5, prior, -1.0).astype(jnp.bfloat16)
        total[...] = jnp.zeros_like(total)

    spread_at = iota((experts, rows), 1) // (2 * CHUNK) + step * (rows // (2 * CHUNK))
    spread = jnp.where(iota((experts, rows), 0) == spread_at, 1.0, 0.0).astype(jnp.bfloat16)
    slots = mm(slot[...], spread)
    lane = iota((tokens, rows), 1)
    piece = lane // CAP
    taken = jnp.where(slots == (lane - piece * CAP).astype(jnp.float32), 1.0, 0.0)
    block_of = piece - piece // BLOCKS * BLOCKS
    picks = jnp.concatenate(
        [jnp.where(block_of == b, taken, 0.0).astype(jnp.bfloat16) for b in range(BLOCKS)], axis=0
    )
    total[...] += mm(picks, back_ref[...])

    @pl.when(step == pl.num_programs(0) - 1)
    def _():
        wide = hidden_ref[...].astype(jnp.float32)
        scale = lax.rsqrt(jnp.mean(wide * wide, axis=-1, keepdims=True) + EPSILON)
        inner = jnp.zeros((tokens, 1), jnp.float32)
        for b in range(BLOCKS):
            columns = slice(b * width, (b + 1) * width)
            rows = slice(b * tokens, (b + 1) * tokens)
            gained = total[rows, :] * gain_ref[:, columns]
            inner += jnp.sum(
                gained * hidden_ref[:, columns].astype(jnp.float32), axis=-1, keepdims=True
            )
        inner = (scale * scale * scale) * (inner / features)
        for b in range(BLOCKS):
            columns = slice(b * width, (b + 1) * width)
            rows = slice(b * tokens, (b + 1) * tokens)
            gained = total[rows, :] * gain_ref[:, columns]
            resid_ref[:, columns] = (
                cot_ref[:, columns].astype(jnp.float32) + scale * gained
                - hidden_ref[:, columns].astype(jnp.float32) * inner
            ).astype(jnp.bfloat16)


def combine(ids, back, hidden, gain, cots, experts, steps=4):
    tokens, features = hidden.shape
    total, width = back.shape
    whole = lambda shape: pl.BlockSpec(shape, lambda i: (0, 0))
    return pl.pallas_call(
        combine_kernel,
        grid=(steps,),
        in_specs=[whole(ids.shape), pl.BlockSpec((total // steps, width), lambda i: (i, 0)),
                  whole(hidden.shape), whole(gain.shape), whole(cots.shape)],
        out_specs=whole(hidden.shape),
        out_shape=jax.ShapeDtypeStruct(hidden.shape, jnp.bfloat16),
        scratch_shapes=[pltpu.VMEM((tokens, experts), jnp.bfloat16),
                        pltpu.VMEM((BLOCKS * tokens, width), jnp.float32)],
        compiler_params=pltpu.CompilerParams(vmem_limit_bytes=61 * MIB),
        cost_estimate=pl.CostEstimate(
            flops=2 * BLOCKS * tokens * total * width, bytes_accessed=12 * MIB, transcendentals=0),
        name="combine",
    )(ids, back, hidden, gain, cots)


STEPS = 4
SAME_L, SAME_R, SAME_T, SAME_B, FAR_C, FAR_L, FAR_R, FAR_T, FAR_B = range(9)
TO_Z, TO_R, TO_L, PASS_R, PASS_L, EXTRA_A, EXTRA_B, EXTRA_C, EXTRA_D = range(9)


EXTRA = 16


def project_kernel(resid_ref, heads_ref, weight_ref, dots_ref,
                   out_heads_ref, out_weight_ref, out_dots_ref,
                   heads, heads_t, dots_all, dots_rows, pieces, total, partial, from_core, summed, from_y, to_z, from_z, blocks,
                   piece_send, piece_recv, core_send, core_recv, y_send, y_recv, z_send, z_recv,
                   block_send, block_y_recv, block_core_recv, block_z_recv,
                   local, dots_send, dots_recv):
    ctx, tp = lax.axis_index("ctx"), lax.axis_index("tp")
    y, z_hi, core = ctx // 4, (ctx // 2) % 2, ctx % 2
    z_lo, x = tp // 4, tp % 4
    right_x, left_x, opposite_x = (x + 1) % 4, (x + 3) % 4, (x + 2) % 4
    here, there = z_lo * 4, (1 - z_lo) * 4
    right, left, far = (ctx, here + right_x), (ctx, here + left_x), (ctx, there + x)
    sibling = (y * 4 + z_hi * 2 + (1 - core), tp)
    across = (y * 4 + (1 - z_hi) * 2 + core, tp)
    plane = lambda other: (other * 4 + z_hi * 2 + core, tp)
    tokens, features = resid_ref.shape
    chunk = features // STEPS
    rows = chunk // 4
    half = tokens // 2
    group = pieces.shape[1]

    columns = heads.shape[1]

    def owner(i):
        return (y + 1 + i) % 4

    def fetch(i):
        lanes = pl.ds(pl.multiple_of(owner(i) * chunk, chunk), chunk)
        return pltpu.make_async_copy(resid_ref.at[:, lanes], pieces.at[i, tp], local.at[i])

    fetch_heads = pltpu.make_async_copy(heads_ref, heads, local.at[STEPS])
    for i in range(STEPS):
        fetch(i).start()
    fetch_heads.start()

    barrier = pltpu.get_barrier_semaphore()
    peers = [(ctx, (tp + d) % group) for d in range(1, group)]
    peers += [sibling, across] + [plane((y + d) % 4) for d in (1, 2, 3)]
    for peer in peers:
        pl.semaphore_signal(barrier, inc=1, device_id=peer, device_id_type=pl.DeviceIdType.MESH)
    pl.semaphore_wait(barrier, len(peers))

    def remote(src, dst, send, recv, device):
        return pltpu.make_async_remote_copy(
            src_ref=src, dst_ref=dst, send_sem=send, recv_sem=recv,
            device_id=device, device_id_type=pl.DeviceIdType.MESH,
        )

    whole, top, bottom = pl.ds(0, tokens), pl.ds(0, half), pl.ds(half, half)
    sent = []

    def send(i, piece, part, kind, lands, device):
        ref = pieces.at[i, piece, part]
        copy = remote(ref, ref, piece_send.at[i, kind], piece_recv.at[i, lands], device)
        copy.start()
        sent.append(copy)

    def arrive(i, piece, part, lands):
        ref = pieces.at[i, piece, part]
        remote(ref, ref, piece_send.at[i, 0], piece_recv.at[i, lands], far).wait_recv()

    def start_own(i):
        fetch(i).wait()
        send(i, tp, whole, TO_R, SAME_L, right)
        send(i, tp, whole, TO_L, SAME_R, left)
        send(i, tp, whole, TO_Z, FAR_C, far)

    def send_block(p, zh, semaphore, lands, device):
        ref = blocks.at[p, zh, core]
        copy = remote(ref, ref, semaphore, lands, device)
        copy.start()
        sent.append(copy)

    def block_arrives(p, zh, whose, lands):
        ref = blocks.at[p, zh, whose]
        remote(ref, ref, block_send.at[0], lands, sibling).wait_recv()

    def start_blocks():
        blocks[y, z_hi, core] = weight_ref[...]
        send_block(y, z_hi, block_send.at[0], block_z_recv, across)
        for i in range(STEPS - 1):
            send_block(y, z_hi, block_send.at[1 + i], block_y_recv.at[0, i], plane((y + 3 - i) % 4))
        send_block(y, z_hi, block_send.at[7], block_core_recv.at[0, STEPS - 1], sibling)

    def pass_blocks():
        block_arrives(y, 1 - z_hi, core, block_z_recv)
        for i in range(STEPS - 1):
            send_block(
                y, 1 - z_hi, block_send.at[4 + i], block_y_recv.at[1, i], plane((y + 3 - i) % 4)
            )
        send_block(y, 1 - z_hi, block_send.at[8], block_core_recv.at[1, STEPS - 1], sibling)

    def share_blocks(i):
        for side in range(2):
            zh = z_hi if side == 0 else 1 - z_hi
            block_arrives(owner(i), zh, core, block_y_recv.at[side, i])
            send_block(
                owner(i), zh, block_send.at[9 + 2 * i + side], block_core_recv.at[side, i], sibling
            )

    def blocks_ready(i):
        for side in range(2):
            zh = z_hi if side == 0 else 1 - z_hi
            block_arrives(owner(i), zh, 1 - core, block_core_recv.at[side, i])

    def first_hops(i):
        if i % 2 == 0:
            arrive(i, there + x, whole, FAR_C)
            send(i, there + x, whole, EXTRA_A, FAR_L, right)
            send(i, there + x, whole, EXTRA_B, FAR_R, left)
        arrive(i, here + left_x, whole, SAME_L)
        send(i, here + left_x, top, PASS_R, SAME_T, right)
        if i % 2 == 1:
            send(i, here + left_x, whole, EXTRA_A, FAR_L, far)
        arrive(i, here + right_x, whole, SAME_R)
        send(i, here + right_x, bottom, PASS_L, SAME_B, left)
        if i % 2 == 1:
            send(i, here + right_x, whole, EXTRA_B, FAR_R, far)

    def second_hops(i):
        if i % 2 == 0:
            arrive(i, there + left_x, whole, FAR_L)
            send(i, there + left_x, top, EXTRA_C, FAR_T, right)
            arrive(i, there + right_x, whole, FAR_R)
            send(i, there + right_x, bottom, EXTRA_D, FAR_B, left)
        else:
            arrive(i, here + opposite_x, top, SAME_T)
            send(i, here + opposite_x, top, EXTRA_C, FAR_T, far)
            arrive(i, here + opposite_x, bottom, SAME_B)
            send(i, here + opposite_x, bottom, EXTRA_D, FAR_B, far)

    def arrivals(i):
        if i % 2 == 0:
            arrive(i, here + opposite_x, top, SAME_T)
            arrive(i, here + opposite_x, bottom, SAME_B)
        else:
            arrive(i, there + x, whole, FAR_C)
            arrive(i, there + left_x, whole, FAR_L)
            arrive(i, there + right_x, whole, FAR_R)
        arrive(i, there + opposite_x, top, FAR_T)
        arrive(i, there + opposite_x, bottom, FAR_B)

    def start_dots():
        dots_all[tp] = dots_ref[...]
        for d in range(1, group):
            ref = dots_all.at[tp]
            copy = remote(
                ref, ref, dots_send.at[d - 1], dots_recv.at[d - 1], (ctx, (tp + d) % group)
            )
            copy.start()
            sent.append(copy)

    def gather_dots():
        for d in range(1, group):
            ref = dots_all.at[(tp + group - d) % group]
            remote(ref, ref, dots_send.at[0], dots_recv.at[d - 1], far).wait_recv()
        sources = dots_all.shape[2]
        count = group * EXTRA
        table = dots_all[...].reshape(count, sources)
        mine = iota((16, sources), 1) == iota((16, sources), 0) * group + tp
        mine = jnp.where(mine, 1.0, 0.0).astype(jnp.bfloat16)
        held = mm(mine, table, CONTRACT_LAST).astype(jnp.bfloat16)
        row, lane = iota((count, 2 * rows), 0), iota((count, 2 * rows), 1)
        device = row // EXTRA
        slot = row - device * EXTRA
        place = jnp.where(slot < CAP, (ctx * 4 + device // 2) * CAP + slot, -1)
        spread = jnp.where(lane == place, 1.0, 0.0).astype(jnp.bfloat16)
        dots_rows[...] = mm(held, spread)

    def turn_heads():
        fetch_heads.wait()
        for r in range(4):
            part = heads.shape[0] // 4
            heads_t[:, r * part:(r + 1) * part] = heads[r * part:(r + 1) * part, :].T

    def weight_partial(i, whose):
        def one(zh, carry):
            local_owner = 2 * zh + (core if whose == 0 else 1 - core)
            first = pl.multiple_of(local_owner * rows, rows)
            right_side = pieces[i, :, :, pl.ds(first, rows)].reshape(group * tokens, rows)
            value = mm(heads_t[...], right_side)
            partial[i, whose, zh, 0:columns] = value.astype(jnp.bfloat16)
            at = iota((16, 2 * rows), 0) == owner(i) * 4 + local_owner
            line = jnp.sum(jnp.where(at, dots_rows[...], 0.0), axis=0, keepdims=True)
            row = iota((EXTRA, rows), 0)
            tail = jnp.where(row == 0, line[:, :rows], jnp.where(row == 1, line[:, rows:], 0.0))
            partial[i, whose, zh, columns:columns + EXTRA] = tail.astype(jnp.bfloat16)
            return carry

        lax.fori_loop(0, 2, one, 0)

    def heads_partial(i):
        def one(r, carry):
            tall = pl.ds(pl.multiple_of(r * 2 * tokens, 2 * tokens), 2 * tokens)
            left_side = pieces[i, pl.ds(2 * r, 2)].reshape(2 * tokens, chunk)
            value = mm(left_side, blocks[owner(i)].reshape(chunk, blocks.shape[-1]))
            if i > 0:
                value = value + total[tall, :]
            if i < STEPS - 1:
                total[tall, :] = value
            else:
                out_heads_ref[tall, :] = value.astype(jnp.bfloat16)
            return carry

        lax.fori_loop(0, group // 2, one, 0)

    def multiply(i, between=()):
        weight_partial(i, 1)
        to_core = remote(partial.at[i, 1], from_core.at[i], core_send.at[i], core_recv.at[i], sibling)
        to_core.start()
        weight_partial(i, 0)
        for hops, other in between:
            hops(other)
        if i == STEPS - 1:
            return to_core
        blocks_ready(i)
        heads_partial(i)
        to_core.wait()
        summed[i] = (
            partial[i, 0].astype(jnp.float32) + from_core[i].astype(jnp.float32)
        ).astype(jnp.bfloat16)
        copy = remote(summed.at[i], from_y.at[i], y_send.at[i], y_recv.at[i], plane(owner(i)))
        copy.start()
        sent.append(copy)

    start_own(0)
    start_own(1)
    start_dots()
    start_blocks()
    turn_heads()
    first_hops(0)
    first_hops(1)
    pass_blocks()
    start_own(2)
    second_hops(0)
    second_hops(1)
    start_own(3)
    gather_dots()
    first_hops(2)
    arrivals(0)
    multiply(0, ((first_hops, 3), (share_blocks, 0)))
    second_hops(2)
    arrivals(1)
    multiply(1, ((second_hops, 3), (share_blocks, 1)))
    share_blocks(2)
    arrivals(2)
    multiply(2)
    arrivals(3)
    to_core = multiply(3)

    last = STEPS - 1

    def reduced(zh):
        value = partial[last, 0, zh].astype(jnp.float32) + from_core[last, zh].astype(jnp.float32)
        for i in range(last):
            value = value + from_y[i, zh].astype(jnp.float32)
        return value

    to_core.wait()
    for i in range(last):
        remote(summed.at[i], from_y.at[i], y_send.at[i], y_recv.at[i], across).wait_recv()
    to_z[...] = reduced(1 - z_hi).astype(jnp.bfloat16)
    copy = remote(to_z, from_z, z_send, z_recv, across)
    copy.start()
    blocks_ready(last)
    heads_partial(last)
    own = reduced(z_hi)
    copy.wait()
    own = own + from_z[...].astype(jnp.float32)
    out_weight_ref[...] = own[:columns].T.astype(jnp.bfloat16)
    out_dots_ref[...] = own[columns:]
    for copy in sent:
        copy.wait_send()


def project(resid, heads, weight, dots, group):
    tokens, features = resid.shape
    columns = heads.shape[1]
    chunk = features // STEPS
    rows = chunk // 4
    tall = columns + EXTRA
    bf16 = jnp.bfloat16
    dma = pltpu.SemaphoreType.DMA
    vmem = pl.BlockSpec(memory_space=pltpu.VMEM)
    anywhere = pl.BlockSpec(memory_space=pltpu.HBM)
    return pl.pallas_call(
        project_kernel,
        in_specs=[anywhere, anywhere, vmem, vmem],
        out_specs=[vmem] * 3,
        out_shape=[jax.ShapeDtypeStruct(heads.shape, bf16), jax.ShapeDtypeStruct((rows, columns), bf16),
                   jax.ShapeDtypeStruct((EXTRA, rows), jnp.float32)],
        scratch_shapes=[
            pltpu.VMEM(heads.shape, bf16),
            pltpu.VMEM(heads.shape[::-1], bf16),
            pltpu.VMEM((group,) + dots.shape, bf16),
            pltpu.VMEM((16, 2 * rows), jnp.float32),
            pltpu.VMEM((STEPS, group, tokens, chunk), bf16),
            pltpu.VMEM(heads.shape, jnp.float32),
            pltpu.VMEM((STEPS, 2, 2, tall, rows), bf16),
            pltpu.VMEM((STEPS, 2, tall, rows), bf16),
            pltpu.VMEM((STEPS - 1, 2, tall, rows), bf16),
            pltpu.VMEM((STEPS - 1, 2, tall, rows), bf16),
            pltpu.VMEM((tall, rows), bf16),
            pltpu.VMEM((tall, rows), bf16),
            pltpu.VMEM((STEPS, 2, 2, rows, columns), bf16),
            dma((STEPS, 9)), dma((STEPS, 9)), dma((STEPS,)), dma((STEPS,)),
            dma((STEPS - 1,)), dma((STEPS - 1,)), dma, dma,
            dma((15,)), dma((2, STEPS - 1)), dma((2, STEPS)), dma,
            dma((STEPS + 1,)), dma((group - 1,)), dma((group - 1,)),
        ],
        compiler_params=pltpu.CompilerParams(
            collective_id=0, has_side_effects=True, vmem_limit_bytes=61 * MIB + MIB // 2),
        cost_estimate=pl.CostEstimate(
            flops=4 * group * tokens * features * columns, bytes_accessed=8 * MIB, transcendentals=0),
        name="project",
    )(resid, heads, weight, dots)


def per_device(
    ctx_heads,
    out_weight,
    hidden_in,
    norm_gain,
    expert_ids,
    route_weights,
    w_gate,
    w_up,
    w_down,
    grad_out,
):
    tokens, features = hidden_in.shape
    devices = lax.axis_size(("ctx", "tp"))
    experts = devices // 2
    axes = ("ctx", "tp")
    exchange = functools.partial(
        lax.all_to_all, axis_name=axes, split_axis=0, concat_axis=0, tiled=True
    )
    width = features // BLOCKS
    gain = norm_gain.reshape(1, features)
    rounded_weights = route_weights.astype(jnp.bfloat16).astype(jnp.float32)
    ids_t, weights_t = expert_ids.T, rounded_weights.T
    send_rows = dispatch(True, ids_t, weights_t, hidden_in, gain, experts)
    send_cots = dispatch(False, ids_t, weights_t, grad_out, gain, experts)
    raw_rows = exchange(send_rows.reshape(devices, CHUNK, width)).reshape(-1, width)
    raw_cots = exchange(send_cots.reshape(devices, CHUNK, width)).reshape(-1, width)
    slot_rows = unpack_chunks(raw_rows)
    gate_pre = mm(slot_rows, w_gate[0])
    up_value = mm(slot_rows, w_up[0])
    grads, slot_cots, activated, gate_grad, up_grad, dots = expert_back(
        raw_cots, gate_pre, up_value, w_gate[0], w_up[0], w_down[0]
    )
    back = exchange(grads.reshape(devices, CHUNK, width)).reshape(-1, width)
    sent_dots = jnp.pad(dots.reshape(devices, CAP).T, ((0, EXTRA - CAP), (0, 0)))
    down_wgrad = mm(activated, slot_cots, CONTRACT_FIRST).astype(jnp.bfloat16)
    gate_wgrad = mm(slot_rows, gate_grad, CONTRACT_FIRST).astype(jnp.bfloat16)
    up_wgrad = mm(slot_rows, up_grad, CONTRACT_FIRST).astype(jnp.bfloat16)
    resid_grad = combine(expert_ids, back, hidden_in, gain, grad_out, experts)

    heads_grad, weight_grad, summed_dots = project(
        resid_grad, ctx_heads, out_weight, sent_dots.astype(jnp.bfloat16), lax.axis_size("tp")
    )
    summed_dots = summed_dots[:2].reshape(-1)[:experts * CAP].reshape(experts, CAP)
    flat_ids = expert_ids.reshape(-1)
    onehot = (flat_ids[:, None] == jnp.arange(experts, dtype=jnp.int32)[None, :]).astype(jnp.int32)
    slot_rank = jnp.sum((jnp.cumsum(onehot, axis=0) - onehot) * onehot, axis=1)
    picked = jnp.dot(onehot.astype(jnp.float32), summed_dots, precision=lax.Precision.HIGHEST)
    at_rank = slot_rank[:, None] == jnp.arange(CAP, dtype=jnp.int32)[None, :]
    route_grads = (
        jnp.sum(jnp.where(at_rank, picked, 0.0), axis=1).reshape(tokens, -1) / rounded_weights
    )
    return (
        heads_grad,
        weight_grad,
        resid_grad,
        route_grads,
        gate_wgrad[None],
        up_wgrad[None],
        down_wgrad[None],
    )


def solution(mesh):
    split = P(("ctx", "tp"), None)
    stack = P(("ctx", "tp"), None, None)
    in_specs = (
        P("ctx", "tp"),
        P("ctx", "tp"),
        split,
        P(),
        split,
        split,
        stack,
        stack,
        stack,
        split,
    )
    out_specs = (P("ctx", "tp"), P("ctx", "tp"), split, split, stack, stack, stack)
    return jax.shard_map(
        per_device, mesh=mesh, in_specs=in_specs, out_specs=out_specs, check_vma=False
    )
```

```python
import functools

import jax
import jax.numpy as jnp
from jax import lax
from jax.experimental import pallas as pl
from jax.experimental.pallas import tpu as pltpu
from jax.sharding import PartitionSpec as P

EPSILON = 1e-06
CAP = 6
BLOCKS = 4
CHUNK = CAP * BLOCKS
CONTRACT_FIRST = (((0,), (0,)), ((), ()))
CONTRACT_LAST = (((1,), (1,)), ((), ()))
MIB = 1 << 20


def iota(shape, dim):
    return lax.broadcasted_iota(jnp.int32, shape, dim)


def mm(a, b, dims=(((1,), (0,)), ((), ()))):
    return lax.dot_general(a, b, dims, preferred_element_type=jnp.float32)


def dispatch_kernel(normalize, ids_ref, weight_ref, value_ref, gain_ref, out_ref, flat, unpack):
    tokens, features = value_ref.shape
    width = features // BLOCKS
    experts = flat.shape[0] // CAP
    group = out_ref.shape[0]
    step = pl.program_id(0)

    @pl.when(step == 0)
    def _():
        expert = iota((experts, tokens), 0)
        first = expert == ids_ref[0:1, :]
        second = expert == ids_ref[1:2, :]
        named = jnp.where(first | second, 1.0, 0.0)
        earlier = jnp.where(iota((tokens, tokens), 0) < iota((tokens, tokens), 1), 1.0, 0.0)
        prior = mm(named.astype(jnp.bfloat16), earlier.astype(jnp.bfloat16))
        unpack[...] = unpack_matrix(group)
        slots = jnp.where(named > 0.5, prior, -1.0).astype(jnp.bfloat16)
        row = iota((experts * CAP, experts), 0)
        expert_of = row // CAP
        spread = jnp.where(expert_of == iota((experts * CAP, experts), 1), 1.0, 0.0)
        spread = spread.astype(jnp.bfloat16)
        place = iota((experts * CAP, tokens), 0)
        place = (place - place // CAP * CAP).astype(jnp.float32)
        taken = mm(spread, slots) == place
        if normalize:
            picks = jnp.where(taken, 1.0, 0.0).astype(jnp.bfloat16)
            wide = value_ref[...].astype(jnp.float32)
            scale = lax.rsqrt(jnp.mean(wide * wide, axis=-1, keepdims=True) + EPSILON)
        else:
            weights = jnp.where(
                first, weight_ref[0:1, :], jnp.where(second, weight_ref[1:2, :], 0.0)
            ).astype(jnp.bfloat16)
            picks = jnp.where(taken, mm(spread, weights), 0.0).astype(jnp.bfloat16)
        for block in range(BLOCKS):
            columns = slice(block * width, (block + 1) * width)
            values = value_ref[:, columns]
            if normalize:
                values = (values.astype(jnp.float32) * scale * gain_ref[:, columns]).astype(jnp.bfloat16)
            flat[:, columns] = mm(picks, values).astype(jnp.bfloat16)

    height = group * CAP
    here = pl.ds(pl.multiple_of(step * height, height), height)
    stacked = jnp.concatenate(
        [flat[here, b * width:(b + 1) * width] for b in range(BLOCKS)], axis=0
    )
    chunks = mm(unpack[...], stacked, CONTRACT_FIRST).reshape(group, CHUNK, width)
    chunks = chunks.astype(jnp.bfloat16)
    for half in range(2):
        out_ref[:, half] = chunks


def dispatch(normalize, ids_t, weights_t, values, gain, experts):
    tokens, features = values.shape
    width = features // BLOCKS
    group = 8
    whole = lambda shape: pl.BlockSpec(shape, lambda i: (0, 0))
    return pl.pallas_call(
        functools.partial(dispatch_kernel, normalize),
        grid=(experts // group,),
        in_specs=[whole(ids_t.shape), whole(weights_t.shape), whole(values.shape), whole(gain.shape)],
        out_specs=pl.BlockSpec((group, 2, CHUNK, width), lambda i: (i, 0, 0, 0)),
        out_shape=jax.ShapeDtypeStruct((experts, 2, CHUNK, width), jnp.bfloat16),
        scratch_shapes=[
            pltpu.VMEM((experts * CAP, features), jnp.bfloat16),
            pltpu.VMEM((group * CHUNK, group * CHUNK), jnp.bfloat16),
        ],
        compiler_params=pltpu.CompilerParams(vmem_limit_bytes=60 * MIB),
        cost_estimate=pl.CostEstimate(
            flops=2 * experts * CHUNK * tokens * features, bytes_accessed=8 * MIB,
            transcendentals=0),
        name="dispatch_rows" if normalize else "dispatch_cots",
    )(ids_t, weights_t, values, gain)


def unpack_matrix(sources):
    rows = sources * CHUNK
    out, inp = iota((rows, rows), 0), iota((rows, rows), 1)
    block = out // (sources * CAP)
    rest = out - block * (sources * CAP)
    source = rest // CAP
    want = source * CHUNK + block * CAP + (rest - source * CAP)
    return jnp.where(inp == want, 1.0, 0.0).astype(jnp.bfloat16)


GROUP = 8


def unpack_rows(unpack, raw_ref, out_ref):
    rows = GROUP * CHUNK
    height = GROUP * CAP
    width = raw_ref.shape[1]
    for g in range(raw_ref.shape[0] // rows):
        flat = mm(unpack, raw_ref[g * rows:(g + 1) * rows, :]).astype(jnp.bfloat16)
        for b in range(BLOCKS):
            out_ref[g * height:(g + 1) * height, b * width:(b + 1) * width] = (
                flat[b * height:(b + 1) * height, :]
            )


def unpack_kernel(raw_ref, out_ref, unpack):
    @pl.when(pl.program_id(0) == 0)
    def _():
        unpack[...] = unpack_matrix(GROUP)

    unpack_rows(unpack[...], raw_ref, out_ref)


def unpack_chunks(raw, steps=8):
    total, width = raw.shape
    rows = total // steps
    return pl.pallas_call(
        unpack_kernel,
        grid=(steps,),
        in_specs=[pl.BlockSpec((rows, width), lambda i: (i, 0))],
        out_specs=pl.BlockSpec((rows // BLOCKS, width * BLOCKS), lambda i: (i, 0)),
        out_shape=jax.ShapeDtypeStruct((total // BLOCKS, width * BLOCKS), jnp.bfloat16),
        scratch_shapes=[pltpu.VMEM((GROUP * CHUNK, GROUP * CHUNK), jnp.bfloat16)],
        compiler_params=pltpu.CompilerParams(vmem_limit_bytes=40 * MIB),
        cost_estimate=pl.CostEstimate(
            flops=2 * total * GROUP * CHUNK * width, bytes_accessed=4 * total * width,
            transcendentals=0),
        name="unpack",
    )(raw)


def back_kernel(raw_ref, gate_ref, up_ref, w_gate_ref, w_up_ref, w_down_ref,
                grads_ref, cots_ref, act_ref, gate_grad_ref, up_grad_ref, dots_ref, unpack):
    @pl.when(pl.program_id(0) == 0)
    def _():
        unpack[...] = unpack_matrix(GROUP)

    unpack_rows(unpack[...], raw_ref, cots_ref)
    back = mm(cots_ref[...], w_down_ref[...], CONTRACT_LAST)
    gate_pre, up_value = gate_ref[...], up_ref[...]
    sigmoid = jax.nn.sigmoid(gate_pre)
    silu = gate_pre * sigmoid
    activated = (silu * up_value).astype(jnp.bfloat16)
    act_ref[...] = activated
    dots_ref[...] = jnp.sum(activated.astype(jnp.float32) * back, axis=-1, keepdims=True)
    gate_grad = (back * up_value * sigmoid * (1.0 + gate_pre * (1.0 - sigmoid))).astype(jnp.bfloat16)
    up_grad = (back * silu).astype(jnp.bfloat16)
    gate_grad_ref[...] = gate_grad
    up_grad_ref[...] = up_grad
    height = GROUP * CAP
    rows = GROUP * CHUNK
    width = raw_ref.shape[1]
    parts = []
    for b in range(BLOCKS):
        columns = slice(b * width, (b + 1) * width)
        parts.append(
            (mm(gate_grad, w_gate_ref[columns, :], CONTRACT_LAST)
             + mm(up_grad, w_up_ref[columns, :], CONTRACT_LAST)).astype(jnp.bfloat16)
        )
    for g in range(raw_ref.shape[0] // rows):
        stacked = jnp.concatenate([p[g * height:(g + 1) * height, :] for p in parts], axis=0)
        grads_ref[g * rows:(g + 1) * rows, :] = mm(
            unpack[...], stacked, CONTRACT_FIRST
        ).astype(jnp.bfloat16)


def expert_back(raw, gate_pre, up_value, w_gate, w_up, w_down, steps=2):
    total, width = raw.shape
    features, hidden = w_gate.shape
    slots = gate_pre.shape[0]
    rows = slots // steps
    tall = lambda shape: pl.BlockSpec(shape, lambda i: (i, 0))
    whole = lambda shape: pl.BlockSpec(shape, lambda i: (0, 0))
    small = jax.ShapeDtypeStruct((slots, hidden), jnp.bfloat16)
    return pl.pallas_call(
        back_kernel,
        grid=(steps,),
        in_specs=[tall((total // steps, width)), tall((rows, hidden)), tall((rows, hidden)),
                  whole(w_gate.shape), whole(w_up.shape), whole(w_down.shape)],
        out_specs=[tall((total // steps, width)), tall((rows, features))]
        + [tall((rows, hidden))] * 3 + [tall((rows, 1))],
        out_shape=[jax.ShapeDtypeStruct(raw.shape, jnp.bfloat16),
                   jax.ShapeDtypeStruct((slots, features), jnp.bfloat16),
                   small, small, small, jax.ShapeDtypeStruct((slots, 1), jnp.float32)],
        scratch_shapes=[pltpu.VMEM((GROUP * CHUNK, GROUP * CHUNK), jnp.bfloat16)],
        compiler_params=pltpu.CompilerParams(vmem_limit_bytes=56 * MIB),
        cost_estimate=pl.CostEstimate(
            flops=6 * slots * features * hidden + 4 * total * GROUP * CHUNK * width,
            bytes_accessed=32 * MIB, transcendentals=slots * hidden),
        name="expert_back",
    )(raw, gate_pre, up_value, w_gate, w_up, w_down)


def combine_kernel(ids_ref, back_ref, hidden_ref, gain_ref, cot_ref, resid_ref, slot, total):
    tokens, features = hidden_ref.shape
    width = features // BLOCKS
    experts = slot.shape[1]
    rows = back_ref.shape[0]
    step = pl.program_id(0)

    @pl.when(step == 0)
    def _():
        expert = iota((tokens, experts), 1)
        named = jnp.where((expert == ids_ref[:, 0:1]) | (expert == ids_ref[:, 1:2]), 1.0, 0.0)
        earlier = jnp.where(iota((tokens, tokens), 1) < iota((tokens, tokens), 0), 1.0, 0.0)
        prior = mm(earlier.astype(jnp.bfloat16), named.astype(jnp.bfloat16))
        slot[...] = jnp.where(named > 0.5, prior, -1.0).astype(jnp.bfloat16)
        total[...] = jnp.zeros_like(total)

    spread_at = iota((experts, rows), 1) // (2 * CHUNK) + step * (rows // (2 * CHUNK))
    spread = jnp.where(iota((experts, rows), 0) == spread_at, 1.0, 0.0).astype(jnp.bfloat16)
    slots = mm(slot[...], spread)
    lane = iota((tokens, rows), 1)
    piece = lane // CAP
    taken = jnp.where(slots == (lane - piece * CAP).astype(jnp.float32), 1.0, 0.0)
    block_of = piece - piece // BLOCKS * BLOCKS
    picks = jnp.concatenate(
        [jnp.where(block_of == b, taken, 0.0).astype(jnp.bfloat16) for b in range(BLOCKS)], axis=0
    )
    total[...] += mm(picks, back_ref[...])

    @pl.when(step == pl.num_programs(0) - 1)
    def _():
        wide = hidden_ref[...].astype(jnp.float32)
        scale = lax.rsqrt(jnp.mean(wide * wide, axis=-1, keepdims=True) + EPSILON)
        inner = jnp.zeros((tokens, 1), jnp.float32)
        for b in range(BLOCKS):
            columns = slice(b * width, (b + 1) * width)
            rows = slice(b * tokens, (b + 1) * tokens)
            gained = total[rows, :] * gain_ref[:, columns]
            inner += jnp.sum(
                gained * hidden_ref[:, columns].astype(jnp.float32), axis=-1, keepdims=True
            )
        inner = (scale * scale * scale) * (inner / features)
        for b in range(BLOCKS):
            columns = slice(b * width, (b + 1) * width)
            rows = slice(b * tokens, (b + 1) * tokens)
            gained = total[rows, :] * gain_ref[:, columns]
            resid_ref[:, columns] = (
                cot_ref[:, columns].astype(jnp.float32) + scale * gained
                - hidden_ref[:, columns].astype(jnp.float32) * inner
            ).astype(jnp.bfloat16)


def combine(ids, back, hidden, gain, cots, experts, steps=4):
    tokens, features = hidden.shape
    total, width = back.shape
    whole = lambda shape: pl.BlockSpec(shape, lambda i: (0, 0))
    return pl.pallas_call(
        combine_kernel,
        grid=(steps,),
        in_specs=[whole(ids.shape), pl.BlockSpec((total // steps, width), lambda i: (i, 0)),
                  whole(hidden.shape), whole(gain.shape), whole(cots.shape)],
        out_specs=whole(hidden.shape),
        out_shape=jax.ShapeDtypeStruct(hidden.shape, jnp.bfloat16),
        scratch_shapes=[pltpu.VMEM((tokens, experts), jnp.bfloat16),
                        pltpu.VMEM((BLOCKS * tokens, width), jnp.float32)],
        compiler_params=pltpu.CompilerParams(vmem_limit_bytes=61 * MIB),
        cost_estimate=pl.CostEstimate(
            flops=2 * BLOCKS * tokens * total * width, bytes_accessed=12 * MIB, transcendentals=0),
        name="combine",
    )(ids, back, hidden, gain, cots)


STEPS = 4
SAME_L, SAME_R, SAME_T, SAME_B, FAR_C, FAR_L, FAR_R, FAR_T, FAR_B = range(9)
TO_Z, TO_R, TO_L, PASS_R, PASS_L, EXTRA_A, EXTRA_B, EXTRA_C, EXTRA_D = range(9)


EXTRA = 16


def project_kernel(resid_ref, heads_ref, weight_ref, dots_ref,
                   out_heads_ref, out_weight_ref, out_dots_ref,
                   heads, heads_t, dots_all, dots_rows, pieces, total, partial, from_core, summed, from_y, to_z, from_z, blocks,
                   piece_send, piece_recv, core_send, core_recv, y_send, y_recv, z_send, z_recv,
                   block_send, block_y_recv, block_core_recv, block_z_recv,
                   local, dots_send, dots_recv):
    ctx, tp = lax.axis_index("ctx"), lax.axis_index("tp")
    y, z_hi, core = ctx // 4, (ctx // 2) % 2, ctx % 2
    z_lo, x = tp // 4, tp % 4
    right_x, left_x, opposite_x = (x + 1) % 4, (x + 3) % 4, (x + 2) % 4
    here, there = z_lo * 4, (1 - z_lo) * 4
    right, left, far = (ctx, here + right_x), (ctx, here + left_x), (ctx, there + x)
    sibling = (y * 4 + z_hi * 2 + (1 - core), tp)
    across = (y * 4 + (1 - z_hi) * 2 + core, tp)
    plane = lambda other: (other * 4 + z_hi * 2 + core, tp)
    tokens, features = resid_ref.shape
    chunk = features // STEPS
    rows = chunk // 4
    half = tokens // 2
    group = pieces.shape[1]

    columns = heads.shape[1]

    def owner(i):
        return (y + 1 + i) % 4

    def fetch(i):
        lanes = pl.ds(pl.multiple_of(owner(i) * chunk, chunk), chunk)
        return pltpu.make_async_copy(resid_ref.at[:, lanes], pieces.at[i, tp], local.at[i])

    fetch_heads = pltpu.make_async_copy(heads_ref, heads, local.at[STEPS])
    for i in range(STEPS):
        fetch(i).start()
    fetch_heads.start()

    barrier = pltpu.get_barrier_semaphore()
    peers = [(ctx, (tp + d) % group) for d in range(1, group)]
    peers += [sibling, across] + [plane((y + d) % 4) for d in (1, 2, 3)]
    for peer in peers:
        pl.semaphore_signal(barrier, inc=1, device_id=peer, device_id_type=pl.DeviceIdType.MESH)
    pl.semaphore_wait(barrier, len(peers))

    def remote(src, dst, send, recv, device):
        return pltpu.make_async_remote_copy(
            src_ref=src, dst_ref=dst, send_sem=send, recv_sem=recv,
            device_id=device, device_id_type=pl.DeviceIdType.MESH,
        )

    whole, top, bottom = pl.ds(0, tokens), pl.ds(0, half), pl.ds(half, half)
    sent = []

    def send(i, piece, part, kind, lands, device):
        ref = pieces.at[i, piece, part]
        copy = remote(ref, ref, piece_send.at[i, kind], piece_recv.at[i, lands], device)
        copy.start()
        sent.append(copy)

    def arrive(i, piece, part, lands):
        ref = pieces.at[i, piece, part]
        remote(ref, ref, piece_send.at[i, 0], piece_recv.at[i, lands], far).wait_recv()

    def start_own(i):
        fetch(i).wait()
        send(i, tp, whole, TO_R, SAME_L, right)
        send(i, tp, whole, TO_L, SAME_R, left)
        send(i, tp, whole, TO_Z, FAR_C, far)

    def send_block(p, zh, semaphore, lands, device):
        ref = blocks.at[p, zh, core]
        copy = remote(ref, ref, semaphore, lands, device)
        copy.start()
        sent.append(copy)

    def block_arrives(p, zh, whose, lands):
        ref = blocks.at[p, zh, whose]
        remote(ref, ref, block_send.at[0], lands, sibling).wait_recv()

    def start_blocks():
        blocks[y, z_hi, core] = weight_ref[...]
        send_block(y, z_hi, block_send.at[0], block_z_recv, across)
        for i in range(STEPS - 1):
            send_block(y, z_hi, block_send.at[1 + i], block_y_recv.at[0, i], plane((y + 3 - i) % 4))
        send_block(y, z_hi, block_send.at[7], block_core_recv.at[0, STEPS - 1], sibling)

    def pass_blocks():
        block_arrives(y, 1 - z_hi, core, block_z_recv)
        for i in range(STEPS - 1):
            send_block(
                y, 1 - z_hi, block_send.at[4 + i], block_y_recv.at[1, i], plane((y + 3 - i) % 4)
            )
        send_block(y, 1 - z_hi, block_send.at[8], block_core_recv.at[1, STEPS - 1], sibling)

    def share_blocks(i):
        for side in range(2):
            zh = z_hi if side == 0 else 1 - z_hi
            block_arrives(owner(i), zh, core, block_y_recv.at[side, i])
            send_block(
                owner(i), zh, block_send.at[9 + 2 * i + side], block_core_recv.at[side, i], sibling
            )

    def blocks_ready(i):
        for side in range(2):
            zh = z_hi if side == 0 else 1 - z_hi
            block_arrives(owner(i), zh, 1 - core, block_core_recv.at[side, i])

    def first_hops(i):
        if i % 2 == 0:
            arrive(i, there + x, whole, FAR_C)
            send(i, there + x, whole, EXTRA_A, FAR_L, right)
            send(i, there + x, whole, EXTRA_B, FAR_R, left)
        arrive(i, here + left_x, whole, SAME_L)
        send(i, here + left_x, top, PASS_R, SAME_T, right)
        if i % 2 == 1:
            send(i, here + left_x, whole, EXTRA_A, FAR_L, far)
        arrive(i, here + right_x, whole, SAME_R)
        send(i, here + right_x, bottom, PASS_L, SAME_B, left)
        if i % 2 == 1:
            send(i, here + right_x, whole, EXTRA_B, FAR_R, far)

    def second_hops(i):
        if i % 2 == 0:
            arrive(i, there + left_x, whole, FAR_L)
            send(i, there + left_x, top, EXTRA_C, FAR_T, right)
            arrive(i, there + right_x, whole, FAR_R)
            send(i, there + right_x, bottom, EXTRA_D, FAR_B, left)
        else:
            arrive(i, here + opposite_x, top, SAME_T)
            send(i, here + opposite_x, top, EXTRA_C, FAR_T, far)
            arrive(i, here + opposite_x, bottom, SAME_B)
            send(i, here + opposite_x, bottom, EXTRA_D, FAR_B, far)

    def arrivals(i):
        if i % 2 == 0:
            arrive(i, here + opposite_x, top, SAME_T)
            arrive(i, here + opposite_x, bottom, SAME_B)
        else:
            arrive(i, there + x, whole, FAR_C)
            arrive(i, there + left_x, whole, FAR_L)
            arrive(i, there + right_x, whole, FAR_R)
        arrive(i, there + opposite_x, top, FAR_T)
        arrive(i, there + opposite_x, bottom, FAR_B)

    def start_dots():
        dots_all[tp] = dots_ref[...]
        for d in range(1, group):
            ref = dots_all.at[tp]
            copy = remote(
                ref, ref, dots_send.at[d - 1], dots_recv.at[d - 1], (ctx, (tp + d) % group)
            )
            copy.start()
            sent.append(copy)

    def gather_dots():
        for d in range(1, group):
            ref = dots_all.at[(tp + group - d) % group]
            remote(ref, ref, dots_send.at[0], dots_recv.at[d - 1], far).wait_recv()
        sources = dots_all.shape[2]
        count = group * EXTRA
        table = dots_all[...].reshape(count, sources)
        mine = iota((16, sources), 1) == iota((16, sources), 0) * group + tp
        mine = jnp.where(mine, 1.0, 0.0).astype(jnp.bfloat16)
        held = mm(mine, table, CONTRACT_LAST).astype(jnp.bfloat16)
        row, lane = iota((count, 2 * rows), 0), iota((count, 2 * rows), 1)
        device = row // EXTRA
        slot = row - device * EXTRA
        place = jnp.where(slot < CAP, (ctx * 4 + device // 2) * CAP + slot, -1)
        spread = jnp.where(lane == place, 1.0, 0.0).astype(jnp.bfloat16)
        dots_rows[...] = mm(held, spread)

    def turn_heads():
        fetch_heads.wait()
        for r in range(4):
            part = heads.shape[0] // 4
            heads_t[:, r * part:(r + 1) * part] = heads[r * part:(r + 1) * part, :].T

    def weight_partial(i, whose):
        def one(zh, carry):
            local_owner = 2 * zh + (core if whose == 0 else 1 - core)
            first = pl.multiple_of(local_owner * rows, rows)
            right_side = pieces[i, :, :, pl.ds(first, rows)].reshape(group * tokens, rows)
            value = mm(heads_t[...], right_side)
            partial[i, whose, zh, 0:columns] = value.astype(jnp.bfloat16)
            at = iota((16, 2 * rows), 0) == owner(i) * 4 + local_owner
            line = jnp.sum(jnp.where(at, dots_rows[...], 0.0), axis=0, keepdims=True)
            row = iota((EXTRA, rows), 0)
            tail = jnp.where(row == 0, line[:, :rows], jnp.where(row == 1, line[:, rows:], 0.0))
            partial[i, whose, zh, columns:columns + EXTRA] = tail.astype(jnp.bfloat16)
            return carry

        lax.fori_loop(0, 2, one, 0)

    def heads_partial(i):
        def one(r, carry):
            tall = pl.ds(pl.multiple_of(r * 2 * tokens, 2 * tokens), 2 * tokens)
            left_side = pieces[i, pl.ds(2 * r, 2)].reshape(2 * tokens, chunk)
            value = mm(left_side, blocks[owner(i)].reshape(chunk, blocks.shape[-1]))
            if i > 0:
                value = value + total[tall, :]
            if i < STEPS - 1:
                total[tall, :] = value
            else:
                out_heads_ref[tall, :] = value.astype(jnp.bfloat16)
            return carry

        lax.fori_loop(0, group // 2, one, 0)

    def multiply(i, between=()):
        weight_partial(i, 1)
        to_core = remote(partial.at[i, 1], from_core.at[i], core_send.at[i], core_recv.at[i], sibling)
        to_core.start()
        weight_partial(i, 0)
        for hops, other in between:
            hops(other)
        if i == STEPS - 1:
            return to_core
        blocks_ready(i)
        heads_partial(i)
        to_core.wait()
        summed[i] = (
            partial[i, 0].astype(jnp.float32) + from_core[i].astype(jnp.float32)
        ).astype(jnp.bfloat16)
        copy = remote(summed.at[i], from_y.at[i], y_send.at[i], y_recv.at[i], plane(owner(i)))
        copy.start()
        sent.append(copy)

    start_own(0)
    start_own(1)
    start_dots()
    start_blocks()
    turn_heads()
    first_hops(0)
    pass_blocks()
    first_hops(1)
    second_hops(0)
    start_own(2)
    second_hops(1)
    start_own(3)
    gather_dots()
    share_blocks(0)
    arrivals(0)
    multiply(0, ((share_blocks, 1),))
    arrivals(1)
    multiply(1, ((first_hops, 2), (first_hops, 3), (share_blocks, 2)))
    second_hops(2)
    second_hops(3)
    arrivals(2)
    multiply(2)
    arrivals(3)
    to_core = multiply(3)

    last = STEPS - 1

    def reduced(zh):
        value = partial[last, 0, zh].astype(jnp.float32) + from_core[last, zh].astype(jnp.float32)
        for i in range(last):
            value = value + from_y[i, zh].astype(jnp.float32)
        return value

    to_core.wait()
    for i in range(last):
        remote(summed.at[i], from_y.at[i], y_send.at[i], y_recv.at[i], across).wait_recv()
    to_z[...] = reduced(1 - z_hi).astype(jnp.bfloat16)
    copy = remote(to_z, from_z, z_send, z_recv, across)
    copy.start()
    blocks_ready(last)
    heads_partial(last)
    own = reduced(z_hi)
    copy.wait()
    own = own + from_z[...].astype(jnp.float32)
    out_weight_ref[...] = own[:columns].T.astype(jnp.bfloat16)
    out_dots_ref[...] = own[columns:]
    for copy in sent:
        copy.wait_send()


def project(resid, heads, weight, dots, group):
    tokens, features = resid.shape
    columns = heads.shape[1]
    chunk = features // STEPS
    rows = chunk // 4
    tall = columns + EXTRA
    bf16 = jnp.bfloat16
    dma = pltpu.SemaphoreType.DMA
    vmem = pl.BlockSpec(memory_space=pltpu.VMEM)
    anywhere = pl.BlockSpec(memory_space=pltpu.HBM)
    return pl.pallas_call(
        project_kernel,
        in_specs=[anywhere, anywhere, vmem, vmem],
        out_specs=[vmem] * 3,
        out_shape=[jax.ShapeDtypeStruct(heads.shape, bf16), jax.ShapeDtypeStruct((rows, columns), bf16),
                   jax.ShapeDtypeStruct((EXTRA, rows), jnp.float32)],
        scratch_shapes=[
            pltpu.VMEM(heads.shape, bf16),
            pltpu.VMEM(heads.shape[::-1], bf16),
            pltpu.VMEM((group,) + dots.shape, bf16),
            pltpu.VMEM((16, 2 * rows), jnp.float32),
            pltpu.VMEM((STEPS, group, tokens, chunk), bf16),
            pltpu.VMEM(heads.shape, jnp.float32),
            pltpu.VMEM((STEPS, 2, 2, tall, rows), bf16),
            pltpu.VMEM((STEPS, 2, tall, rows), bf16),
            pltpu.VMEM((STEPS - 1, 2, tall, rows), bf16),
            pltpu.VMEM((STEPS - 1, 2, tall, rows), bf16),
            pltpu.VMEM((tall, rows), bf16),
            pltpu.VMEM((tall, rows), bf16),
            pltpu.VMEM((STEPS, 2, 2, rows, columns), bf16),
            dma((STEPS, 9)), dma((STEPS, 9)), dma((STEPS,)), dma((STEPS,)),
            dma((STEPS - 1,)), dma((STEPS - 1,)), dma, dma,
            dma((15,)), dma((2, STEPS - 1)), dma((2, STEPS)), dma,
            dma((STEPS + 1,)), dma((group - 1,)), dma((group - 1,)),
        ],
        compiler_params=pltpu.CompilerParams(
            collective_id=0, has_side_effects=True, vmem_limit_bytes=61 * MIB),
        cost_estimate=pl.CostEstimate(
            flops=4 * group * tokens * features * columns, bytes_accessed=8 * MIB, transcendentals=0),
        name="project",
    )(resid, heads, weight, dots)


def per_device(
    ctx_heads,
    out_weight,
    hidden_in,
    norm_gain,
    expert_ids,
    route_weights,
    w_gate,
    w_up,
    w_down,
    grad_out,
):
    tokens, features = hidden_in.shape
    devices = lax.axis_size(("ctx", "tp"))
    experts = devices // 2
    axes = ("ctx", "tp")
    exchange = functools.partial(
        lax.all_to_all, axis_name=axes, split_axis=0, concat_axis=0, tiled=True
    )
    width = features // BLOCKS
    gain = norm_gain.reshape(1, features)
    rounded_weights = route_weights.astype(jnp.bfloat16).astype(jnp.float32)
    ids_t, weights_t = expert_ids.T, rounded_weights.T
    send_rows = dispatch(True, ids_t, ids_t, hidden_in, gain, experts)
    send_cots = dispatch(False, ids_t, weights_t, grad_out, gain, experts)
    raw_rows = exchange(send_rows.reshape(devices, CHUNK, width)).reshape(-1, width)
    raw_cots = exchange(send_cots.reshape(devices, CHUNK, width)).reshape(-1, width)
    slot_rows = unpack_chunks(raw_rows)
    gate_pre = mm(slot_rows, w_gate[0])
    up_value = mm(slot_rows, w_up[0])
    grads, slot_cots, activated, gate_grad, up_grad, dots = expert_back(
        raw_cots, gate_pre, up_value, w_gate[0], w_up[0], w_down[0]
    )
    back = exchange(grads.reshape(devices, CHUNK, width)).reshape(-1, width)
    sent_dots = jnp.pad(dots.reshape(devices, CAP).T, ((0, EXTRA - CAP), (0, 0)))
    down_wgrad = mm(activated, slot_cots, CONTRACT_FIRST).astype(jnp.bfloat16)
    gate_wgrad = mm(slot_rows, gate_grad, CONTRACT_FIRST).astype(jnp.bfloat16)
    up_wgrad = mm(slot_rows, up_grad, CONTRACT_FIRST).astype(jnp.bfloat16)
    resid_grad = combine(expert_ids, back, hidden_in, gain, grad_out, experts)

    heads_grad, weight_grad, summed_dots = project(
        resid_grad, ctx_heads, out_weight, sent_dots.astype(jnp.bfloat16), lax.axis_size("tp")
    )
    summed_dots = summed_dots[:2].reshape(-1)[:experts * CAP].reshape(experts, CAP)
    flat_ids = expert_ids.reshape(-1)
    onehot = (flat_ids[:, None] == jnp.arange(experts, dtype=jnp.int32)[None, :]).astype(jnp.int32)
    slot_rank = jnp.sum((jnp.cumsum(onehot, axis=0) - onehot) * onehot, axis=1)
    picked = jnp.dot(onehot.astype(jnp.float32), summed_dots, precision=lax.Precision.HIGHEST)
    at_rank = slot_rank[:, None] == jnp.arange(CAP, dtype=jnp.int32)[None, :]
    route_grads = (
        jnp.sum(jnp.where(at_rank, picked, 0.0), axis=1).reshape(tokens, -1) / rounded_weights
    )
    return (
        heads_grad,
        weight_grad,
        resid_grad,
        route_grads,
        gate_wgrad[None],
        up_wgrad[None],
        down_wgrad[None],
    )


def solution(mesh):
    split = P(("ctx", "tp"), None)
    stack = P(("ctx", "tp"), None, None)
    in_specs = (
        P("ctx", "tp"),
        P("ctx", "tp"),
        split,
        P(),
        split,
        split,
        stack,
        stack,
        stack,
        split,
    )
    out_specs = (P("ctx", "tp"), P("ctx", "tp"), split, split, stack, stack, stack)
    return jax.shard_map(
        per_device, mesh=mesh, in_specs=in_specs, out_specs=out_specs, check_vma=False
    )
```

```python
import functools

import jax
import jax.numpy as jnp
from jax import lax
from jax.experimental import pallas as pl
from jax.experimental.pallas import tpu as pltpu
from jax.sharding import PartitionSpec as P

EPSILON = 1e-06
CAP = 6
BLOCKS = 4
CHUNK = CAP * BLOCKS
CONTRACT_FIRST = (((0,), (0,)), ((), ()))
CONTRACT_LAST = (((1,), (1,)), ((), ()))
MIB = 1 << 20


def iota(shape, dim):
    return lax.broadcasted_iota(jnp.int32, shape, dim)


def mm(a, b, dims=(((1,), (0,)), ((), ()))):
    return lax.dot_general(a, b, dims, preferred_element_type=jnp.float32)


def dispatch_kernel(normalize, ids_ref, weight_ref, value_ref, gain_ref, out_ref, flat, unpack):
    tokens, features = value_ref.shape
    width = features // BLOCKS
    experts = flat.shape[0] // CAP
    group = out_ref.shape[0]
    step = pl.program_id(0)

    @pl.when(step == 0)
    def _():
        expert = iota((experts, tokens), 0)
        first = expert == ids_ref[0:1, :]
        second = expert == ids_ref[1:2, :]
        named = jnp.where(first | second, 1.0, 0.0)
        earlier = jnp.where(iota((tokens, tokens), 0) < iota((tokens, tokens), 1), 1.0, 0.0)
        prior = mm(named.astype(jnp.bfloat16), earlier.astype(jnp.bfloat16))
        unpack[...] = unpack_matrix(group)
        slots = jnp.where(named > 0.5, prior, -1.0).astype(jnp.bfloat16)
        row = iota((experts * CAP, experts), 0)
        expert_of = row // CAP
        spread = jnp.where(expert_of == iota((experts * CAP, experts), 1), 1.0, 0.0)
        spread = spread.astype(jnp.bfloat16)
        place = iota((experts * CAP, tokens), 0)
        place = (place - place // CAP * CAP).astype(jnp.float32)
        taken = mm(spread, slots) == place
        if normalize:
            picks = jnp.where(taken, 1.0, 0.0).astype(jnp.bfloat16)
            wide = value_ref[...].astype(jnp.float32)
            scale = lax.rsqrt(jnp.mean(wide * wide, axis=-1, keepdims=True) + EPSILON)
        else:
            weights = jnp.where(
                first, weight_ref[0:1, :], jnp.where(second, weight_ref[1:2, :], 0.0)
            ).astype(jnp.bfloat16)
            picks = jnp.where(taken, mm(spread, weights), 0.0).astype(jnp.bfloat16)
        for block in range(BLOCKS):
            columns = slice(block * width, (block + 1) * width)
            values = value_ref[:, columns]
            if normalize:
                values = (values.astype(jnp.float32) * scale * gain_ref[:, columns]).astype(jnp.bfloat16)
            flat[:, columns] = mm(picks, values).astype(jnp.bfloat16)

    height = group * CAP
    here = pl.ds(pl.multiple_of(step * height, height), height)
    stacked = jnp.concatenate(
        [flat[here, b * width:(b + 1) * width] for b in range(BLOCKS)], axis=0
    )
    chunks = mm(unpack[...], stacked, CONTRACT_FIRST).reshape(group, CHUNK, width)
    chunks = chunks.astype(jnp.bfloat16)
    for half in range(2):
        out_ref[:, half] = chunks


def dispatch(normalize, ids_t, weights_t, values, gain, experts):
    tokens, features = values.shape
    width = features // BLOCKS
    group = 8
    whole = lambda shape: pl.BlockSpec(shape, lambda i: (0, 0))
    return pl.pallas_call(
        functools.partial(dispatch_kernel, normalize),
        grid=(experts // group,),
        in_specs=[whole(ids_t.shape), whole(weights_t.shape), whole(values.shape), whole(gain.shape)],
        out_specs=pl.BlockSpec((group, 2, CHUNK, width), lambda i: (i, 0, 0, 0)),
        out_shape=jax.ShapeDtypeStruct((experts, 2, CHUNK, width), jnp.bfloat16),
        scratch_shapes=[
            pltpu.VMEM((experts * CAP, features), jnp.bfloat16),
            pltpu.VMEM((group * CHUNK, group * CHUNK), jnp.bfloat16),
        ],
        compiler_params=pltpu.CompilerParams(vmem_limit_bytes=60 * MIB),
        cost_estimate=pl.CostEstimate(
            flops=2 * experts * CHUNK * tokens * features, bytes_accessed=8 * MIB,
            transcendentals=0),
        name="dispatch_rows" if normalize else "dispatch_cots",
    )(ids_t, weights_t, values, gain)


def unpack_matrix(sources):
    rows = sources * CHUNK
    out, inp = iota((rows, rows), 0), iota((rows, rows), 1)
    block = out // (sources * CAP)
    rest = out - block * (sources * CAP)
    source = rest // CAP
    want = source * CHUNK + block * CAP + (rest - source * CAP)
    return jnp.where(inp == want, 1.0, 0.0).astype(jnp.bfloat16)


GROUP = 8


def unpack_rows(unpack, raw_ref, out_ref):
    rows = GROUP * CHUNK
    height = GROUP * CAP
    width = raw_ref.shape[1]
    for g in range(raw_ref.shape[0] // rows):
        flat = mm(unpack, raw_ref[g * rows:(g + 1) * rows, :]).astype(jnp.bfloat16)
        for b in range(BLOCKS):
            out_ref[g * height:(g + 1) * height, b * width:(b + 1) * width] = (
                flat[b * height:(b + 1) * height, :]
            )


def unpack_kernel(raw_ref, out_ref, unpack):
    @pl.when(pl.program_id(0) == 0)
    def _():
        unpack[...] = unpack_matrix(GROUP)

    unpack_rows(unpack[...], raw_ref, out_ref)


def unpack_chunks(raw, steps=8):
    total, width = raw.shape
    rows = total // steps
    return pl.pallas_call(
        unpack_kernel,
        grid=(steps,),
        in_specs=[pl.BlockSpec((rows, width), lambda i: (i, 0))],
        out_specs=pl.BlockSpec((rows // BLOCKS, width * BLOCKS), lambda i: (i, 0)),
        out_shape=jax.ShapeDtypeStruct((total // BLOCKS, width * BLOCKS), jnp.bfloat16),
        scratch_shapes=[pltpu.VMEM((GROUP * CHUNK, GROUP * CHUNK), jnp.bfloat16)],
        compiler_params=pltpu.CompilerParams(vmem_limit_bytes=40 * MIB),
        cost_estimate=pl.CostEstimate(
            flops=2 * total * GROUP * CHUNK * width, bytes_accessed=4 * total * width,
            transcendentals=0),
        name="unpack",
    )(raw)


def back_kernel(raw_ref, gate_ref, up_ref, w_gate_ref, w_up_ref, w_down_ref,
                grads_ref, cots_ref, act_ref, gate_grad_ref, up_grad_ref, dots_ref, unpack):
    @pl.when(pl.program_id(0) == 0)
    def _():
        unpack[...] = unpack_matrix(GROUP)

    unpack_rows(unpack[...], raw_ref, cots_ref)
    back = mm(cots_ref[...], w_down_ref[...], CONTRACT_LAST)
    gate_pre, up_value = gate_ref[...], up_ref[...]
    sigmoid = jax.nn.sigmoid(gate_pre)
    silu = gate_pre * sigmoid
    activated = (silu * up_value).astype(jnp.bfloat16)
    act_ref[...] = activated
    dots_ref[...] = jnp.sum(activated.astype(jnp.float32) * back, axis=-1, keepdims=True)
    gate_grad = (back * up_value * sigmoid * (1.0 + gate_pre * (1.0 - sigmoid))).astype(jnp.bfloat16)
    up_grad = (back * silu).astype(jnp.bfloat16)
    gate_grad_ref[...] = gate_grad
    up_grad_ref[...] = up_grad
    height = GROUP * CAP
    rows = GROUP * CHUNK
    width = raw_ref.shape[1]
    parts = []
    for b in range(BLOCKS):
        columns = slice(b * width, (b + 1) * width)
        parts.append(
            (mm(gate_grad, w_gate_ref[columns, :], CONTRACT_LAST)
             + mm(up_grad, w_up_ref[columns, :], CONTRACT_LAST)).astype(jnp.bfloat16)
        )
    for g in range(raw_ref.shape[0] // rows):
        stacked = jnp.concatenate([p[g * height:(g + 1) * height, :] for p in parts], axis=0)
        grads_ref[g * rows:(g + 1) * rows, :] = mm(
            unpack[...], stacked, CONTRACT_FIRST
        ).astype(jnp.bfloat16)


def expert_back(raw, gate_pre, up_value, w_gate, w_up, w_down, steps=2):
    total, width = raw.shape
    features, hidden = w_gate.shape
    slots = gate_pre.shape[0]
    rows = slots // steps
    tall = lambda shape: pl.BlockSpec(shape, lambda i: (i, 0))
    whole = lambda shape: pl.BlockSpec(shape, lambda i: (0, 0))
    small = jax.ShapeDtypeStruct((slots, hidden), jnp.bfloat16)
    return pl.pallas_call(
        back_kernel,
        grid=(steps,),
        in_specs=[tall((total // steps, width)), tall((rows, hidden)), tall((rows, hidden)),
                  whole(w_gate.shape), whole(w_up.shape), whole(w_down.shape)],
        out_specs=[tall((total // steps, width)), tall((rows, features))]
        + [tall((rows, hidden))] * 3 + [tall((rows, 1))],
        out_shape=[jax.ShapeDtypeStruct(raw.shape, jnp.bfloat16),
                   jax.ShapeDtypeStruct((slots, features), jnp.bfloat16),
                   small, small, small, jax.ShapeDtypeStruct((slots, 1), jnp.float32)],
        scratch_shapes=[pltpu.VMEM((GROUP * CHUNK, GROUP * CHUNK), jnp.bfloat16)],
        compiler_params=pltpu.CompilerParams(vmem_limit_bytes=56 * MIB),
        cost_estimate=pl.CostEstimate(
            flops=6 * slots * features * hidden + 4 * total * GROUP * CHUNK * width,
            bytes_accessed=32 * MIB, transcendentals=slots * hidden),
        name="expert_back",
    )(raw, gate_pre, up_value, w_gate, w_up, w_down)


def combine_kernel(ids_ref, back_ref, hidden_ref, gain_ref, cot_ref, resid_ref, slot, total):
    tokens, features = hidden_ref.shape
    width = features // BLOCKS
    experts = slot.shape[1]
    rows = back_ref.shape[0]
    step = pl.program_id(0)

    @pl.when(step == 0)
    def _():
        expert = iota((tokens, experts), 1)
        named = jnp.where((expert == ids_ref[:, 0:1]) | (expert == ids_ref[:, 1:2]), 1.0, 0.0)
        earlier = jnp.where(iota((tokens, tokens), 1) < iota((tokens, tokens), 0), 1.0, 0.0)
        prior = mm(earlier.astype(jnp.bfloat16), named.astype(jnp.bfloat16))
        slot[...] = jnp.where(named > 0.5, prior, -1.0).astype(jnp.bfloat16)
        total[...] = jnp.zeros_like(total)

    spread_at = iota((experts, rows), 1) // (2 * CHUNK) + step * (rows // (2 * CHUNK))
    spread = jnp.where(iota((experts, rows), 0) == spread_at, 1.0, 0.0).astype(jnp.bfloat16)
    slots = mm(slot[...], spread)
    lane = iota((tokens, rows), 1)
    piece = lane // CAP
    taken = jnp.where(slots == (lane - piece * CAP).astype(jnp.float32), 1.0, 0.0)
    block_of = piece - piece // BLOCKS * BLOCKS
    picks = jnp.concatenate(
        [jnp.where(block_of == b, taken, 0.0).astype(jnp.bfloat16) for b in range(BLOCKS)], axis=0
    )
    total[...] += mm(picks, back_ref[...])

    @pl.when(step == pl.num_programs(0) - 1)
    def _():
        wide = hidden_ref[...].astype(jnp.float32)
        scale = lax.rsqrt(jnp.mean(wide * wide, axis=-1, keepdims=True) + EPSILON)
        inner = jnp.zeros((tokens, 1), jnp.float32)
        for b in range(BLOCKS):
            columns = slice(b * width, (b + 1) * width)
            rows = slice(b * tokens, (b + 1) * tokens)
            gained = total[rows, :] * gain_ref[:, columns]
            inner += jnp.sum(
                gained * hidden_ref[:, columns].astype(jnp.float32), axis=-1, keepdims=True
            )
        inner = (scale * scale * scale) * (inner / features)
        for b in range(BLOCKS):
            columns = slice(b * width, (b + 1) * width)
            rows = slice(b * tokens, (b + 1) * tokens)
            gained = total[rows, :] * gain_ref[:, columns]
            resid_ref[:, columns] = (
                cot_ref[:, columns].astype(jnp.float32) + scale * gained
                - hidden_ref[:, columns].astype(jnp.float32) * inner
            ).astype(jnp.bfloat16)


def combine(ids, back, hidden, gain, cots, experts, steps=4):
    tokens, features = hidden.shape
    total, width = back.shape
    whole = lambda shape: pl.BlockSpec(shape, lambda i: (0, 0))
    return pl.pallas_call(
        combine_kernel,
        grid=(steps,),
        in_specs=[whole(ids.shape), pl.BlockSpec((total // steps, width), lambda i: (i, 0)),
                  whole(hidden.shape), whole(gain.shape), whole(cots.shape)],
        out_specs=whole(hidden.shape),
        out_shape=jax.ShapeDtypeStruct(hidden.shape, jnp.bfloat16),
        scratch_shapes=[pltpu.VMEM((tokens, experts), jnp.bfloat16),
                        pltpu.VMEM((BLOCKS * tokens, width), jnp.float32)],
        compiler_params=pltpu.CompilerParams(vmem_limit_bytes=61 * MIB),
        cost_estimate=pl.CostEstimate(
            flops=2 * BLOCKS * tokens * total * width, bytes_accessed=12 * MIB, transcendentals=0),
        name="combine",
    )(ids, back, hidden, gain, cots)


STEPS = 4
SAME_L, SAME_R, SAME_T, SAME_B, FAR_C, FAR_L, FAR_R, FAR_T, FAR_B = range(9)
TO_Z, TO_R, TO_L, PASS_R, PASS_L, EXTRA_A, EXTRA_B, EXTRA_C, EXTRA_D = range(9)


EXTRA = 16


def project_kernel(resid_ref, heads_ref, weight_ref, dots_ref,
                   out_heads_ref, out_weight_ref, out_dots_ref,
                   heads, heads_t, dots_all, dots_rows, pieces, total, partial, from_core, summed, from_y, to_z, from_z, blocks,
                   piece_send, piece_recv, core_send, core_recv, y_send, y_recv, z_send, z_recv,
                   block_send, block_y_recv, block_core_recv, block_z_recv,
                   local, dots_send, dots_recv):
    ctx, tp = lax.axis_index("ctx"), lax.axis_index("tp")
    y, z_hi, core = ctx // 4, (ctx // 2) % 2, ctx % 2
    z_lo, x = tp // 4, tp % 4
    right_x, left_x, opposite_x = (x + 1) % 4, (x + 3) % 4, (x + 2) % 4
    here, there = z_lo * 4, (1 - z_lo) * 4
    right, left, far = (ctx, here + right_x), (ctx, here + left_x), (ctx, there + x)
    sibling = (y * 4 + z_hi * 2 + (1 - core), tp)
    across = (y * 4 + (1 - z_hi) * 2 + core, tp)
    plane = lambda other: (other * 4 + z_hi * 2 + core, tp)
    tokens, features = resid_ref.shape
    chunk = features // STEPS
    rows = chunk // 4
    half = tokens // 2
    group = pieces.shape[1]

    columns = heads.shape[1]

    def owner(i):
        return (y + 1 + i) % 4

    def fetch(i):
        lanes = pl.ds(pl.multiple_of(owner(i) * chunk, chunk), chunk)
        return pltpu.make_async_copy(resid_ref.at[:, lanes], pieces.at[i, tp], local.at[i])

    fetch_heads = pltpu.make_async_copy(heads_ref, heads, local.at[STEPS])
    for i in range(STEPS):
        fetch(i).start()
    fetch_heads.start()

    barrier = pltpu.get_barrier_semaphore()
    peers = [(ctx, (tp + d) % group) for d in range(1, group)]
    peers += [sibling, across] + [plane((y + d) % 4) for d in (1, 2, 3)]
    for peer in peers:
        pl.semaphore_signal(barrier, inc=1, device_id=peer, device_id_type=pl.DeviceIdType.MESH)
    pl.semaphore_wait(barrier, len(peers))

    def remote(src, dst, send, recv, device):
        return pltpu.make_async_remote_copy(
            src_ref=src, dst_ref=dst, send_sem=send, recv_sem=recv,
            device_id=device, device_id_type=pl.DeviceIdType.MESH,
        )

    whole, top, bottom = pl.ds(0, tokens), pl.ds(0, half), pl.ds(half, half)
    sent = []

    def send(i, piece, part, kind, lands, device):
        ref = pieces.at[i, piece, part]
        copy = remote(ref, ref, piece_send.at[i, kind], piece_recv.at[i, lands], device)
        copy.start()
        sent.append(copy)

    def arrive(i, piece, part, lands):
        ref = pieces.at[i, piece, part]
        remote(ref, ref, piece_send.at[i, 0], piece_recv.at[i, lands], far).wait_recv()

    def start_own(i):
        fetch(i).wait()
        if i % 2 == 0:
            send(i, tp, whole, TO_Z, FAR_C, far)
        send(i, tp, whole, TO_R, SAME_L, right)
        send(i, tp, whole, TO_L, SAME_R, left)
        if i % 2 == 1:
            send(i, tp, whole, TO_Z, FAR_C, far)

    def send_block(p, zh, semaphore, lands, device):
        ref = blocks.at[p, zh, core]
        copy = remote(ref, ref, semaphore, lands, device)
        copy.start()
        sent.append(copy)

    def block_arrives(p, zh, whose, lands):
        ref = blocks.at[p, zh, whose]
        remote(ref, ref, block_send.at[0], lands, sibling).wait_recv()

    def start_blocks():
        blocks[y, z_hi, core] = weight_ref[...]
        send_block(y, z_hi, block_send.at[0], block_z_recv, across)
        for i in range(STEPS - 1):
            send_block(y, z_hi, block_send.at[1 + i], block_y_recv.at[0, i], plane((y + 3 - i) % 4))
        send_block(y, z_hi, block_send.at[7], block_core_recv.at[0, STEPS - 1], sibling)

    def pass_blocks():
        block_arrives(y, 1 - z_hi, core, block_z_recv)
        for i in range(STEPS - 1):
            send_block(
                y, 1 - z_hi, block_send.at[4 + i], block_y_recv.at[1, i], plane((y + 3 - i) % 4)
            )
        send_block(y, 1 - z_hi, block_send.at[8], block_core_recv.at[1, STEPS - 1], sibling)

    def share_blocks(i):
        for side in range(2):
            zh = z_hi if side == 0 else 1 - z_hi
            block_arrives(owner(i), zh, core, block_y_recv.at[side, i])
            send_block(
                owner(i), zh, block_send.at[9 + 2 * i + side], block_core_recv.at[side, i], sibling
            )

    def blocks_ready(i):
        for side in range(2):
            zh = z_hi if side == 0 else 1 - z_hi
            block_arrives(owner(i), zh, 1 - core, block_core_recv.at[side, i])

    def first_hops(i):
        if i % 2 == 0:
            arrive(i, there + x, whole, FAR_C)
            send(i, there + x, whole, EXTRA_A, FAR_L, right)
            send(i, there + x, whole, EXTRA_B, FAR_R, left)
        arrive(i, here + left_x, whole, SAME_L)
        send(i, here + left_x, top, PASS_R, SAME_T, right)
        if i % 2 == 1:
            send(i, here + left_x, whole, EXTRA_A, FAR_L, far)
        arrive(i, here + right_x, whole, SAME_R)
        send(i, here + right_x, bottom, PASS_L, SAME_B, left)
        if i % 2 == 1:
            send(i, here + right_x, whole, EXTRA_B, FAR_R, far)

    def second_hops(i):
        if i % 2 == 0:
            arrive(i, there + left_x, whole, FAR_L)
            send(i, there + left_x, top, EXTRA_C, FAR_T, right)
            arrive(i, there + right_x, whole, FAR_R)
            send(i, there + right_x, bottom, EXTRA_D, FAR_B, left)
        else:
            arrive(i, here + opposite_x, top, SAME_T)
            send(i, here + opposite_x, top, EXTRA_C, FAR_T, far)
            arrive(i, here + opposite_x, bottom, SAME_B)
            send(i, here + opposite_x, bottom, EXTRA_D, FAR_B, far)

    def arrivals(i):
        if i % 2 == 0:
            arrive(i, here + opposite_x, top, SAME_T)
            arrive(i, here + opposite_x, bottom, SAME_B)
        else:
            arrive(i, there + x, whole, FAR_C)
            arrive(i, there + left_x, whole, FAR_L)
            arrive(i, there + right_x, whole, FAR_R)
        arrive(i, there + opposite_x, top, FAR_T)
        arrive(i, there + opposite_x, bottom, FAR_B)

    def start_dots():
        dots_all[tp] = dots_ref[...]
        for d in range(1, group):
            ref = dots_all.at[tp]
            copy = remote(
                ref, ref, dots_send.at[d - 1], dots_recv.at[d - 1], (ctx, (tp + d) % group)
            )
            copy.start()
            sent.append(copy)

    def gather_dots():
        for d in range(1, group):
            ref = dots_all.at[(tp + group - d) % group]
            remote(ref, ref, dots_send.at[0], dots_recv.at[d - 1], far).wait_recv()
        sources = dots_all.shape[2]
        count = group * EXTRA
        table = dots_all[...].reshape(count, sources)
        mine = iota((16, sources), 1) == iota((16, sources), 0) * group + tp
        mine = jnp.where(mine, 1.0, 0.0).astype(jnp.bfloat16)
        held = mm(mine, table, CONTRACT_LAST).astype(jnp.bfloat16)
        row, lane = iota((count, 2 * rows), 0), iota((count, 2 * rows), 1)
        device = row // EXTRA
        slot = row - device * EXTRA
        place = jnp.where(slot < CAP, (ctx * 4 + device // 2) * CAP + slot, -1)
        spread = jnp.where(lane == place, 1.0, 0.0).astype(jnp.bfloat16)
        dots_rows[...] = mm(held, spread)

    def turn_heads():
        fetch_heads.wait()
        for r in range(4):
            part = heads.shape[0] // 4
            heads_t[:, r * part:(r + 1) * part] = heads[r * part:(r + 1) * part, :].T

    def weight_partial(i, whose):
        def one(zh, carry):
            local_owner = 2 * zh + (core if whose == 0 else 1 - core)
            first = pl.multiple_of(local_owner * rows, rows)
            right_side = pieces[i, :, :, pl.ds(first, rows)].reshape(group * tokens, rows)
            value = mm(heads_t[...], right_side)
            partial[i, whose, zh, 0:columns] = value.astype(jnp.bfloat16)
            at = iota((16, 2 * rows), 0) == owner(i) * 4 + local_owner
            line = jnp.sum(jnp.where(at, dots_rows[...], 0.0), axis=0, keepdims=True)
            row = iota((EXTRA, rows), 0)
            tail = jnp.where(row == 0, line[:, :rows], jnp.where(row == 1, line[:, rows:], 0.0))
            partial[i, whose, zh, columns:columns + EXTRA] = tail.astype(jnp.bfloat16)
            return carry

        lax.fori_loop(0, 2, one, 0)

    def heads_partial(i):
        def one(r, carry):
            tall = pl.ds(pl.multiple_of(r * 2 * tokens, 2 * tokens), 2 * tokens)
            left_side = pieces[i, pl.ds(2 * r, 2)].reshape(2 * tokens, chunk)
            value = mm(left_side, blocks[owner(i)].reshape(chunk, blocks.shape[-1]))
            if i > 0:
                value = value + total[tall, :]
            if i < STEPS - 1:
                total[tall, :] = value
            else:
                out_heads_ref[tall, :] = value.astype(jnp.bfloat16)
            return carry

        lax.fori_loop(0, group // 2, one, 0)

    def multiply(i, between=()):
        weight_partial(i, 1)
        to_core = remote(partial.at[i, 1], from_core.at[i], core_send.at[i], core_recv.at[i], sibling)
        to_core.start()
        weight_partial(i, 0)
        for hops, other in between:
            hops(other)
        if i == STEPS - 1:
            return to_core
        blocks_ready(i)
        heads_partial(i)
        to_core.wait()
        summed[i] = (
            partial[i, 0].astype(jnp.float32) + from_core[i].astype(jnp.float32)
        ).astype(jnp.bfloat16)
        copy = remote(summed.at[i], from_y.at[i], y_send.at[i], y_recv.at[i], plane(owner(i)))
        copy.start()
        sent.append(copy)

    start_own(0)
    start_own(1)
    start_dots()
    start_blocks()
    turn_heads()
    first_hops(0)
    pass_blocks()
    first_hops(1)
    second_hops(0)
    start_own(2)
    second_hops(1)
    start_own(3)
    gather_dots()
    share_blocks(0)
    arrivals(0)
    multiply(0, ((first_hops, 2), (share_blocks, 1)))
    arrivals(1)
    multiply(1, ((first_hops, 3), (share_blocks, 2)))
    second_hops(2)
    second_hops(3)
    arrivals(2)
    multiply(2)
    arrivals(3)
    to_core = multiply(3)

    last = STEPS - 1

    def reduced(zh):
        value = partial[last, 0, zh].astype(jnp.float32) + from_core[last, zh].astype(jnp.float32)
        for i in range(last):
            value = value + from_y[i, zh].astype(jnp.float32)
        return value

    to_core.wait()
    for i in range(last):
        remote(summed.at[i], from_y.at[i], y_send.at[i], y_recv.at[i], across).wait_recv()
    to_z[...] = reduced(1 - z_hi).astype(jnp.bfloat16)
    copy = remote(to_z, from_z, z_send, z_recv, across)
    copy.start()
    blocks_ready(last)
    heads_partial(last)
    own = reduced(z_hi)
    copy.wait()
    own = own + from_z[...].astype(jnp.float32)
    out_weight_ref[...] = own[:columns].T.astype(jnp.bfloat16)
    out_dots_ref[...] = own[columns:]
    for copy in sent:
        copy.wait_send()


def project(resid, heads, weight, dots, group):
    tokens, features = resid.shape
    columns = heads.shape[1]
    chunk = features // STEPS
    rows = chunk // 4
    tall = columns + EXTRA
    bf16 = jnp.bfloat16
    dma = pltpu.SemaphoreType.DMA
    vmem = pl.BlockSpec(memory_space=pltpu.VMEM)
    anywhere = pl.BlockSpec(memory_space=pltpu.HBM)
    return pl.pallas_call(
        project_kernel,
        in_specs=[anywhere, anywhere, vmem, vmem],
        out_specs=[vmem] * 3,
        out_shape=[jax.ShapeDtypeStruct(heads.shape, bf16), jax.ShapeDtypeStruct((rows, columns), bf16),
                   jax.ShapeDtypeStruct((EXTRA, rows), jnp.float32)],
        scratch_shapes=[
            pltpu.VMEM(heads.shape, bf16),
            pltpu.VMEM(heads.shape[::-1], bf16),
            pltpu.VMEM((group,) + dots.shape, bf16),
            pltpu.VMEM((16, 2 * rows), jnp.float32),
            pltpu.VMEM((STEPS, group, tokens, chunk), bf16),
            pltpu.VMEM(heads.shape, jnp.float32),
            pltpu.VMEM((STEPS, 2, 2, tall, rows), bf16),
            pltpu.VMEM((STEPS, 2, tall, rows), bf16),
            pltpu.VMEM((STEPS - 1, 2, tall, rows), bf16),
            pltpu.VMEM((STEPS - 1, 2, tall, rows), bf16),
            pltpu.VMEM((tall, rows), bf16),
            pltpu.VMEM((tall, rows), bf16),
            pltpu.VMEM((STEPS, 2, 2, rows, columns), bf16),
            dma((STEPS, 9)), dma((STEPS, 9)), dma((STEPS,)), dma((STEPS,)),
            dma((STEPS - 1,)), dma((STEPS - 1,)), dma, dma,
            dma((15,)), dma((2, STEPS - 1)), dma((2, STEPS)), dma,
            dma((STEPS + 1,)), dma((group - 1,)), dma((group - 1,)),
        ],
        compiler_params=pltpu.CompilerParams(
            collective_id=0, has_side_effects=True, vmem_limit_bytes=61 * MIB),
        cost_estimate=pl.CostEstimate(
            flops=4 * group * tokens * features * columns, bytes_accessed=8 * MIB, transcendentals=0),
        name="project",
    )(resid, heads, weight, dots)


def per_device(
    ctx_heads,
    out_weight,
    hidden_in,
    norm_gain,
    expert_ids,
    route_weights,
    w_gate,
    w_up,
    w_down,
    grad_out,
):
    tokens, features = hidden_in.shape
    devices = lax.axis_size(("ctx", "tp"))
    experts = devices // 2
    axes = ("ctx", "tp")
    exchange = functools.partial(
        lax.all_to_all, axis_name=axes, split_axis=0, concat_axis=0, tiled=True
    )
    width = features // BLOCKS
    gain = norm_gain.reshape(1, features)
    rounded_weights = route_weights.astype(jnp.bfloat16).astype(jnp.float32)
    ids_t, weights_t = expert_ids.T, rounded_weights.T
    send_rows = dispatch(True, ids_t, ids_t, hidden_in, gain, experts)
    send_cots = dispatch(False, ids_t, weights_t, grad_out, gain, experts)
    raw_rows = exchange(send_rows.reshape(devices, CHUNK, width)).reshape(-1, width)
    raw_cots = exchange(send_cots.reshape(devices, CHUNK, width)).reshape(-1, width)
    slot_rows = unpack_chunks(raw_rows)
    gate_pre = mm(slot_rows, w_gate[0])
    up_value = mm(slot_rows, w_up[0])
    grads, slot_cots, activated, gate_grad, up_grad, dots = expert_back(
        raw_cots, gate_pre, up_value, w_gate[0], w_up[0], w_down[0]
    )
    back = exchange(grads.reshape(devices, CHUNK, width)).reshape(-1, width)
    sent_dots = jnp.pad(dots.reshape(devices, CAP).T, ((0, EXTRA - CAP), (0, 0)))
    down_wgrad = mm(activated, slot_cots, CONTRACT_FIRST).astype(jnp.bfloat16)
    gate_wgrad = mm(slot_rows, gate_grad, CONTRACT_FIRST).astype(jnp.bfloat16)
    up_wgrad = mm(slot_rows, up_grad, CONTRACT_FIRST).astype(jnp.bfloat16)
    resid_grad = combine(expert_ids, back, hidden_in, gain, grad_out, experts)

    heads_grad, weight_grad, summed_dots = project(
        resid_grad, ctx_heads, out_weight, sent_dots.astype(jnp.bfloat16), lax.axis_size("tp")
    )
    summed_dots = summed_dots[:2].reshape(-1)[:experts * CAP].reshape(experts, CAP)
    flat_ids = expert_ids.reshape(-1)
    onehot = (flat_ids[:, None] == jnp.arange(experts, dtype=jnp.int32)[None, :]).astype(jnp.int32)
    slot_rank = jnp.sum((jnp.cumsum(onehot, axis=0) - onehot) * onehot, axis=1)
    picked = jnp.dot(onehot.astype(jnp.float32), summed_dots, precision=lax.Precision.HIGHEST)
    at_rank = slot_rank[:, None] == jnp.arange(CAP, dtype=jnp.int32)[None, :]
    route_grads = (
        jnp.sum(jnp.where(at_rank, picked, 0.0), axis=1).reshape(tokens, -1) / rounded_weights
    )
    return (
        heads_grad,
        weight_grad,
        resid_grad,
        route_grads,
        gate_wgrad[None],
        up_wgrad[None],
        down_wgrad[None],
    )


def solution(mesh):
    split = P(("ctx", "tp"), None)
    stack = P(("ctx", "tp"), None, None)
    in_specs = (
        P("ctx", "tp"),
        P("ctx", "tp"),
        split,
        P(),
        split,
        split,
        stack,
        stack,
        stack,
        split,
    )
    out_specs = (P("ctx", "tp"), P("ctx", "tp"), split, split, stack, stack, stack)
    return jax.shard_map(
        per_device, mesh=mesh, in_specs=in_specs, out_specs=out_specs, check_vma=False
    )
```
